32 devices in a mesh: dp: 2 (over x), expert: 16 (over z, y, core).
Axes of the slice: x: 2, y: 2, z: 4, core: 2. Of those that a mesh axis runs over, the one named last changes fastest.
Arguments:
- images: bfloat16 [96, 197, 768], P(('dp', 'expert')), may hold values from -6 to 6
- cotangent: bfloat16 [96, 197, 768], P(('dp', 'expert')), may hold values from -6 to 6
- routes: int32 [96, 197, 2], P(('dp', 'expert')), may hold values from 0 to 15, all different within a row
- priority: int32 [32, 591], P(('dp', 'expert')), may hold values from 0 to 590, each once within a row
- qkv_weight: float32 [768, 2304], P('dp'), may hold values from -0.21875 to 0.21875
- qkv_first: float32 [768, 2304], P('dp'), may hold values from -0.00018310547 to 0.00018310547
- qkv_second: float32 [768, 2304], P('dp'), may hold values from 6.4207827e-12 to 1.02732524e-10
- proj_weight: float32 [768, 768], P('dp'), may hold values from -0.875 to 0.875
- proj_first: float32 [768, 768], P('dp'), may hold values from -0.00018310547 to 0.00018310547
- proj_second: float32 [768, 768], P('dp'), may hold values from 6.4207827e-12 to 1.02732524e-10
- router_weight: float32 [768, 16], P('dp'), may hold values from -0.15625 to 0.15625
- router_first: float32 [768, 16], P('dp'), may hold values from -0.00018310547 to 0.00018310547
- router_second: float32 [768, 16], P('dp'), may hold values from 6.4207827e-12 to 1.02732524e-10
- norm_params: float32 [4, 768], P(None, 'dp'), may hold values from -0.9 to 2.1
- norm_first: float32 [4, 768], P(None, 'dp'), may hold values from -0.0007324219 to 0.0007324219
- norm_second: float32 [4, 768], P(None, 'dp'), may hold values from 1.02732524e-10 to 1.6437204e-09
- inner_weight: float32 [16, 768, 3072], P('expert', None, 'dp'), may hold values from -0.25259074 to 0.25259074
- inner_first: float32 [16, 768, 3072], P('expert', None, 'dp'), may hold values from -0.00018310547 to 0.00018310547
- inner_second: float32 [16, 768, 3072], P('expert', None, 'dp'), may hold values from 6.4207827e-12 to 1.02732524e-10
- outer_weight: float32 [16, 3072, 768], P('expert', 'dp'), may hold values from -0.15625 to 0.15625
- outer_first: float32 [16, 3072, 768], P('expert', 'dp'), may hold values from -0.00018310547 to 0.00018310547
- outer_second: float32 [16, 3072, 768], P('expert', 'dp'), may hold values from 6.4207827e-12 to 1.02732524e-10
Outputs:
- output: bfloat16 [96, 197, 768], P(('dp', 'expert'))
- input_grad: bfloat16 [96, 197, 768], P(('dp', 'expert'))
- grad_norm: float32 [], replicated
- new_qkv: float32 [768, 2304], P('dp')
- new_qkv_first: float32 [768, 2304], P('dp')
- new_qkv_second: float32 [768, 2304], P('dp')
- new_proj: float32 [768, 768], P('dp')
- new_proj_first: float32 [768, 768], P('dp')
- new_proj_second: float32 [768, 768], P('dp')
- new_router: float32 [768, 16], P('dp')
- new_router_first: float32 [768, 16], P('dp')
- new_router_second: float32 [768, 16], P('dp')
- new_norm: float32 [4, 768], P(None, 'dp')
- new_norm_first: float32 [4, 768], P(None, 'dp')
- new_norm_second: float32 [4, 768], P(None, 'dp')
- new_inner: float32 [16, 768, 3072], P('expert', None, 'dp')
- new_inner_first: float32 [16, 768, 3072], P('expert', None, 'dp')
- new_inner_second: float32 [16, 768, 3072], P('expert', None, 'dp')
- new_outer: float32 [16, 3072, 768], P('expert', 'dp')
- new_outer_first: float32 [16, 3072, 768], P('expert', 'dp')
- new_outer_second: float32 [16, 3072, 768], P('expert', 'dp')
The draws below stay inside these ranges and needn't reach their ends.
Inputs may be any that keep to these rules, and one draw needn't show every extreme that they name: `routes`: each token names two different experts. `priority`: each row is an order of the 591 tokens of one device.
All inputs are finite; a program needn't handle non-finite values.
Results may differ from the reference program's by a relative error of at most 0.025.
The reference program's roundings to bfloat16 on the way count: a program that leaves them out, or rounds other values in their place, can miss the bound.
Values may be sent and summed in bfloat16 or wider, within the bound.
A program may use at most 256 MiB of HBM per device.

```python
import math
import jax
import jax.numpy as jnp
from jax import lax

D = 768
HEADS = 12
HDIM = 64
HID = 3072
SEQ = 197
IMG_DEV = 3
STEP = 10
EXPERTS = 16
TOK_DEV = 591
IMAGES = 96
CAP = 84
DEVICES = 32


def draw_inner_weight(key, part):
    key = jax.random.fold_in(key, 11)
    column = jnp.arange(HID, dtype=jnp.float32) / (HID - 1) - 0.5
    position = jnp.arange(EXPERTS, dtype=jnp.float32) / max(EXPERTS - 1, 1) - 0.5
    base = jnp.clip(jax.random.normal(key, (EXPERTS, D, HID), jnp.float32), -4.0, 4.0)
    rise = 1.7
    factor = rise ** (column[None, None, :] + position[:, None, None])
    return base * factor * D ** (-0.5)


def draw_norm_params(key, part):
    key = jax.random.fold_in(key, 12)
    gain_key, shift_key = jax.random.split(key)
    place = jnp.arange(D, dtype=jnp.float32) / (D - 1) - 0.5
    rise = 1.7
    shifts = jnp.clip(0.3 * jax.random.normal(shift_key, (2, D), jnp.float32), -0.9, 0.9)
    gains = rise ** place[None, :] * jax.random.uniform(gain_key, (2, D), jnp.float32, 0.6, 1.4)
    return jnp.stack([gains[0], shifts[0], gains[1], shifts[1]])


def levels(own_key, dims, cuts, smallest, top_value):
    level = 1.0
    for axis_at, blocks in cuts:
        steps = jax.random.uniform(jax.random.fold_in(jax.random.fold_in(own_key, 6), axis_at), (blocks,), jnp.float32, smallest / len(cuts), top_value / len(cuts))
        level = level * jnp.repeat(jnp.exp(steps), dims[axis_at] // blocks).reshape((-1,) + (1,) * (len(dims) - 1 - axis_at))
    return level


def picks_of(own_key, rows, amount, top, lift):
    sequence = jax.random.permutation(jax.random.fold_in(own_key, 1), amount)
    pull = sequence
    for power in range(3):
        pull = pull * pull // amount
    pull = pull * lift // amount
    tickets = jax.random.randint(jax.random.fold_in(own_key, 2), (rows, amount), 0, 4096) + pull
    sure = jax.random.permutation(jax.random.fold_in(own_key, 3), rows)[jnp.arange(amount) % rows]
    tickets = jnp.where(jnp.arange(rows)[:, None] == sure[None, :], 1 << 14, tickets)
    merit = tickets * amount + jnp.arange(amount)
    return lax.top_k(merit.astype(jnp.int32), top)[1].astype(jnp.int32)


def gaussian(stream_key, shape, spread, most, shards=(), kind=jnp.bfloat16):
    array = spread * jax.random.normal(stream_key, shape, jnp.float32)
    if shards:
        array = array * levels(stream_key, shape, shards, -0.22, 0.18)
    return jnp.clip(array, -most, most).astype(kind)


def setup_inputs(seed: int = 0) -> dict:
    arg_keys = jax.random.split(jax.random.key(seed), 23)
    return {
        "images": gaussian(arg_keys[0], (IMAGES, SEQ, D), 1.0, 6.0, ((0, 32),)),
        "cotangent": gaussian(arg_keys[1], (IMAGES, SEQ, D), 1.0, 6.0, ((0, 32),)),
        "routes": picks_of(arg_keys[2], IMAGES * SEQ, EXPERTS, 2, 1024).reshape((IMAGES, SEQ, 2)),
        "priority": jax.vmap(lambda own: jax.random.permutation(own, TOK_DEV))(jax.random.split(arg_keys[3], DEVICES)).reshape((DEVICES, TOK_DEV)).astype(jnp.int32),
        "qkv_weight": gaussian(arg_keys[4], (D, 3 * D), D ** -0.5, 0.21875, ((0, 2),), jnp.float32),
        "qkv_first": gaussian(arg_keys[5], (D, 3 * D), (0.111 * (4 * D * D + D * EXPERTS + 2 * EXPERTS * D * HID + 4 * D) ** -0.5), 0.00018310547, ((0, 2),), jnp.float32),
        "qkv_second": jnp.clip(jnp.exp(math.log(1.0273252387671405e-10) - 2.7725887 * jax.random.uniform(arg_keys[6], (D, 3 * D), jnp.float32) ** levels(arg_keys[6], (D, 3 * D), ((0, 2),), -0.2, 0.2)), 6.4207827422946284e-12, 1.0273252387671405e-10),
        "proj_weight": gaussian(arg_keys[7], (D, D), (D // 16) ** -0.5, 0.875, ((0, 2),), jnp.float32),
        "proj_first": gaussian(arg_keys[8], (D, D), (0.111 * (4 * D * D + D * EXPERTS + 2 * EXPERTS * D * HID + 4 * D) ** -0.5), 0.00018310547, ((0, 2),), jnp.float32),
        "proj_second": jnp.clip(jnp.exp(math.log(1.0273252387671405e-10) - 2.7725887 * jax.random.uniform(arg_keys[9], (D, D), jnp.float32) ** levels(arg_keys[9], (D, D), ((0, 2),), -0.2, 0.2)), 6.4207827422946284e-12, 1.0273252387671405e-10),
        "router_weight": gaussian(arg_keys[10], (D, EXPERTS), (2 * D) ** -0.5, 0.15625, ((0, 2),), jnp.float32),
        "router_first": gaussian(arg_keys[11], (D, EXPERTS), (0.111 * (4 * D * D + D * EXPERTS + 2 * EXPERTS * D * HID + 4 * D) ** -0.5), 0.00018310547, ((0, 2),), jnp.float32),
        "router_second": jnp.clip(jnp.exp(math.log(1.0273252387671405e-10) - 2.7725887 * jax.random.uniform(arg_keys[12], (D, EXPERTS), jnp.float32) ** levels(arg_keys[12], (D, EXPERTS), ((0, 2),), -0.2, 0.2)), 6.4207827422946284e-12, 1.0273252387671405e-10),
        "norm_params": draw_norm_params(jax.random.fold_in(arg_keys[22], 71), 0),
        "norm_first": gaussian(arg_keys[14], (4, D), (0.444 * (4 * D * D + D * EXPERTS + 2 * EXPERTS * D * HID + 4 * D) ** -0.5), 0.0007324219, ((1, 2),), jnp.float32),
        "norm_second": jnp.clip(jnp.exp(math.log(1.6437203820274249e-09) - 2.7725887 * jax.random.uniform(arg_keys[15], (4, D), jnp.float32) ** levels(arg_keys[15], (4, D), ((1, 2),), -0.2, 0.2)), 1.0273252387671405e-10, 1.6437203820274249e-09),
        "inner_weight": draw_inner_weight(jax.random.fold_in(arg_keys[22], 71), 0),
        "inner_first": gaussian(arg_keys[17], (EXPERTS, D, HID), (0.111 * (4 * D * D + D * EXPERTS + 2 * EXPERTS * D * HID + 4 * D) ** -0.5), 0.00018310547, ((0, 16), (2, 2)), jnp.float32),
        "inner_second": jnp.clip(jnp.exp(math.log(1.0273252387671405e-10) - 2.7725887 * jax.random.uniform(arg_keys[18], (EXPERTS, D, HID), jnp.float32) ** levels(arg_keys[18], (EXPERTS, D, HID), ((0, 16), (2, 2)), -0.2, 0.2)), 6.4207827422946284e-12, 1.0273252387671405e-10),
        "outer_weight": gaussian(arg_keys[19], (EXPERTS, HID, D), (HID // 2) ** -0.5, 0.15625, ((0, 16), (1, 2)), jnp.float32),
        "outer_first": gaussian(arg_keys[20], (EXPERTS, HID, D), (0.111 * (4 * D * D + D * EXPERTS + 2 * EXPERTS * D * HID + 4 * D) ** -0.5), 0.00018310547, ((0, 16), (1, 2)), jnp.float32),
        "outer_second": jnp.clip(jnp.exp(math.log(1.0273252387671405e-10) - 2.7725887 * jax.random.uniform(arg_keys[21], (EXPERTS, HID, D), jnp.float32) ** levels(arg_keys[21], (EXPERTS, HID, D), ((0, 16), (1, 2)), -0.2, 0.2)), 6.4207827422946284e-12, 1.0273252387671405e-10),
    }


@jax.custom_vjp
def low(v):
    return lax.optimization_barrier(v.astype(jnp.bfloat16)).astype(jnp.float32)

@jax.custom_vjp
def low_back(v):
    return v

def low_keep(v):
    return (low(v), None)

def low_pass(kept, grad):
    return (grad,)

def back_keep(v):
    return (v, None)

def back_low(kept, grad):
    return (low(grad),)
low.defvjp(low_keep, low_pass)
low_back.defvjp(back_keep, back_low)
LN_EPS = 1e-06
BETA_ONE = 0.9
BETA_TWO = 0.999
ADAM_EPS = 1e-08
RATE_MATRIX = 0.06
RATE_VECTOR = 0.4
DECAY = 0.1
CLIP_NORM = 1.0
HIGHEST = lax.Precision.HIGHEST

def hdot(left, right):
    return jnp.dot(left, right, precision=HIGHEST, preferred_element_type=jnp.float32)

def layer_norm(values, gain, shift):
    centre = lax.optimization_barrier(jnp.mean(values, axis=-1, keepdims=True))
    centered = values - centre
    rstd = lax.rsqrt(lax.optimization_barrier(jnp.mean(centered * centered, axis=-1, keepdims=True)) + LN_EPS)
    return centered * rstd * gain + shift

def slot_tables(order, picks, num_experts, capacity):
    tok_count = order.shape[0]
    pair_tok = jnp.concatenate([order, order]).astype(jnp.int32)
    pair_k = jnp.concatenate([jnp.zeros((tok_count,), jnp.int32), jnp.ones((tok_count,), jnp.int32)])
    pair_expert = picks[pair_tok, pair_k].astype(jnp.int32)
    onehot = (pair_expert[:, None] == jnp.arange(num_experts, dtype=jnp.int32)[None, :]).astype(jnp.int32)
    before = jnp.cumsum(onehot, axis=0) - onehot
    slot = lax.optimization_barrier(jnp.sum(before * onehot, axis=1)).astype(jnp.int32)
    place = jnp.where(slot < capacity, pair_expert * capacity + slot, num_experts * capacity).astype(jnp.int32)
    slot_tok = jnp.full((num_experts * capacity + 1,), tok_count, jnp.int32).at[place].set(pair_tok)[:-1]
    slot_k = jnp.zeros((num_experts * capacity + 1,), jnp.int32).at[place].set(pair_k)[:-1]
    tok_slot = jnp.zeros((tok_count, 2), jnp.int32).at[pair_tok, pair_k].set(slot)
    return (slot_tok, slot_k, tok_slot)

def adam_step(weight, first, second, grad, rate, decay):
    new_first = BETA_ONE * first + (1.0 - BETA_ONE) * grad
    new_second = BETA_TWO * second + (1.0 - BETA_TWO) * grad * grad
    first_hat = new_first / (1.0 - BETA_ONE ** STEP)
    second_hat = new_second / (1.0 - BETA_TWO ** STEP)
    new_weight = weight - rate * (first_hat / (jnp.sqrt(second_hat) + ADAM_EPS) + decay * weight)
    return (new_weight, new_first, new_second)

def reference(images, cotangent, routes, priority, qkv_weight, qkv_first, qkv_second, proj_weight, proj_first, proj_second, router_weight, router_first, router_second, norm_params, norm_first, norm_second, inner_weight, inner_first, inner_second, outer_weight, outer_first, outer_second):
    scale = float(HDIM) ** (-0.5)
    picks = routes.reshape(DEVICES, TOK_DEV, 2).astype(jnp.int32)

    def device_tables(order, chosen):
        return slot_tables(order, chosen, EXPERTS, CAP)
    slot_tok, slot_k, tok_slot = jax.vmap(device_tables)(priority.astype(jnp.int32), picks)
    offsets = jnp.arange(DEVICES, dtype=jnp.int32) * (TOK_DEV + 1)
    row_index = jnp.transpose(slot_tok.reshape(DEVICES, EXPERTS, CAP) + offsets[:, None, None], (1, 0, 2)).reshape(EXPERTS, DEVICES * CAP)
    kept = (tok_slot < CAP).astype(jnp.float32)
    pair_row = picks * (DEVICES * CAP) + (jnp.arange(DEVICES, dtype=jnp.int32) * CAP)[:, None, None] + jnp.minimum(tok_slot, CAP - 1)

    def forward(inputs, qkv_w, proj_w, router_w, norm_w, inner_w, outer_w):
        qkv_b = low(qkv_w)
        proj_b = low(proj_w)
        router_b = low(router_w)
        norm_b = low(norm_w)
        inner_b = low(inner_w)
        outer_b = low(outer_w)

        def attend(block):
            flat = block.reshape(TOK_DEV, D)
            h_one = low(layer_norm(flat, norm_b[0], norm_b[1]))
            mixed = low(low_back(hdot(h_one, qkv_b))).reshape(IMG_DEV, SEQ, 3, HEADS, HDIM)
            scores = low_back(jnp.einsum('bqhd,bkhd->bhqk', mixed[:, :, 0], mixed[:, :, 1], precision=HIGHEST) * scale)
            weights = low(jax.nn.softmax(scores, axis=-1))
            context = low(low_back(jnp.einsum('bhqk,bkhd->bqhd', weights, mixed[:, :, 2], precision=HIGHEST)))
            after = flat + low_back(hdot(context.reshape(TOK_DEV, D), proj_b))
            h_two = low(layer_norm(after, norm_b[2], norm_b[3]))
            logits = low_back(hdot(h_two, router_b))
            return (after, h_two, logits)
        after, h_two, logits = lax.map(jax.checkpoint(attend), inputs.reshape(DEVICES, IMG_DEV, SEQ, D))
        router = jax.nn.softmax(logits, axis=-1)
        chosen = jnp.take_along_axis(router, picks, axis=-1)
        gates = chosen / lax.optimization_barrier(jnp.sum(chosen, axis=-1, keepdims=True))
        padded = jnp.concatenate([h_two, jnp.zeros((DEVICES, 1, D), jnp.float32)], axis=1).reshape(DEVICES * (TOK_DEV + 1), D)

        def expert(pack):
            index, inner, outer = pack
            rows = low_back(padded[index])
            hidden = low_back(hdot(rows, inner))
            act = low(jax.nn.gelu(hidden, approximate=False))
            return low(low_back(hdot(act, outer)))
        results = lax.map(jax.checkpoint(expert), (row_index, inner_b, outer_b)).reshape(EXPERTS * DEVICES * CAP, D)
        pair_out = results[pair_row] * kept[..., None]
        return after + lax.optimization_barrier(jnp.sum(pair_out * gates[..., None], axis=2))
    final, pullback = jax.vjp(forward, images.astype(jnp.float32), qkv_weight, proj_weight, router_weight, norm_params, inner_weight, outer_weight)
    grads = pullback(cotangent.reshape(DEVICES, TOK_DEV, D).astype(jnp.float32))
    output = final.reshape(IMAGES, SEQ, D).astype(jnp.bfloat16)
    input_grad = grads[0].reshape(IMAGES, SEQ, D).astype(jnp.bfloat16)
    squares = jnp.float32(0.0)
    for grad in grads[1:]:
        squares = squares + jnp.sum(grad * grad)
    grad_norm = jnp.sqrt(squares)
    clip = CLIP_NORM / jnp.maximum(grad_norm, CLIP_NORM)
    qkv_new = adam_step(qkv_weight, qkv_first, qkv_second, grads[1] * clip, RATE_MATRIX, DECAY)
    proj_new = adam_step(proj_weight, proj_first, proj_second, grads[2] * clip, RATE_MATRIX, DECAY)
    router_new = adam_step(router_weight, router_first, router_second, grads[3] * clip, RATE_MATRIX, DECAY)
    norm_new = adam_step(norm_params, norm_first, norm_second, grads[4] * clip, RATE_VECTOR, 0.0)
    inner_new = adam_step(inner_weight, inner_first, inner_second, grads[5] * clip, RATE_MATRIX, DECAY)
    outer_new = adam_step(outer_weight, outer_first, outer_second, grads[6] * clip, RATE_MATRIX, DECAY)
    return (output, input_grad, grad_norm, qkv_new[0], qkv_new[1], qkv_new[2], proj_new[0], proj_new[1], proj_new[2], router_new[0], router_new[1], router_new[2], norm_new[0], norm_new[1], norm_new[2], inner_new[0], inner_new[1], inner_new[2], outer_new[0], outer_new[1], outer_new[2])
```

```python
import functools

import jax
import jax.numpy as jnp
from jax import lax
from jax.experimental import pallas as pl
from jax.experimental.pallas import tpu as pltpu
from jax.sharding import PartitionSpec as P

HEADS = 12
HDIM = 64
STEP = 10
SCALE = float(HDIM) ** (-0.5)

LN_EPS = 1e-06
BETA_ONE = 0.9
BETA_TWO = 0.999
ADAM_EPS = 1e-08
RATE_MATRIX = 0.06
RATE_VECTOR = 0.4
DECAY = 0.1
CLIP_NORM = 1.0

BF = jnp.bfloat16
F32 = jnp.float32
I32 = jnp.int32
NEG = -1e30
BLOCK = 128
TILE = 512
VMEM_CAP = 60 * 1024 * 1024

TAIL_C = 0.31
TAIL = (
    0.03601999959102291,
    -0.14256280554259812,
    0.15715769015924325,
    -0.017324403713695688,
    0.11173640397253812,
    0.10712570259185507,
    0.12420698490047791,
    0.12363964793348867,
    7.947371491008614e-07,
)
INV_SQRT_TAU = 0.3989422804014327


def up(value, step):
    return -(-value // step) * step


def dot(left, right):
    return lax.dot_general(left, right, (((1,), (0,)), ((), ())), preferred_element_type=F32)


def dot_nt(left, right):
    return lax.dot_general(left, right, (((1,), (1,)), ((), ())), preferred_element_type=F32)


def dot_tn(left, right):
    return lax.dot_general(left, right, (((0,), (0,)), ((), ())), preferred_element_type=F32)


def iota(shape, axis):
    return lax.broadcasted_iota(I32, shape, axis)


def hot(mask):
    return jnp.where(mask, 1.0, 0.0).astype(BF)


def normed_of(values):
    centre = jnp.mean(values, axis=-1, keepdims=True)
    centered = values - centre
    rstd = lax.rsqrt(jnp.mean(centered * centered, axis=-1, keepdims=True) + LN_EPS)
    return centered * rstd, rstd


def norm_back_rows(grad, normed, rstd, gain):
    scaled = grad * gain
    inner_mean = jnp.mean(scaled, axis=-1, keepdims=True)
    cross_mean = jnp.mean(scaled * normed, axis=-1, keepdims=True)
    return rstd * (scaled - inner_mean - normed * cross_mean)


def split3(values):
    high = values.astype(BF)
    rest = values - high.astype(F32)
    mid = rest.astype(BF)
    low = (rest - mid.astype(F32)).astype(BF)
    return high, mid, low


def call(kernel, out_shape, *args, scratch=(), specs=None, flops=0, moved=0):
    vmem = pl.BlockSpec(memory_space=pltpu.VMEM)
    single = not isinstance(out_shape, (tuple, list))
    return pl.pallas_call(
        kernel,
        out_shape=out_shape,
        in_specs=[vmem] * len(args) if specs is None else specs,
        out_specs=vmem if single else [vmem] * len(out_shape),
        scratch_shapes=list(scratch),
        compiler_params=pltpu.CompilerParams(vmem_limit_bytes=VMEM_CAP),
        cost_estimate=pl.CostEstimate(flops=int(flops), bytes_accessed=int(moved), transcendentals=0),
    )(*args)


def shape(dims, kind):
    return jax.ShapeDtypeStruct(dims, kind)


MESH = pl.DeviceIdType.MESH


def remote(source, target, send, recv, device):
    return pltpu.make_async_remote_copy(
        src_ref=source, dst_ref=target, send_sem=send, recv_sem=recv, device_id=device, device_id_type=MESH
    )


def rows_at(start, size, unit=16):
    return pl.ds(pl.multiple_of(start, unit), size)


class Exchange:
    def __init__(self, send, recv, send_sem, recv_sem, local_sem, cp, exps):
        self.send, self.recv, self.send_sem, self.recv_sem, self.local_sem = send, recv, send_sem, recv_sem, local_sem
        self.cp, self.chips = cp, exps // 2
        self.at_dp, self.me = lax.axis_index("dp"), lax.axis_index("expert")
        self.core, self.chip = self.me % 2, self.me // 2

    def out(self, r, j):
        there = ((self.chip + r) % self.chips) * 2 + j
        return remote(
            self.send.at[rows_at(there * self.cp, self.cp), :],
            self.recv.at[rows_at(self.me * self.cp, self.cp), :],
            self.send_sem.at[2 * r + j],
            self.recv_sem.at[2 * r + self.core],
            (self.at_dp, there),
        )

    def back(self, r, j):
        there = ((self.chip + self.chips - r) % self.chips) * 2 + j
        return remote(
            self.send.at[rows_at(self.me * self.cp, self.cp), :],
            self.recv.at[rows_at(there * self.cp, self.cp), :],
            self.send_sem.at[2 * r + j],
            self.recv_sem.at[2 * r + j],
            (self.at_dp, there),
        )

    def own(self):
        at = rows_at(self.me * self.cp, self.cp)
        return pltpu.make_async_copy(self.send.at[at, :], self.recv.at[at, :], self.local_sem)

    def start(self, r):
        @pl.when(r == 0)
        def _():
            self.out(0, 1 - self.core).start()
            self.own().start()

        @pl.when(r > 0)
        def _():
            self.out(r, 0).start()
            self.out(r, 1).start()

    def finish(self):
        self.own().wait()
        self.out(0, 1 - self.core).wait_send()
        self.back(0, 1 - self.core).wait_recv()

        def step(r, carry):
            for j in range(2):
                self.out(r, j).wait_send()
                self.back(r, j).wait_recv()
            return carry

        lax.fori_loop(1, self.chips, step, 0)


def front_kernel(*refs, pair, imgs, seq, sp, nt, cap, cp, ck, exps):
    refs = list(refs)
    images_ref, cot_in_ref, picks_ref, order_row_ref, order_col_ref, small_ref, dense_ref = refs[:7]
    del refs[:7]
    if pair:
        inner_ref, outer_ref = refs[:2]
        del refs[:2]
    w_ref, small_all, h1_ref, mixed_ref, ctx_ref, after_ref, h2_ref, router_out, gates_ref, place_out = refs[:10]
    recv_ref, recv_cot_ref = refs[10:12]
    del refs[:12]
    if pair:
        inner_out, outer_out = refs[:2]
        del refs[:2]
    x_ref, cot_ref, send_ref, send_cot_ref, pad_ref = refs[:5]
    cot_ssem, cot_rsem, row_ssem, row_rsem, local_sem, weight_ssem, weight_rsem = refs[5:]
    feat = images_ref.shape[-1]
    at_dp, me = lax.axis_index("dp"), lax.axis_index("expert")
    core, chip = me % 2, me // 2
    chips = exps // 2
    shard = dense_ref.shape[0]
    half = shard // 2

    barrier = pltpu.get_barrier_semaphore()

    def greet(r, carry):
        pl.semaphore_signal(
            barrier, inc=1, device_id=(at_dp, (me + r) % exps), device_id_type=MESH
        )
        return carry

    lax.fori_loop(1, exps, greet, 0)
    if pair:
        pl.semaphore_signal(barrier, inc=1, device_id=(1 - at_dp, me), device_id_type=MESH)
    pl.semaphore_wait(barrier, exps - 1 + int(pair))

    if pair:
        other_dp, other_core = (1 - at_dp, me), (at_dp, chip * 2 + 1 - core)
        small_copy = remote(
            small_ref, small_all.at[at_dp], weight_ssem.at[0], weight_rsem.at[0], other_dp
        )
        small_copy.start()
        landed = w_ref.at[rows_at((1 - at_dp) * shard + core * half, half), :]
        dense_copy = remote(
            dense_ref.at[rows_at(core * half, half), :],
            w_ref.at[rows_at(at_dp * shard + core * half, half), :],
            weight_ssem.at[1], weight_rsem.at[1], other_dp,
        )
        dense_copy.start()
        swap_copy = remote(landed, landed, weight_ssem.at[2], weight_rsem.at[2], other_core)
        inner_copy = remote(inner_ref, inner_out, weight_ssem.at[3], weight_rsem.at[3], other_dp)
        outer_copy = remote(outer_ref, outer_out, weight_ssem.at[4], weight_rsem.at[4], other_dp)

    for ref, source in ((x_ref, images_ref), (cot_ref, cot_in_ref)):
        ref[...] = jnp.zeros(ref.shape, BF)
        for i in range(imgs):
            ref[i * sp : i * sp + seq, :] = source[i]
    first, second = picks_ref[0:1, :], picks_ref[1:2, :]
    sub, lane = iota((nt, nt), 0), iota((nt, nt), 1)
    pos_row = jnp.sum(jnp.where(order_col_ref[...] == lane, sub.astype(F32), 0.0), axis=0, keepdims=True)
    pos_col = jnp.sum(jnp.where(order_row_ref[...] == sub, lane.astype(F32), 0.0), axis=1, keepdims=True)
    earlier = hot(pos_col < pos_row)
    exp_id = iota((exps, nt), 0)
    hot0 = jnp.where(exp_id == first, 1.0, 0.0)
    hot1 = jnp.where(exp_id == second, 1.0, 0.0)
    before0 = dot(hot0.astype(BF), earlier)
    before1 = dot(hot1.astype(BF), earlier) + jnp.sum(hot0, axis=1, keepdims=True)
    slot0 = jnp.sum(hot0 * before0, axis=0, keepdims=True).astype(I32)
    slot1 = jnp.sum(hot1 * before1, axis=0, keepdims=True).astype(I32)
    ok0, ok1 = (slot0 < cap) & (first >= 0), (slot1 < cap) & (second >= 0)
    place0, place1 = jnp.where(ok0, first * cp + slot0, -1), jnp.where(ok1, second * cp + slot1, -1)
    place_out[0:1, :] = jnp.where(ok0, first * ck + slot0, -1)
    place_out[1:2, :] = jnp.where(ok1, second * ck + slot1, -1)
    place_out[2:8, :] = jnp.full((6, nt), -1, I32)

    cot_rows = Exchange(send_cot_ref, recv_cot_ref, cot_ssem, cot_rsem, local_sem.at[0], cp, exps)

    def cot_chunk(r, carry):
        base = ((chip + r) % chips) * (2 * cp)
        row = iota((2 * cp, nt), 0) + base
        pick = hot((row == place0) | (row == place1))
        send_cot_ref[rows_at(base, 2 * cp), :] = dot(pick, cot_ref[...]).astype(BF)
        cot_rows.start(r)
        return carry

    lax.fori_loop(0, chips, cot_chunk, 0)

    if pair:
        small_all[at_dp] = small_ref[...]
        w_ref[rows_at(at_dp * shard, shard), :] = dense_ref[...]
        small_copy.wait_recv()
        small = jnp.concatenate([small_all[0], small_all[1]], axis=1)
    else:
        small_all[...] = small_ref[...]
        w_ref[...] = dense_ref[...]
        small = small_all[...]
    norm = small[exps : exps + 4].astype(F32)
    router_w = small[:exps]

    def first_norm(i, carry):
        at = rows_at(i * BLOCK, BLOCK, BLOCK)
        normed, _ = normed_of(x_ref[at, :].astype(F32))
        h1_ref[at, :] = (normed * norm[0:1] + norm[1:2]).astype(BF)
        return carry

    lax.fori_loop(0, nt // BLOCK, first_norm, 0)

    if pair:
        dense_copy.wait_recv()
        swap_copy.start()
        inner_copy.start()
        outer_copy.start()
        swap_copy.wait_recv()

    step = 384

    def project(i, carry):
        at = rows_at(i * step, step, 128)
        mixed_ref[:, at] = dot(h1_ref[...], w_ref[:, at]).astype(BF)
        return carry

    lax.fori_loop(0, 3 * feat // step, project, 0)

    pairs = feat // 128
    key_ok = iota((sp, sp), 1) < seq
    left = iota((sp, 128), 1) < HDIM

    def attend(i, carry):
        rows = rows_at((i // pairs) * sp, sp)
        col = (i % pairs) * 128
        query = mixed_ref[rows, rows_at(col, 128, 128)]
        keys = mixed_ref[rows, rows_at(col + feat, 128, 128)]
        values = mixed_ref[rows, rows_at(col + 2 * feat, 128, 128)]
        outs = []
        for mask in (left, ~left):
            scores = dot_nt(jnp.where(mask, query, jnp.zeros_like(query)), keys) * SCALE
            scores = jnp.where(key_ok, scores, NEG)
            top = jnp.max(scores, axis=-1, keepdims=True)
            grown = jnp.exp(scores - top)
            probs = grown / jnp.sum(grown, axis=-1, keepdims=True)
            outs.append(dot(probs.astype(BF), values))
        ctx_ref[rows, rows_at(col, 128, 128)] = jnp.where(left, outs[0], outs[1]).astype(BF)
        return carry

    ctx_ref[imgs * sp : nt, :] = jnp.zeros((nt - imgs * sp, feat), BF)
    lax.fori_loop(0, imgs * pairs, attend, 0)

    def second_norm(i, carry):
        at = rows_at(i * BLOCK, BLOCK, BLOCK)
        after = x_ref[at, :].astype(F32) + dot(ctx_ref[at, :], w_ref[:, 3 * feat : 4 * feat])
        after_ref[at, :] = after
        normed, _ = normed_of(after)
        h2_ref[at, :] = (normed * norm[2:3] + norm[3:4]).astype(BF)
        return carry

    lax.fori_loop(0, nt // BLOCK, second_norm, 0)

    h2 = h2_ref[...]
    logits = dot_nt(router_w, h2)
    grown = jnp.exp(logits - jnp.max(logits, axis=0, keepdims=True))
    router = grown / jnp.sum(grown, axis=0, keepdims=True)
    router_out[...] = router
    chosen0 = jnp.sum(jnp.where(exp_id == first, router, 0.0), axis=0, keepdims=True)
    chosen1 = jnp.sum(jnp.where(exp_id == second, router, 0.0), axis=0, keepdims=True)
    total = chosen0 + chosen1
    total = jnp.where(total > 0.0, total, 1.0)
    gate0, gate1 = chosen0 / total, chosen1 / total
    for i, row in enumerate((chosen0, chosen1, gate0, gate1)):
        gates_ref[i : i + 1, :] = row
    gates_ref[4:8, :] = jnp.zeros((4, nt), F32)

    zero_rows = jnp.zeros((5, nt), F32)
    parts0 = jnp.concatenate([v.astype(F32) for v in split3(gate0)] + [zero_rows], axis=0).astype(BF)
    parts1 = jnp.concatenate([v.astype(F32) for v in split3(gate1)] + [zero_rows], axis=0).astype(BF)
    pad_ref[...] = jnp.zeros(pad_ref.shape, F32)
    token_rows = Exchange(send_ref, recv_ref, row_ssem, row_rsem, local_sem.at[1], cp, exps)

    def row_chunk(r, carry):
        base = ((chip + r) % chips) * (2 * cp)
        row = iota((2 * cp, nt), 0) + base
        pick0, pick1 = hot(row == place0), hot(row == place1)
        rows = dot(pick0 + pick1, h2_ref[...])
        spread = dot_nt(parts0, pick0) + dot_nt(parts1, pick1)
        line = iota((2 * cp, feat), 0)
        for j in range(2):
            for k in range(3):
                pad_ref[j : j + 1, k * 128 : k * 128 + cp] = spread[k : k + 1, j * cp : (j + 1) * cp]
            rows = rows + jnp.where(line == j * cp + cap, pad_ref[j : j + 1, :], 0.0)
        send_ref[rows_at(base, 2 * cp), :] = rows.astype(BF)
        token_rows.start(r)
        return carry

    lax.fori_loop(0, chips, row_chunk, 0)

    if pair:
        small_copy.wait_send()
        dense_copy.wait_send()
        swap_copy.wait_send()
        inner_copy.wait()
        outer_copy.wait()
    cot_rows.finish()
    token_rows.finish()


def run_front(images, cot, picks, order_row, order_col, small, dense, weights, *, nt, sp, cap, cp, ck, exps):
    imgs, seq, feat = images.shape
    pair = weights is not None
    rows = exps * cp
    vmem, hbm = pl.BlockSpec(memory_space=pltpu.VMEM), pl.BlockSpec(memory_space=pl.ANY)
    dma = pltpu.SemaphoreType.DMA
    outs = [
        shape((feat, 4 * feat), BF),
        shape((2,) + small.shape if pair else small.shape, BF),
        shape((nt, feat), BF),
        shape((nt, 3 * feat), BF),
        shape((nt, feat), BF),
        shape((nt, feat), F32),
        shape((nt, feat), BF),
        shape((exps, nt), F32),
        shape((8, nt), F32),
        shape((8, nt), I32),
        shape((rows, feat), BF),
        shape((rows, feat), BF),
    ]
    ins = [images, cot, picks, order_row, order_col, small, dense]
    if pair:
        ins += list(weights)
        outs += [shape(w.shape, BF) for w in weights]
    return pl.pallas_call(
        functools.partial(
            front_kernel, pair=pair, imgs=imgs, seq=seq, sp=sp, nt=nt, cap=cap, cp=cp, ck=ck, exps=exps
        ),
        out_shape=outs,
        in_specs=[vmem] * 7 + [hbm] * (len(ins) - 7),
        out_specs=[vmem] * 10 + [hbm] * (len(outs) - 10),
        scratch_shapes=[
            pltpu.VMEM((nt, feat), BF),
            pltpu.VMEM((nt, feat), BF),
            pltpu.VMEM((rows, feat), BF),
            pltpu.VMEM((rows, feat), BF),
            pltpu.VMEM((8, feat), F32),
            dma((exps,)), dma((exps,)), dma((exps,)), dma((exps,)), dma((2,)), dma((5,)), dma((5,)),
        ],
        compiler_params=pltpu.CompilerParams(
            vmem_limit_bytes=VMEM_CAP, collective_id=3, has_side_effects=True
        ),
        cost_estimate=pl.CostEstimate(flops=20_000_000_000, bytes_accessed=60_000_000, transcendentals=0),
    )(*ins)


def gelu_both(hidden):
    size = jnp.abs(hidden)
    bell = jnp.exp(hidden * hidden * -0.5)
    t = 1.0 / (1.0 + TAIL_C * size)
    poly = jnp.full_like(t, TAIL[0])
    for c in TAIL[1:]:
        poly = poly * t + c
    tail = bell * poly
    below = jnp.where(hidden >= 0.0, 1.0 - tail, tail)
    return hidden * below, below + hidden * (bell * INV_SQRT_TAU)


def expert_kernel(recv_ref, dfin_ref, *refs, pieces, tiles, cap, cp, exps, block):
    weights = refs[: 2 * pieces]
    act_ref, dhid_ref, rows_ref, dres_ref, result_ref, drows_ref, sum_r, sum_d, wi_ref, wo_ref, dfin_c = refs[2 * pieces :]
    j = pl.program_id(0)
    rows, feat = rows_ref.shape
    pair = 2 * cp
    apart = recv_ref.shape[0] // exps
    sub = iota((pair, 128), 0)
    lane = iota((pair, 128), 1)
    upper = sub < cp
    diag = lane == jnp.where(upper, sub, sub - cp)

    @pl.when(j == 0)
    def _():
        sum_r[...] = jnp.zeros_like(sum_r)
        sum_d[...] = jnp.zeros_like(sum_d)

        def gate_rows(i, carry):
            at = rows_at(i * pair, pair)
            full = rows_at(i * 2 * apart, 2 * apart)

            def compact(ref):
                values = ref[full, :].astype(F32)
                if apart == cp:
                    return values
                return jnp.concatenate([values[:cp], values[apart : apart + cp]], axis=0)

            recv, dfin = compact(recv_ref), compact(dfin_ref)
            rows_ref[at, :] = recv.astype(BF)
            dfin_c[at, :] = dfin.astype(BF)
            lead = recv[:, 0:384]
            place = iota((pair, 384), 0)
            spread = []
            for k in range(2):
                row = jnp.sum(jnp.where(place == k * cp + cap, lead, 0.0), axis=0, keepdims=True)
                spread.append(row[:, 0:128] + row[:, 128:256] + row[:, 256:384])
            both = jnp.where(upper, spread[0], spread[1])
            gate = jnp.sum(jnp.where(diag, both, 0.0), axis=1, keepdims=True)
            dres_ref[at, :] = (gate * dfin).astype(BF)
            return carry

        lax.fori_loop(0, exps // 2, gate_rows, 0)

    done = 0
    for i in range(pieces):

        @pl.when((j >= done) & (j < done + tiles[i]))
        def _(i=i):
            wi_ref[...] = weights[2 * i][...]
            wo_ref[...] = weights[2 * i + 1][...]

        done += tiles[i]

    for i in range(rows // block):
        at = pl.ds(i * block, block)
        hidden = dot(rows_ref[at, :], wi_ref[...])
        act, slope = gelu_both(hidden)
        act = act.astype(BF)
        dact = dot_nt(dres_ref[at, :], wo_ref[...])
        dhid = (slope * dact).astype(BF)
        act_ref[at, :] = act
        dhid_ref[at, :] = dhid
        sum_r[at, :] += dot(act, wo_ref[...])
        sum_d[at, :] += dot_nt(dhid, wi_ref[...])

    @pl.when(j == done - 1)
    def _():
        def finish(i, carry):
            at = pl.ds(pl.multiple_of(i * pair, 16), pair)
            result = sum_r[at, :].astype(BF)
            result_ref[at, :] = result
            dgate = jnp.sum(result.astype(F32) * dfin_c[at, :].astype(F32), axis=1, keepdims=True)
            line = iota((pair, feat), 0)
            drows = sum_d[at, :]
            for k in range(2):
                mine = upper if k == 0 else ~upper
                row = jnp.sum(jnp.where(diag & mine, dgate, 0.0), axis=0, keepdims=True)
                wide = jnp.concatenate(
                    [v.astype(F32) for v in split3(row)] + [jnp.zeros((1, feat - 384), F32)], axis=1
                )
                drows = drows + jnp.where(line == k * cp + cap, wide, 0.0)
            drows_ref[at, :] = drows.astype(BF)
            return carry

        lax.fori_loop(0, exps // 2, finish, 0)


def run_expert(recv, dfin, weights, cap, cp, exps):
    full, feat = recv.shape
    rows = exps * cp
    tile = min(TILE, min(w[0].shape[1] for w in weights))
    tiles = [w[0].shape[1] // tile for w in weights]
    total = sum(tiles)
    whole = pl.BlockSpec((rows, feat), lambda j: (0, 0))
    wide_in = pl.BlockSpec((full, feat), lambda j: (0, 0))
    in_specs, flat, done = [wide_in, wide_in], [], 0
    for (inner, outer), count in zip(weights, tiles):
        in_specs.append(
            pl.BlockSpec((feat, tile), lambda j, d=done, c=count: (0, jnp.clip(j - d, 0, c - 1)))
        )
        in_specs.append(
            pl.BlockSpec((tile, feat), lambda j, d=done, c=count: (jnp.clip(j - d, 0, c - 1), 0))
        )
        flat += [inner, outer]
        done += count
    wide = pl.BlockSpec((rows, tile), lambda j: (0, j))
    block = next(b for b in (352, 384, 256, 128, 16) if rows % b == 0)
    kernel = functools.partial(
        expert_kernel, pieces=len(weights), tiles=tiles, cap=cap, cp=cp, exps=exps, block=block
    )
    return pl.pallas_call(
        kernel,
        grid=(total,),
        in_specs=in_specs,
        out_specs=[wide, wide, whole, whole, whole, whole],
        out_shape=[
            shape((rows, total * tile), BF),
            shape((rows, total * tile), BF),
            shape((rows, feat), BF),
            shape((rows, feat), BF),
            shape((rows, feat), BF),
            shape((rows, feat), BF),
        ],
        scratch_shapes=[
            pltpu.VMEM((rows, feat), F32),
            pltpu.VMEM((rows, feat), F32),
            pltpu.VMEM((feat, tile), BF),
            pltpu.VMEM((tile, feat), BF),
            pltpu.VMEM((rows, feat), BF),
        ],
        compiler_params=pltpu.CompilerParams(
            vmem_limit_bytes=VMEM_CAP, dimension_semantics=("arbitrary",)
        ),
        cost_estimate=pl.CostEstimate(
            flops=8 * rows * feat * total * tile, bytes_accessed=30_000_000, transcendentals=0
        ),
    )(recv, dfin, *flat)


def middle_kernel(
    back_ref, place_col_ref, place_ref, picks_ref, gates_ref, router_ref, router_w_ref, h2_ref, after_ref, cot_ref,
    norm_ref, w_ref, dafter_ref, dattn_ref, dctx_ref, grad_router_ref, grad_vec_ref, dlog_ref, *, cap, cp, exps
):
    rows, feat = back_ref.shape
    nt = cot_ref.shape[0]
    spare = hot(iota((exps, rows), 1) == iota((exps, rows), 0) * cp + cap)
    lines = dot(spare, back_ref[:, 0:384])
    exp_id = iota((exps, nt), 0)
    dgate, match = [], []
    for k in range(2):
        pick = picks_ref[k : k + 1, :]
        place = place_ref[k : k + 1, :]
        slot = jnp.where(place >= 0, place - pick * cp, -1)
        slot_hot = hot(iota((128, nt), 0) == slot)
        found = (
            dot(lines[:, 0:128].astype(BF), slot_hot)
            + dot(lines[:, 128:256].astype(BF), slot_hot)
            + dot(lines[:, 256:384].astype(BF), slot_hot)
        )
        match.append(jnp.where(exp_id == pick, 1.0, 0.0))
        dgate.append(jnp.sum(match[k] * found, axis=0, keepdims=True))
    chosen = (gates_ref[0:1, :], gates_ref[1:2, :])
    total = chosen[0] + chosen[1]
    total = jnp.where(total > 0.0, total, 1.0)
    cross = (dgate[0] * chosen[0] + dgate[1] * chosen[1]) / (total * total)
    drouter = match[0] * (dgate[0] / total - cross) + match[1] * (dgate[1] / total - cross)
    router = router_ref[...]
    dlogits = (router * (drouter - jnp.sum(router * drouter, axis=0, keepdims=True))).astype(BF)
    dlog_ref[...] = dlogits
    grad_router_ref[...] = dot(dlogits, h2_ref[...])
    norm = norm_ref[...].astype(F32)
    grad_vec_ref[...] = jnp.zeros_like(grad_vec_ref)

    def tokens(i, carry):
        at = pl.ds(pl.multiple_of(i * BLOCK, BLOCK), BLOCK)
        slots = iota((BLOCK, rows), 1)
        pick = hot((slots == place_col_ref[at, 0:1]) | (slots == place_col_ref[at, 1:2]))
        dh2 = dot(pick, back_ref[...]) + dot_tn(dlog_ref[:, at], router_w_ref[...])
        normed, rstd = normed_of(after_ref[at, :])
        grad_vec_ref[0:1, :] += jnp.sum(dh2 * normed, axis=0, keepdims=True)
        grad_vec_ref[1:2, :] += jnp.sum(dh2, axis=0, keepdims=True)
        dafter = cot_ref[at, :].astype(F32) + norm_back_rows(dh2, normed, rstd, norm[2:3])
        dafter_ref[at, :] = dafter
        dattn = dafter.astype(BF)
        dattn_ref[at, :] = dattn
        dctx_ref[at, :] = dot_nt(dattn, w_ref[:, 3 * feat : 4 * feat]).astype(BF)
        return carry

    lax.fori_loop(0, nt // BLOCK, tokens, 0)


def attention_back_kernel(mixed_ref, dctx_ref, dmixed_ref, *, imgs, seq, sp):
    nt, feat = dctx_ref.shape
    pairs = feat // 128
    key_ok = iota((sp, sp), 1) < seq
    left = iota((sp, 128), 1) < HDIM

    def attend(i, carry):
        rows = pl.ds(pl.multiple_of((i // pairs) * sp, 16), sp)
        col = (i % pairs) * 128
        at_q = pl.ds(pl.multiple_of(col, 128), 128)
        at_k = pl.ds(pl.multiple_of(col + feat, 128), 128)
        at_v = pl.ds(pl.multiple_of(col + 2 * feat, 128), 128)
        query, keys, values = mixed_ref[rows, at_q], mixed_ref[rows, at_k], mixed_ref[rows, at_v]
        dctx = dctx_ref[rows, at_q]
        zero = jnp.zeros_like(query)
        dq = dk = dv = 0.0
        for mask in (left, ~left):
            query_h = jnp.where(mask, query, zero)
            keys_h = jnp.where(mask, keys, zero)
            dctx_h = jnp.where(mask, dctx, zero)
            scores = jnp.where(key_ok, dot_nt(query_h, keys) * SCALE, NEG)
            top = jnp.max(scores, axis=-1, keepdims=True)
            grown = jnp.exp(scores - top)
            probs = grown / jnp.sum(grown, axis=-1, keepdims=True)
            dv = dv + dot_tn(probs.astype(BF), dctx_h)
            dweights = dot_nt(dctx_h, values)
            dscores = (probs * (dweights - jnp.sum(probs * dweights, axis=-1, keepdims=True))).astype(BF)
            dq = dq + dot(dscores, keys_h)
            dk = dk + dot_tn(dscores, query_h)
        dmixed_ref[rows, at_q] = (dq * SCALE).astype(BF)
        dmixed_ref[rows, at_k] = (dk * SCALE).astype(BF)
        dmixed_ref[rows, at_v] = dv.astype(BF)
        return carry

    dmixed_ref[pl.ds(imgs * sp, nt - imgs * sp), :] = jnp.zeros((nt - imgs * sp, 3 * feat), BF)
    lax.fori_loop(0, imgs * pairs, attend, 0)


def output_kernel(back_ref, place_col_ref, gates_col_ref, after_ref, out_ref):
    rows, feat = back_ref.shape
    nt = after_ref.shape[0]

    def tokens(i, carry):
        at = pl.ds(pl.multiple_of(i * BLOCK, BLOCK), BLOCK)
        slots = iota((BLOCK, rows), 1)
        final = after_ref[at, :]
        for k in range(2):
            pick = hot(slots == place_col_ref[at, k : k + 1])
            final = final + gates_col_ref[at, k : k + 1] * dot(pick, back_ref[...])
        out_ref[at, :] = final.astype(BF)
        return carry

    lax.fori_loop(0, nt // BLOCK, tokens, 0)


CHUNKS = 4
PEERS = 8


def reduce_kernel(dense_ref, small_ref, out_ref, small_out, from_core, pair_sum, from_dp, dp_sum, from_peer, mine,
                  small_in, core_send, core_recv, dp_send, dp_recv, peer_send, peer_recv, gather_send, gather_recv,
                  last_send, last_recv, small_send, small_recv):
    at_dp, at_exp = lax.axis_index("dp"), lax.axis_index("expert")
    core, chip = at_exp % 2, at_exp // 2
    rows, cols = dense_ref.shape
    half, quarter = rows // 2, rows // 4
    piece, width = quarter // CHUNKS, cols // PEERS
    other_core = (at_dp, chip * 2 + (1 - core))
    other_dp = (1 - at_dp, at_exp)
    peers = [(at_dp, ((chip + r) % PEERS) * 2 + core) for r in range(1, PEERS)]

    barrier = pltpu.get_barrier_semaphore()
    for device in [other_core, other_dp] + peers:
        pl.semaphore_signal(barrier, inc=1, device_id=device, device_id_type=pl.DeviceIdType.MESH)
    pl.semaphore_wait(barrier, PEERS + 1)

    def copy(source, target, send, recv, device):
        return pltpu.make_async_remote_copy(
            src_ref=source, dst_ref=target, send_sem=send, recv_sem=recv,
            device_id=device, device_id_type=pl.DeviceIdType.MESH,
        )

    def spot(part, owner, k):
        return pl.ds(pl.multiple_of(part * half + owner * quarter + k * piece, 16), piece)

    started = []

    def go(*args, keep=True):
        made = copy(*args)
        made.start()
        if keep:
            started.append(made)
        return made

    steps = [other_core, other_dp] + [(at_dp, (chip ^ bit) * 2 + core) for bit in (1, 2, 4)]
    small_out[...] = small_ref[...]

    def small_go(i):
        return go(small_out, small_in.at[i], small_send.at[i], small_recv.at[i], steps[i], keep=False)

    def small_take(made, i):
        made.wait()
        small_out[...] = small_out[...] + small_in[i]

    core_copies = [
        [
            go(dense_ref.at[spot(part, 1 - core, k), :], from_core.at[part, k], core_send.at[part, k],
               core_recv.at[part, k], other_core)
            for part in range(2)
        ]
        for k in range(CHUNKS)
    ]
    small_copy = small_go(0)
    dp_copies = []
    for k in range(CHUNKS):
        for part in range(2):
            core_copies[k][part].wait_recv()
            pair_sum[part, k] = (
                dense_ref[spot(part, core, k), :].astype(F32) + from_core[part, k].astype(F32)
            ).astype(BF)
        dp_copies.append(go(pair_sum.at[1 - at_dp, k], from_dp.at[k], dp_send.at[k], dp_recv.at[k], other_dp))
    small_take(small_copy, 0)
    small_copy = small_go(1)
    peer_copies = []
    for k in range(CHUNKS):
        dp_copies[k].wait_recv()
        dp_sum[k] = (pair_sum[at_dp, k].astype(F32) + from_dp[k].astype(F32)).astype(BF)
        peer_copies.append([
            go(dp_sum.at[k, :, pl.ds(pl.multiple_of(((chip + r) % PEERS) * width, 128), width)],
               from_peer.at[k, r - 1], peer_send.at[k, r - 1], peer_recv.at[k, r - 1], peers[r - 1])
            for r in range(1, PEERS)
        ])
        if k == 0:
            small_take(small_copy, 1)
            small_copy = small_go(2)
    own = pl.ds(pl.multiple_of(chip * width, 128), width)
    gather_copies = []
    for k in range(CHUNKS):
        total = dp_sum[k, :, own].astype(F32)
        for r in range(1, PEERS):
            peer_copies[k][r - 1].wait_recv()
            total = total + from_peer[k, r - 1].astype(F32)
        mine[k] = total.astype(BF)
        place = pl.ds(pl.multiple_of(core * quarter + k * piece, 16), piece)
        out_ref[place, own] = mine[k]
        gather_copies.append([
            go(mine.at[k], out_ref.at[place, own], gather_send.at[k, r - 1], gather_recv.at[k, r - 1], peers[r - 1])
            for r in range(1, PEERS)
        ])
        if k < 2:
            small_take(small_copy, 2 + k)
            small_copy = small_go(3 + k)
    small_take(small_copy, 4)
    last_copies = []
    for k in range(CHUNKS):
        for made in gather_copies[k]:
            made.wait_recv()
        place = pl.ds(pl.multiple_of(core * quarter + k * piece, 16), piece)
        last_copies.append(go(out_ref.at[place, :], out_ref.at[place, :], last_send.at[k], last_recv.at[k], other_core))
    for made in last_copies:
        made.wait_recv()
    for made in started:
        made.wait_send()


def reduce_all(dense, small):
    rows, cols = dense.shape
    piece, width = rows // 4 // CHUNKS, cols // PEERS
    dma = pltpu.SemaphoreType.DMA
    vmem = pl.BlockSpec(memory_space=pltpu.VMEM)
    return pl.pallas_call(
        reduce_kernel,
        out_shape=(shape((rows // 2, cols), BF), shape(small.shape, F32)),
        in_specs=[vmem, vmem],
        out_specs=(vmem, vmem),
        scratch_shapes=[
            pltpu.VMEM((2, CHUNKS, piece, cols), BF),
            pltpu.VMEM((2, CHUNKS, piece, cols), BF),
            pltpu.VMEM((CHUNKS, piece, cols), BF),
            pltpu.VMEM((CHUNKS, piece, cols), BF),
            pltpu.VMEM((CHUNKS, PEERS - 1, piece, width), BF),
            pltpu.VMEM((CHUNKS, piece, width), BF),
            pltpu.VMEM((5,) + small.shape, F32),
            dma((2, CHUNKS)), dma((2, CHUNKS)),
            dma((CHUNKS,)), dma((CHUNKS,)),
            dma((CHUNKS, PEERS - 1)), dma((CHUNKS, PEERS - 1)),
            dma((CHUNKS, PEERS - 1)), dma((CHUNKS, PEERS - 1)),
            dma((CHUNKS,)), dma((CHUNKS,)),
            dma((5,)), dma((5,)),
        ],
        compiler_params=pltpu.CompilerParams(
            vmem_limit_bytes=VMEM_CAP, collective_id=1, has_side_effects=True
        ),
        cost_estimate=pl.CostEstimate(flops=1_000_000_000, bytes_accessed=200_000_000, transcendentals=0),
    )(dense, small)


def total_kernel(part_ref, out_ref, landed, send_sem, recv_sem, *, shards, exps):
    at_dp, at_exp = lax.axis_index("dp"), lax.axis_index("expert")
    count = shards * exps
    me = at_dp * exps + at_exp
    devices = [(((me + r) % count) // exps, ((me + r) % count) % exps) for r in range(1, count)]
    barrier = pltpu.get_barrier_semaphore()
    for device in devices:
        pl.semaphore_signal(barrier, inc=1, device_id=device, device_id_type=pl.DeviceIdType.MESH)
    pl.semaphore_wait(barrier, count - 1)
    copies = []
    for r, device in enumerate(devices):
        copies.append(pltpu.make_async_remote_copy(
            src_ref=part_ref, dst_ref=landed.at[r], send_sem=send_sem.at[r], recv_sem=recv_sem.at[r],
            device_id=device, device_id_type=pl.DeviceIdType.MESH,
        ))
        copies[-1].start()
    total = part_ref[...]
    for r, made in enumerate(copies):
        made.wait_recv()
        total = total + landed[r]
    out_ref[...] = total
    for made in copies:
        made.wait_send()


def total_of(part, shards, exps):
    count = shards * exps
    vmem = pl.BlockSpec(memory_space=pltpu.VMEM)
    return pl.pallas_call(
        functools.partial(total_kernel, shards=shards, exps=exps),
        out_shape=shape((8, 128), F32),
        in_specs=[vmem],
        out_specs=vmem,
        scratch_shapes=[
            pltpu.VMEM((count - 1, 8, 128), F32),
            pltpu.SemaphoreType.DMA((count - 1,)),
            pltpu.SemaphoreType.DMA((count - 1,)),
        ],
        compiler_params=pltpu.CompilerParams(collective_id=2, has_side_effects=True),
    )(jnp.full((8, 128), part, F32))[0, 0]


def adam_step(weight, first, second, grad, rate, decay):
    new_first = BETA_ONE * first + (1.0 - BETA_ONE) * grad
    new_second = BETA_TWO * second + (1.0 - BETA_TWO) * grad * grad
    first_hat = new_first / (1.0 - BETA_ONE**STEP)
    second_hat = new_second / (1.0 - BETA_TWO**STEP)
    new_weight = weight - rate * (first_hat / (jnp.sqrt(second_hat) + ADAM_EPS) + decay * weight)
    return (new_weight, new_first, new_second)


def body(
    images,
    cotangent,
    routes,
    priority,
    qkv_weight,
    qkv_first,
    qkv_second,
    proj_weight,
    proj_first,
    proj_second,
    router_weight,
    router_first,
    router_second,
    norm_params,
    norm_first,
    norm_second,
    inner_weight,
    inner_first,
    inner_second,
    outer_weight,
    outer_first,
    outer_second,
):
    exps = lax.axis_size("expert")
    shards = lax.axis_size("dp")
    imgs, seq, feat = images.shape
    tok = imgs * seq
    cap = (18 * tok + 8 * exps - 1) // (8 * exps)
    cp = up(cap + 1, 8)
    sp = up(seq, 16)
    nt = up(imgs * sp, BLOCK)
    rows = exps * cp
    at_dp, at_exp = lax.axis_index("dp"), lax.axis_index("expert")
    ring = [(0, 1), (1, 0)]
    shard_rows = qkv_weight.shape[0]
    by_kernel = shards == 2 and exps == 2 * PEERS

    def spread(values, fill=0):
        values = jnp.pad(values, ((0, 0), (0, sp - seq), (0, 0)), constant_values=fill)
        values = values.reshape(imgs * sp, values.shape[-1])
        return jnp.pad(values, ((0, nt - imgs * sp), (0, 0)), constant_values=fill)

    def unspread(values):
        return values[: imgs * sp].reshape(imgs, sp, -1)[:, :seq]

    def exchange(values):
        return lax.all_to_all(
            values.reshape(exps, cp, feat), "expert", split_axis=0, concat_axis=0, tiled=True
        ).reshape(rows, feat)

    dense = jnp.concatenate([qkv_weight.astype(BF), proj_weight.astype(BF)], axis=1)
    small = jnp.concatenate([router_weight.astype(BF).T, norm_params.astype(BF)], axis=0)
    small = jnp.pad(small, ((0, up(exps + 4, 16) - exps - 4), (0, 0)))
    inner_b, outer_b = inner_weight[0].astype(BF), outer_weight[0].astype(BF)
    if shards > 2:
        dense = lax.all_gather(dense, "dp", axis=0, tiled=True)
        small = lax.all_gather(small, "dp", axis=1, tiled=True)
    picks = jnp.concatenate([spread(routes, -1).T, jnp.full((6, nt), -1, I32)], axis=0)
    order = priority[0] + (priority[0] // seq) * (sp - seq)
    order = jnp.pad(order, (0, nt - tok), constant_values=-1)
    w_full, small, h1, mixed, context, after, h2, router, gates, place, recv, recv_cot, *others = run_front(
        images, cotangent, picks, order[None, :], order[:, None], small, dense,
        (inner_b, outer_b) if shards == 2 else None,
        nt=nt, sp=sp, cap=cap, cp=up(cap + 1, 16), ck=cp, exps=exps,
    )
    if shards == 2:
        small = jnp.concatenate([small[0], small[1]], axis=1)
        weights = ((inner_b, outer_b), tuple(others))
    else:
        weights = (
            (
                lax.all_gather(inner_b, "dp", axis=1, tiled=True),
                lax.all_gather(outer_b, "dp", axis=0, tiled=True),
            ),
        )
    router_t, norm_b = small[:exps], small[exps : exps + 4]
    x = spread(images)
    cot = spread(cotangent)
    place_col = place[0:2].T
    gates_col = gates[2:4].T

    act, dhid, recv, dres, result, drows = run_expert(recv, recv_cot, weights, cap, cp, exps)
    back_grad = exchange(drows)

    def tn(left, right):
        return lax.dot_general(left, right, (((0,), (0,)), ((), ())), preferred_element_type=F32)

    if shards == 2:
        mid = inner_b.shape[1]
        far_inner, far_outer = tn(recv, dhid[:, mid:]).astype(BF), tn(act[:, mid:], dres).astype(BF)
        far_inner, far_outer, recv, act = lax.optimization_barrier((far_inner, far_outer, recv, act))
        sent_inner = lax.ppermute(far_inner, "dp", ring)
        sent_outer = lax.ppermute(far_outer, "dp", ring)
        own_inner, own_outer = tn(recv, dhid[:, :mid]), tn(act[:, :mid], dres)
        back_grad, own_inner, own_outer = lax.optimization_barrier((back_grad, own_inner, own_outer))
    else:
        shard_inner = lax.psum_scatter(
            tn(recv, dhid).astype(BF), "dp", scatter_dimension=1, tiled=True
        ).astype(F32)[None]
        shard_outer = lax.psum_scatter(
            tn(act, dres).astype(BF), "dp", scatter_dimension=0, tiled=True
        ).astype(F32)[None]

    dafter, dattn, dctx, grad_router_t, grad_two = call(
        functools.partial(middle_kernel, cap=cap, cp=cp, exps=exps),
        (
            shape((nt, feat), F32),
            shape((nt, feat), BF),
            shape((nt, feat), BF),
            shape((exps, feat), F32),
            shape((8, feat), F32),
        ),
        back_grad, place_col, place, picks, gates, router, router_t, h2, after, cot, norm_b, w_full,
        scratch=[pltpu.VMEM((exps, nt), BF)],
        flops=2 * rows * nt * feat + 2 * nt * feat * feat, moved=14_000_000,
    )
    grad_proj = tn(context, dattn)
    dmixed = call(
        functools.partial(attention_back_kernel, imgs=imgs, seq=seq, sp=sp),
        shape((nt, 3 * feat), BF),
        mixed, dctx,
        flops=14 * nt * sp * feat, moved=8_000_000,
    )
    grad_qkv = tn(h1, dmixed)
    result_sent, _ = lax.optimization_barrier((result, back_grad))
    returned = exchange(result_sent)
    output = unspread(
        call(
            output_kernel,
            shape((nt, feat), BF),
            returned, place_col, gates_col, after,
            flops=4 * rows * nt * feat, moved=6_000_000,
        )
    )

    dh1 = lax.dot_general(
        dmixed, w_full[:, : 3 * feat], (((1,), (1,)), ((), ())), preferred_element_type=F32
    )
    norm_vals = norm_b.astype(F32)
    normed, rstd = normed_of(x.astype(F32))
    input_grad = unspread((dafter + norm_back_rows(dh1, normed, rstd, norm_vals[0])).astype(BF))
    grad_vector = jnp.stack(
        [jnp.sum(dh1 * normed, axis=0), jnp.sum(dh1, axis=0), grad_two[0], grad_two[1]]
    )

    dense_grad = jnp.concatenate([grad_qkv.astype(BF), grad_proj.astype(BF)], axis=1)
    small_grad = jnp.concatenate([grad_router_t, grad_vector], axis=0)
    small_grad = jnp.pad(small_grad, ((0, up(exps + 4, 8) - exps - 4), (0, 0)))
    dense_grad, output, input_grad = lax.optimization_barrier((dense_grad, output, input_grad))
    if by_kernel:
        shard_dense, small_grad = reduce_all(dense_grad, small_grad)
        if shards == 2:
            sent_inner, sent_outer, shard_dense = lax.optimization_barrier((sent_inner, sent_outer, shard_dense))
        shard_dense = shard_dense.astype(F32)
    else:
        dense_grad = lax.psum(dense_grad, ("dp", "expert"))
        small_grad = lax.psum(small_grad, ("dp", "expert"))
        shard_dense = lax.dynamic_slice_in_dim(dense_grad, at_dp * shard_rows, shard_rows, 0).astype(F32)
    if shards == 2:
        shard_inner = (own_inner + sent_inner.astype(F32))[None]
        shard_outer = (own_outer + sent_outer.astype(F32))[None]
    shard_small = lax.dynamic_slice_in_dim(small_grad, at_dp * shard_rows, shard_rows, 1)
    shard_qkv, shard_proj = shard_dense[:, : 3 * feat], shard_dense[:, 3 * feat :]
    shard_router, shard_vector = shard_small[:exps].T, shard_small[exps : exps + 4]

    dense_squares = jnp.sum(shard_dense * shard_dense) + jnp.sum(shard_small * shard_small)
    expert_squares = jnp.sum(shard_inner * shard_inner) + jnp.sum(shard_outer * shard_outer)
    local_squares = expert_squares + jnp.where(at_exp == 0, dense_squares, jnp.float32(0.0))
    if by_kernel:
        grad_norm = jnp.sqrt(total_of(local_squares, shards, exps))
    else:
        grad_norm = jnp.sqrt(lax.psum(local_squares, ("dp", "expert")))
    clip = CLIP_NORM / jnp.maximum(grad_norm, CLIP_NORM)
    qkv_new = adam_step(qkv_weight, qkv_first, qkv_second, shard_qkv * clip, RATE_MATRIX, DECAY)
    proj_new = adam_step(proj_weight, proj_first, proj_second, shard_proj * clip, RATE_MATRIX, DECAY)
    router_new = adam_step(
        router_weight, router_first, router_second, shard_router * clip, RATE_MATRIX, DECAY
    )
    norm_new = adam_step(norm_params, norm_first, norm_second, shard_vector * clip, RATE_VECTOR, 0.0)
    inner_new = adam_step(
        inner_weight, inner_first, inner_second, shard_inner * clip, RATE_MATRIX, DECAY
    )
    outer_new = adam_step(
        outer_weight, outer_first, outer_second, shard_outer * clip, RATE_MATRIX, DECAY
    )
    return (
        output,
        input_grad,
        grad_norm,
        *qkv_new,
        *proj_new,
        *router_new,
        *norm_new,
        *inner_new,
        *outer_new,
    )


def solution(mesh):
    tokens = P(("dp", "expert"), None, None)
    dense = P("dp", None)
    vector = P(None, "dp")
    inner = P("expert", None, "dp")
    outer = P("expert", "dp", None)
    return jax.shard_map(
        body,
        mesh=mesh,
        in_specs=(tokens, tokens, tokens, P(("dp", "expert"), None))
        + (dense,) * 9
        + (vector,) * 3
        + (inner,) * 3
        + (outer,) * 3,
        out_specs=(tokens, tokens, P())
        + (dense,) * 9
        + (vector,) * 3
        + (inner,) * 3
        + (outer,) * 3,
        check_vma=False,
    )
```

```python
import functools

import jax
import jax.numpy as jnp
from jax import lax
from jax.experimental import pallas as pl
from jax.experimental.pallas import tpu as pltpu
from jax.sharding import PartitionSpec as P

HEADS = 12
HDIM = 64
STEP = 10
SCALE = float(HDIM) ** (-0.5)

LN_EPS = 1e-06
BETA_ONE = 0.9
BETA_TWO = 0.999
ADAM_EPS = 1e-08
RATE_MATRIX = 0.06
RATE_VECTOR = 0.4
DECAY = 0.1
CLIP_NORM = 1.0

BF = jnp.bfloat16
F32 = jnp.float32
I32 = jnp.int32
NEG = -1e30
BLOCK = 128
BIG = 320
TILE = 512
VMEM_CAP = 60 * 1024 * 1024

TAIL_C = 0.31
TAIL = (
    0.03601999959102291,
    -0.14256280554259812,
    0.15715769015924325,
    -0.017324403713695688,
    0.11173640397253812,
    0.10712570259185507,
    0.12420698490047791,
    0.12363964793348867,
    7.947371491008614e-07,
)
INV_SQRT_TAU = 0.3989422804014327


def up(value, step):
    return -(-value // step) * step


def dot(left, right):
    return lax.dot_general(left, right, (((1,), (0,)), ((), ())), preferred_element_type=F32)


def dot_nt(left, right):
    return lax.dot_general(left, right, (((1,), (1,)), ((), ())), preferred_element_type=F32)


def dot_tn(left, right):
    return lax.dot_general(left, right, (((0,), (0,)), ((), ())), preferred_element_type=F32)


def iota(shape, axis):
    return lax.broadcasted_iota(I32, shape, axis)


def hot(mask):
    return jnp.where(mask, 1.0, 0.0).astype(BF)


def normed_of(values):
    centre = jnp.mean(values, axis=-1, keepdims=True)
    centered = values - centre
    rstd = lax.rsqrt(jnp.mean(centered * centered, axis=-1, keepdims=True) + LN_EPS)
    return centered * rstd, rstd


def norm_back_rows(grad, normed, rstd, gain):
    scaled = grad * gain
    inner_mean = jnp.mean(scaled, axis=-1, keepdims=True)
    cross_mean = jnp.mean(scaled * normed, axis=-1, keepdims=True)
    return rstd * (scaled - inner_mean - normed * cross_mean)


def split3(values):
    high = values.astype(BF)
    rest = values - high.astype(F32)
    mid = rest.astype(BF)
    low = (rest - mid.astype(F32)).astype(BF)
    return high, mid, low


def call(kernel, out_shape, *args, scratch=(), specs=None, flops=0, moved=0):
    vmem = pl.BlockSpec(memory_space=pltpu.VMEM)
    single = not isinstance(out_shape, (tuple, list))
    return pl.pallas_call(
        kernel,
        out_shape=out_shape,
        in_specs=[vmem] * len(args) if specs is None else specs,
        out_specs=vmem if single else [vmem] * len(out_shape),
        scratch_shapes=list(scratch),
        compiler_params=pltpu.CompilerParams(vmem_limit_bytes=VMEM_CAP),
        cost_estimate=pl.CostEstimate(flops=int(flops), bytes_accessed=int(moved), transcendentals=0),
    )(*args)


def shape(dims, kind):
    return jax.ShapeDtypeStruct(dims, kind)


MESH = pl.DeviceIdType.MESH


def remote(source, target, send, recv, device):
    return pltpu.make_async_remote_copy(
        src_ref=source, dst_ref=target, send_sem=send, recv_sem=recv, device_id=device, device_id_type=MESH
    )


def rows_at(start, size, unit=16):
    return pl.ds(pl.multiple_of(start, unit), size)


class Exchange:
    def __init__(self, send, recv, send_sem, recv_sem, local_sem, cp, exps):
        self.send, self.recv, self.send_sem, self.recv_sem, self.local_sem = send, recv, send_sem, recv_sem, local_sem
        self.cp, self.chips = cp, exps // 2
        self.at_dp, self.me = lax.axis_index("dp"), lax.axis_index("expert")
        self.core, self.chip = self.me % 2, self.me // 2

    def out(self, r, j):
        there = ((self.chip + r) % self.chips) * 2 + j
        return remote(
            self.send.at[rows_at(there * self.cp, self.cp), :],
            self.recv.at[rows_at(self.me * self.cp, self.cp), :],
            self.send_sem.at[2 * r + j],
            self.recv_sem.at[2 * r + self.core],
            (self.at_dp, there),
        )

    def back(self, r, j):
        there = ((self.chip + self.chips - r) % self.chips) * 2 + j
        return remote(
            self.send.at[rows_at(self.me * self.cp, self.cp), :],
            self.recv.at[rows_at(there * self.cp, self.cp), :],
            self.send_sem.at[2 * r + j],
            self.recv_sem.at[2 * r + j],
            (self.at_dp, there),
        )

    def own(self):
        at = rows_at(self.me * self.cp, self.cp)
        return pltpu.make_async_copy(self.send.at[at, :], self.recv.at[at, :], self.local_sem)

    def start(self, r):
        @pl.when(r == 0)
        def _():
            self.out(0, 1 - self.core).start()
            self.own().start()

        @pl.when(r > 0)
        def _():
            self.out(r, 0).start()
            self.out(r, 1).start()

    def finish(self):
        self.own().wait()
        self.out(0, 1 - self.core).wait_send()
        self.back(0, 1 - self.core).wait_recv()

        def step(r, carry):
            for j in range(2):
                self.out(r, j).wait_send()
                self.back(r, j).wait_recv()
            return carry

        lax.fori_loop(1, self.chips, step, 0)


def front_kernel(*refs, pair, imgs, seq, sp, nt, cap, cp, ck, exps):
    refs = list(refs)
    images_ref, cot_in_ref, picks_ref, order_row_ref, order_col_ref, small_ref, dense_ref = refs[:7]
    del refs[:7]
    if pair:
        inner_ref, outer_ref = refs[:2]
        del refs[:2]
    w_ref, small_all, h1_ref, mixed_ref, ctx_ref, after_ref, h2_ref, router_out, gates_ref, place_out = refs[:10]
    x_ref, cot_ref, recv_ref, recv_cot_ref = refs[10:14]
    del refs[:14]
    if pair:
        inner_out, outer_out = refs[:2]
        del refs[:2]
    send_ref, send_cot_ref, pad_ref = refs[:3]
    cot_ssem, cot_rsem, row_ssem, row_rsem, local_sem, weight_ssem, weight_rsem = refs[3:]
    feat = images_ref.shape[-1]
    at_dp, me = lax.axis_index("dp"), lax.axis_index("expert")
    core, chip = me % 2, me // 2
    chips = exps // 2
    shard = dense_ref.shape[0]
    half = shard // 2

    barrier = pltpu.get_barrier_semaphore()

    def greet(r, carry):
        pl.semaphore_signal(
            barrier, inc=1, device_id=(at_dp, (me + r) % exps), device_id_type=MESH
        )
        return carry

    lax.fori_loop(1, exps, greet, 0)
    if pair:
        pl.semaphore_signal(barrier, inc=1, device_id=(1 - at_dp, me), device_id_type=MESH)
    pl.semaphore_wait(barrier, exps - 1 + int(pair))

    if pair:
        other_dp, other_core = (1 - at_dp, me), (at_dp, chip * 2 + 1 - core)
        small_copy = remote(
            small_ref, small_all.at[at_dp], weight_ssem.at[0], weight_rsem.at[0], other_dp
        )
        small_copy.start()
        landed = w_ref.at[rows_at((1 - at_dp) * shard + core * half, half), :]
        dense_copy = remote(
            dense_ref.at[rows_at(core * half, half), :],
            w_ref.at[rows_at(at_dp * shard + core * half, half), :],
            weight_ssem.at[1], weight_rsem.at[1], other_dp,
        )
        dense_copy.start()
        swap_copy = remote(landed, landed, weight_ssem.at[2], weight_rsem.at[2], other_core)
        inner_copy = remote(inner_ref, inner_out, weight_ssem.at[3], weight_rsem.at[3], other_dp)
        outer_copy = remote(
            outer_ref.at[0 : outer_out.shape[0], :], outer_out, weight_ssem.at[4], weight_rsem.at[4], other_dp
        )

    for ref, source in ((x_ref, images_ref), (cot_ref, cot_in_ref)):
        ref[...] = jnp.zeros(ref.shape, BF)
        for i in range(imgs):
            ref[i * sp : i * sp + seq, :] = source[i]
    first, second = picks_ref[0:1, :], picks_ref[1:2, :]
    sub, lane = iota((nt, nt), 0), iota((nt, nt), 1)
    pos_row = jnp.sum(jnp.where(order_col_ref[...] == lane, sub.astype(F32), 0.0), axis=0, keepdims=True)
    pos_col = jnp.sum(jnp.where(order_row_ref[...] == sub, lane.astype(F32), 0.0), axis=1, keepdims=True)
    earlier = hot(pos_col < pos_row)
    exp_id = iota((exps, nt), 0)
    hot0 = jnp.where(exp_id == first, 1.0, 0.0)
    hot1 = jnp.where(exp_id == second, 1.0, 0.0)
    before0 = dot(hot0.astype(BF), earlier)
    before1 = dot(hot1.astype(BF), earlier) + jnp.sum(hot0, axis=1, keepdims=True)
    slot0 = jnp.sum(hot0 * before0, axis=0, keepdims=True).astype(I32)
    slot1 = jnp.sum(hot1 * before1, axis=0, keepdims=True).astype(I32)
    ok0, ok1 = (slot0 < cap) & (first >= 0), (slot1 < cap) & (second >= 0)
    place0, place1 = jnp.where(ok0, first * cp + slot0, -1), jnp.where(ok1, second * cp + slot1, -1)
    place_out[0:1, :] = jnp.where(ok0, first * ck + slot0, -1)
    place_out[1:2, :] = jnp.where(ok1, second * ck + slot1, -1)
    place_out[2:3, :] = place0
    place_out[3:4, :] = place1
    place_out[4:8, :] = jnp.full((4, nt), -1, I32)

    cot_rows = Exchange(send_cot_ref, recv_cot_ref, cot_ssem, cot_rsem, local_sem.at[0], cp, exps)

    def cot_chunk(r, carry):
        base = ((chip + r) % chips) * (2 * cp)
        row = iota((2 * cp, nt), 0) + base
        pick = hot((row == place0) | (row == place1))
        send_cot_ref[rows_at(base, 2 * cp), :] = dot(pick, cot_ref[...]).astype(BF)
        cot_rows.start(r)
        return carry

    lax.fori_loop(0, chips, cot_chunk, 0)

    if pair:
        small_all[at_dp] = small_ref[...]
        w_ref[rows_at(at_dp * shard, shard), :] = dense_ref[...]
        small_copy.wait_recv()
        small = jnp.concatenate([small_all[0], small_all[1]], axis=1)
    else:
        small_all[...] = small_ref[...]
        w_ref[...] = dense_ref[...]
        small = small_all[...]
    norm = small[exps : exps + 4].astype(F32)
    router_w = small[:exps]

    def first_norm(i, carry):
        at = rows_at(i * BLOCK, BLOCK, BLOCK)
        normed, _ = normed_of(x_ref[at, :].astype(F32))
        h1_ref[at, :] = (normed * norm[0:1] + norm[1:2]).astype(BF)
        return carry

    lax.fori_loop(0, nt // BLOCK, first_norm, 0)

    if pair:
        dense_copy.wait_recv()
        swap_copy.start()
        inner_copy.start()
        outer_copy.start()
        swap_copy.wait_recv()

    step = 384

    def project(i, carry):
        at = rows_at(i * step, step, 128)
        mixed_ref[:, at] = dot(h1_ref[...], w_ref[:, at]).astype(BF)
        return carry

    lax.fori_loop(0, 3 * feat // step, project, 0)

    pairs = feat // 128
    key_ok = iota((sp, sp), 1) < seq
    left = iota((sp, 128), 1) < HDIM

    def attend(i, carry):
        rows = rows_at((i // pairs) * sp, sp)
        col = (i % pairs) * 128
        query = mixed_ref[rows, rows_at(col, 128, 128)]
        keys = mixed_ref[rows, rows_at(col + feat, 128, 128)]
        values = mixed_ref[rows, rows_at(col + 2 * feat, 128, 128)]
        outs = []
        for mask in (left, ~left):
            scores = dot_nt(jnp.where(mask, query, jnp.zeros_like(query)), keys) * SCALE
            scores = jnp.where(key_ok, scores, NEG)
            top = jnp.max(scores, axis=-1, keepdims=True)
            grown = jnp.exp(scores - top)
            probs = grown / jnp.sum(grown, axis=-1, keepdims=True)
            outs.append(dot(probs.astype(BF), values))
        ctx_ref[rows, rows_at(col, 128, 128)] = jnp.where(left, outs[0], outs[1]).astype(BF)
        return carry

    ctx_ref[imgs * sp : nt, :] = jnp.zeros((nt - imgs * sp, feat), BF)
    lax.fori_loop(0, imgs * pairs, attend, 0)

    def second_norm(i, carry):
        at = rows_at(i * BLOCK, BLOCK, BLOCK)
        after = x_ref[at, :].astype(F32) + dot(ctx_ref[at, :], w_ref[:, 3 * feat : 4 * feat])
        after_ref[at, :] = after
        normed, _ = normed_of(after)
        h2_ref[at, :] = (normed * norm[2:3] + norm[3:4]).astype(BF)
        return carry

    lax.fori_loop(0, nt // BLOCK, second_norm, 0)

    h2 = h2_ref[...]
    logits = dot_nt(router_w, h2)
    grown = jnp.exp(logits - jnp.max(logits, axis=0, keepdims=True))
    router = grown / jnp.sum(grown, axis=0, keepdims=True)
    router_out[...] = router
    chosen0 = jnp.sum(jnp.where(exp_id == first, router, 0.0), axis=0, keepdims=True)
    chosen1 = jnp.sum(jnp.where(exp_id == second, router, 0.0), axis=0, keepdims=True)
    total = chosen0 + chosen1
    total = jnp.where(total > 0.0, total, 1.0)
    gate0, gate1 = chosen0 / total, chosen1 / total
    for i, row in enumerate((chosen0, chosen1, gate0, gate1)):
        gates_ref[i : i + 1, :] = row
    gates_ref[4:8, :] = jnp.zeros((4, nt), F32)

    zero_rows = jnp.zeros((5, nt), F32)
    parts0 = jnp.concatenate([v.astype(F32) for v in split3(gate0)] + [zero_rows], axis=0).astype(BF)
    parts1 = jnp.concatenate([v.astype(F32) for v in split3(gate1)] + [zero_rows], axis=0).astype(BF)
    pad_ref[...] = jnp.zeros(pad_ref.shape, F32)
    token_rows = Exchange(send_ref, recv_ref, row_ssem, row_rsem, local_sem.at[1], cp, exps)

    def row_chunk(r, carry):
        base = ((chip + r) % chips) * (2 * cp)
        row = iota((2 * cp, nt), 0) + base
        pick0, pick1 = hot(row == place0), hot(row == place1)
        rows = dot(pick0 + pick1, h2_ref[...])
        spread = dot_nt(parts0, pick0) + dot_nt(parts1, pick1)
        line = iota((2 * cp, feat), 0)
        for j in range(2):
            for k in range(3):
                pad_ref[j : j + 1, k * 128 : k * 128 + cp] = spread[k : k + 1, j * cp : (j + 1) * cp]
            rows = rows + jnp.where(line == j * cp + cap, pad_ref[j : j + 1, :], 0.0)
        send_ref[rows_at(base, 2 * cp), :] = rows.astype(BF)
        token_rows.start(r)
        return carry

    lax.fori_loop(0, chips, row_chunk, 0)

    if pair:
        small_copy.wait_send()
        dense_copy.wait_send()
        swap_copy.wait_send()
        inner_copy.wait()
        outer_copy.wait()
    cot_rows.finish()
    token_rows.finish()


def run_front(images, cot, picks, order_row, order_col, small, dense, weights, *, nt, sp, cap, cp, ck, exps):
    imgs, seq, feat = images.shape
    pair = weights is not None
    rows = exps * cp
    vmem, hbm = pl.BlockSpec(memory_space=pltpu.VMEM), pl.BlockSpec(memory_space=pl.ANY)
    dma = pltpu.SemaphoreType.DMA
    outs = [
        shape((feat, 4 * feat), BF),
        shape((2,) + small.shape if pair else small.shape, BF),
        shape((nt, feat), BF),
        shape((nt, 3 * feat), BF),
        shape((nt, feat), BF),
        shape((nt, feat), F32),
        shape((nt, feat), BF),
        shape((exps, nt), F32),
        shape((8, nt), F32),
        shape((8, nt), I32),
        shape((nt, feat), BF),
        shape((nt, feat), BF),
        shape((rows, feat), BF),
        shape((rows, feat), BF),
    ]
    ins = [images, cot, picks, order_row, order_col, small, dense]
    if pair:
        ins += list(weights)
        outs += [shape(weights[0].shape, BF), shape((TILE, feat), BF)]
    return pl.pallas_call(
        functools.partial(
            front_kernel, pair=pair, imgs=imgs, seq=seq, sp=sp, nt=nt, cap=cap, cp=cp, ck=ck, exps=exps
        ),
        out_shape=outs,
        in_specs=[vmem] * 7 + [hbm] * (len(ins) - 7),
        out_specs=[vmem] * 12 + [hbm] * (len(outs) - 12),
        scratch_shapes=[
            pltpu.VMEM((rows, feat), BF),
            pltpu.VMEM((rows, feat), BF),
            pltpu.VMEM((8, feat), F32),
            dma((exps,)), dma((exps,)), dma((exps,)), dma((exps,)), dma((2,)), dma((5,)), dma((5,)),
        ],
        compiler_params=pltpu.CompilerParams(
            vmem_limit_bytes=VMEM_CAP, collective_id=3, has_side_effects=True
        ),
        cost_estimate=pl.CostEstimate(flops=20_000_000_000, bytes_accessed=60_000_000, transcendentals=0),
    )(*ins)


def gelu_both(hidden):
    size = jnp.abs(hidden)
    bell = jnp.exp(hidden * hidden * -0.5)
    t = 1.0 / (1.0 + TAIL_C * size)
    poly = jnp.full_like(t, TAIL[0])
    for c in TAIL[1:]:
        poly = poly * t + c
    tail = bell * poly
    below = jnp.where(hidden >= 0.0, 1.0 - tail, tail)
    return hidden * below, below + hidden * (bell * INV_SQRT_TAU)


def expert_kernel(recv_ref, dfin_ref, *refs, pair, count, cap, cp, apart, exps, block):
    refs = list(refs)
    inner_ref, outer_ref = refs[:2]
    del refs[:2]
    if pair:
        inner_far, outer_far, outer_all = refs[:3]
        del refs[:3]
    act_ref, dhid_ref, rows_ref, dres_ref, result_ref, drows_ref = refs[:6]
    sum_r, sum_d, wi_ref, wo_ref, dfin_c = refs[6:11]
    j = pl.program_id(0)
    rows, feat = rows_ref.shape
    two = 2 * cp
    sub = iota((two, 128), 0)
    lane = iota((two, 128), 1)
    upper = sub < cp
    diag = lane == jnp.where(upper, sub, sub - cp)
    mine = count // 2 if pair else count
    tile = wi_ref.shape[1]

    if pair:
        landed, send_sem, recv_sem = refs[11:]
        other_dp = (1 - lax.axis_index("dp"), lax.axis_index("expert"))
        copies = [
            remote(
                outer_all.at[(t + 1) * tile : (t + 2) * tile, :], landed.at[t], send_sem.at[t], recv_sem.at[t], other_dp
            )
            for t in range(mine - 1)
        ]

        @pl.when(j == 0)
        def _():
            barrier = pltpu.get_barrier_semaphore()
            pl.semaphore_signal(barrier, inc=1, device_id=other_dp, device_id_type=MESH)
            pl.semaphore_wait(barrier, 1)
            for made in copies:
                made.start()

    @pl.when(j == 0)
    def _():
        sum_r[...] = jnp.zeros_like(sum_r)
        sum_d[...] = jnp.zeros_like(sum_d)

        def gate_rows(i, carry):
            at = rows_at(i * two, two)
            full = rows_at(i * 2 * apart, 2 * apart)

            def compact(ref):
                values = ref[full, :].astype(F32)
                if apart == cp:
                    return values
                return jnp.concatenate([values[:cp], values[apart : apart + cp]], axis=0)

            recv, dfin = compact(recv_ref), compact(dfin_ref)
            rows_ref[at, :] = recv.astype(BF)
            dfin_c[at, :] = dfin.astype(BF)
            lead = recv[:, 0:384]
            place = iota((two, 384), 0)
            spread = []
            for k in range(2):
                row = jnp.sum(jnp.where(place == k * cp + cap, lead, 0.0), axis=0, keepdims=True)
                spread.append(row[:, 0:128] + row[:, 128:256] + row[:, 256:384])
            both = jnp.where(upper, spread[0], spread[1])
            gate = jnp.sum(jnp.where(diag, both, 0.0), axis=1, keepdims=True)
            dres_ref[at, :] = (gate * dfin).astype(BF)
            return carry

        lax.fori_loop(0, exps // 2, gate_rows, 0)

    @pl.when(j < mine)
    def _():
        wi_ref[...] = inner_ref[...]
        wo_ref[...] = outer_ref[...]

    if pair:

        @pl.when(j >= mine)
        def _():
            wi_ref[...] = inner_far[...]

        @pl.when(j == mine)
        def _():
            wo_ref[...] = outer_far[...]

        for t in range(mine - 1):

            @pl.when(j == mine + 1 + t)
            def _(t=t):
                copies[t].wait()
                wo_ref[...] = landed[t]

    for i in range(rows // block):
        at = pl.ds(i * block, block)
        hidden = dot(rows_ref[at, :], wi_ref[...])
        act, slope = gelu_both(hidden)
        act = act.astype(BF)
        dact = dot_nt(dres_ref[at, :], wo_ref[...])
        dhid = (slope * dact).astype(BF)
        act_ref[at, :] = act
        dhid_ref[at, :] = dhid
        sum_r[at, :] += dot(act, wo_ref[...])
        sum_d[at, :] += dot_nt(dhid, wi_ref[...])

    @pl.when(j == count - 1)
    def _():
        def finish(i, carry):
            at = rows_at(i * two, two)
            full = rows_at(i * 2 * apart, 2 * apart)
            result = sum_r[at, :].astype(BF).astype(F32)
            if apart == cp:
                result_ref[full, :] = result.astype(BF)
            else:
                gap = jnp.zeros((apart - cp, feat), F32)
                result_ref[full, :] = jnp.concatenate([result[:cp], gap, result[cp:], gap], axis=0).astype(BF)
            dgate = jnp.sum(result * dfin_c[at, :].astype(F32), axis=1, keepdims=True)
            line = iota((two, feat), 0)
            drows = sum_d[at, :]
            for k in range(2):
                chosen = upper if k == 0 else ~upper
                row = jnp.sum(jnp.where(diag & chosen, dgate, 0.0), axis=0, keepdims=True)
                wide = jnp.concatenate(
                    [v.astype(F32) for v in split3(row)] + [jnp.zeros((1, feat - 384), F32)], axis=1
                )
                drows = drows + jnp.where(line == k * cp + cap, wide, 0.0)
            drows_ref[at, :] = drows.astype(BF)
            return carry

        lax.fori_loop(0, exps // 2, finish, 0)


def run_expert(recv, dfin, own, far, cap, cp, exps):
    full, feat = recv.shape
    rows = exps * cp
    inner, outer = own
    tile = min(TILE, inner.shape[1])
    mine = inner.shape[1] // tile
    pair = far is not None
    count = 2 * mine if pair else mine
    whole = pl.BlockSpec((rows, feat), lambda j: (0, 0))
    wide_in = pl.BlockSpec((full, feat), lambda j: (0, 0))
    in_specs = [
        wide_in,
        wide_in,
        pl.BlockSpec((feat, tile), lambda j: (0, jnp.minimum(j, mine - 1))),
        pl.BlockSpec((tile, feat), lambda j: (jnp.minimum(j, mine - 1), 0)),
    ]
    args = [recv, dfin, inner, outer]
    scratch = [
        pltpu.VMEM((rows, feat), F32),
        pltpu.VMEM((rows, feat), F32),
        pltpu.VMEM((feat, tile), BF),
        pltpu.VMEM((tile, feat), BF),
        pltpu.VMEM((rows, feat), BF),
    ]
    if pair:
        in_specs += [
            pl.BlockSpec((feat, tile), lambda j: (0, jnp.maximum(j - mine, 0))),
            pl.BlockSpec((tile, feat), lambda j: (0, 0)),
            pl.BlockSpec(memory_space=pl.ANY),
        ]
        args += [*far, outer]
        scratch += [
            pltpu.VMEM((mine - 1, tile, feat), BF),
            pltpu.SemaphoreType.DMA((mine - 1,)),
            pltpu.SemaphoreType.DMA((mine - 1,)),
        ]
    wide = pl.BlockSpec((rows, tile), lambda j: (0, j))
    block = next(b for b in (352, 384, 256, 128, 16) if rows % b == 0)
    kernel = functools.partial(
        expert_kernel, pair=pair, count=count, cap=cap, cp=cp, apart=full // exps, exps=exps, block=block
    )
    return pl.pallas_call(
        kernel,
        grid=(count,),
        in_specs=in_specs,
        out_specs=[wide, wide, whole, whole, wide_in, whole],
        out_shape=[
            shape((rows, count * tile), BF),
            shape((rows, count * tile), BF),
            shape((rows, feat), BF),
            shape((rows, feat), BF),
            shape((full, feat), BF),
            shape((rows, feat), BF),
        ],
        scratch_shapes=scratch,
        compiler_params=pltpu.CompilerParams(
            vmem_limit_bytes=VMEM_CAP,
            dimension_semantics=("arbitrary",),
            collective_id=4 if pair else None,
            has_side_effects=pair,
        ),
        cost_estimate=pl.CostEstimate(
            flops=8 * rows * feat * count * tile, bytes_accessed=30_000_000, transcendentals=0
        ),
    )(*args)


CHUNKS = 4
DEEP = 4


def back_kernel(*refs, reduce, imgs, seq, sp, cap, cp, apart, exps):
    refs = list(refs)

    def take(count):
        taken = refs[:count]
        del refs[:count]
        return taken

    back_ref, place_col_ref, place_ref, picks_ref, gates_ref, gates_col_ref, router_ref, router_w_ref = take(8)
    h2_ref, after_ref, cot_ref, norm_ref, w_ref, mixed_ref, h1_ref, ctx_ref, x_ref, result_ref = take(10)
    if reduce:
        outer_ref = take(1)[0]
    out_ref, small_out, input_grad_ref, output_ref = take(4)
    if reduce:
        outer_out = take(1)[0]
    dafter_ref, dattn_ref, dctx_ref, dmixed_ref, grads_ref, turned_ref, rows_out_ref = take(7)
    nt, feat = cot_ref.shape
    rows = back_ref.shape[0]
    pairs = feat // 128
    groups = CHUNKS - 1
    per = pairs // groups
    width = per * 128
    key_ok = iota((sp, sp), 1) < seq
    left = iota((sp, 128), 1) < HDIM

    if reduce:
        landed, from_core, pair_sum, from_dp, dp_sum, from_y, y_sum, from_z, mine, small_in = take(10)
        (row_ssem, row_rsem, local_sem, core_send, core_recv, dp_send, dp_recv, y_send, y_recv, z_send, z_recv,
         tall_send, tall_recv, wide_send, wide_recv, last_send, last_recv, small_send, small_recv,
         outer_send, outer_recv) = take(21)
        at_dp, me = lax.axis_index("dp"), lax.axis_index("expert")
        core, chip = me % 2, me // 2
        half, quarter = feat // 2, feat // 4
        tall, wide = quarter // DEEP, feat // 2
        deep, side = chip // 2, chip % 2
        other_core, other_dp = (at_dp, chip * 2 + 1 - core), (1 - at_dp, me)
        other_side = (at_dp, (deep * 2 + 1 - side) * 2 + core)
        line = [(deep + r) % DEEP for r in range(1, DEEP)]
        peers = [(at_dp, (there * 2 + side) * 2 + core) for there in line]
        barrier = pltpu.get_barrier_semaphore()

        def greet(r, carry):
            pl.semaphore_signal(barrier, inc=1, device_id=(at_dp, (me + r) % exps), device_id_type=MESH)
            return carry

        lax.fori_loop(1, exps, greet, 0)
        pl.semaphore_signal(barrier, inc=1, device_id=other_dp, device_id_type=MESH)
        pl.semaphore_wait(barrier, exps)
        result_rows = Exchange(result_ref, landed, row_ssem, row_rsem, local_sem, apart, exps)

        def result_go(r, carry):
            result_rows.start(r)
            return carry

        lax.fori_loop(0, exps // 2, result_go, 0)

        def core_copy(k, part):
            return remote(
                grads_ref.at[k, rows_at(part * half + (1 - core) * quarter, quarter), :],
                from_core.at[k, part], core_send.at[k, part], core_recv.at[k, part], other_core,
            )

        my_rows = rows_at(core * quarter, quarter)
        my_part = rows_at(core * quarter + deep * tall, tall)
        my_side, far_side = rows_at(side * wide, wide, 128), rows_at((1 - side) * wide, wide, 128)

        def dp_copy(k):
            return remote(pair_sum.at[k, 1 - at_dp], from_dp.at[k], dp_send.at[k], dp_recv.at[k], other_dp)

        def y_copy(k):
            return remote(dp_sum.at[k, :, far_side], from_y.at[k], y_send.at[k], y_recv.at[k], other_side)

        def z_copy(k, r):
            return remote(
                y_sum.at[k, rows_at(line[r] * tall, tall), :], from_z.at[k, r], z_send.at[k, r], z_recv.at[k, r], peers[r]
            )

        def tall_copy(k, r):
            return remote(
                mine.at[k], out_ref.at[k, my_part, my_side], tall_send.at[k, r], tall_recv.at[k, r], peers[r]
            )

        def wide_copy(k):
            place = out_ref.at[k, my_rows, my_side]
            return remote(place, place, wide_send.at[k], wide_recv.at[k], other_side)

        def last_copy(k):
            place = out_ref.at[k, my_rows, :]
            return remote(place, place, last_send.at[k], last_recv.at[k], other_core)

        def outer_copy(i):
            size = outer_ref.shape[0] // 2
            at = pl.ds(i * size, size)
            return remote(outer_ref.at[at, :], outer_out.at[at, :], outer_send.at[i], outer_recv.at[i], other_dp)

        outer_copy(0).start()
        steps = [other_core, other_dp] + [(at_dp, (chip ^ bit) * 2 + core) for bit in (1, 2, 4)]

        def small_copy(i):
            return remote(small_out, small_in.at[i], small_send.at[i], small_recv.at[i], steps[i])

    def core_start(k):
        core_copy(k, 0).start()
        core_copy(k, 1).start()

    def core_done(k):
        for part in range(2):
            core_copy(k, part).wait_recv()
            pair_sum[k, part] = (
                grads_ref[k, rows_at(part * half + core * quarter, quarter), :].astype(F32)
                + from_core[k, part].astype(F32)
            ).astype(BF)
        dp_copy(k).start()

    def dp_done(k):
        dp_copy(k).wait_recv()
        dp_sum[k] = (pair_sum[k, at_dp].astype(F32) + from_dp[k].astype(F32)).astype(BF)
        y_copy(k).start()

    def y_done(k):
        y_copy(k).wait_recv()
        y_sum[k] = (dp_sum[k, :, my_side].astype(F32) + from_y[k].astype(F32)).astype(BF)
        for r in range(DEEP - 1):
            z_copy(k, r).start()

    def z_done(k):
        total = y_sum[k, rows_at(deep * tall, tall), :].astype(F32)
        for r in range(DEEP - 1):
            z_copy(k, r).wait_recv()
            total = total + from_z[k, r].astype(F32)
        mine[k] = total.astype(BF)
        out_ref[k, my_part, my_side] = mine[k]
        for r in range(DEEP - 1):
            tall_copy(k, r).start()

    def tall_done(k):
        for r in range(DEEP - 1):
            tall_copy(k, r).wait_recv()
        wide_copy(k).start()

    def wide_done(k):
        wide_copy(k).wait_recv()
        last_copy(k).start()

    stages = (core_start, core_done, dp_done, y_done, z_done, tall_done, wide_done)

    def turn(number):
        if reduce:
            for k in reversed(range(CHUNKS)):
                if 0 <= number - k < len(stages):
                    stages[number - k](k)

    def small_go(i):
        if reduce:
            small_copy(i).start()

    def small_take(i):
        if reduce:
            small_copy(i).wait()
            small_out[...] = small_out[...] + small_in[i]

    spare = hot(iota((exps, rows), 1) == iota((exps, rows), 0) * cp + cap)
    lines = dot(spare, back_ref[:, 0:384])
    exp_id = iota((exps, nt), 0)
    dgate, match = [], []
    for k in range(2):
        pick = picks_ref[k : k + 1, :]
        place = place_ref[k : k + 1, :]
        slot = jnp.where(place >= 0, place - pick * cp, -1)
        slot_hot = hot(iota((128, nt), 0) == slot)
        found = (
            dot(lines[:, 0:128].astype(BF), slot_hot)
            + dot(lines[:, 128:256].astype(BF), slot_hot)
            + dot(lines[:, 256:384].astype(BF), slot_hot)
        )
        match.append(jnp.where(exp_id == pick, 1.0, 0.0))
        dgate.append(jnp.sum(match[k] * found, axis=0, keepdims=True))
    chosen = (gates_ref[0:1, :], gates_ref[1:2, :])
    total = chosen[0] + chosen[1]
    total = jnp.where(total > 0.0, total, 1.0)
    cross = (dgate[0] * chosen[0] + dgate[1] * chosen[1]) / (total * total)
    drouter = match[0] * (dgate[0] / total - cross) + match[1] * (dgate[1] / total - cross)
    router = router_ref[...]
    dlogits = (router * (drouter - jnp.sum(router * drouter, axis=0, keepdims=True))).astype(BF)
    norm = norm_ref[...].astype(F32)
    small_out[0:exps, :] = dot(dlogits, h2_ref[...])
    small_out[exps:, :] = jnp.zeros((small_out.shape[0] - exps, feat), F32)

    for start in range(0, nt, BIG):
        at = slice(start, start + BIG)
        slots = iota((BIG, rows), 1)
        pick = hot((slots == place_col_ref[at, 0:1]) | (slots == place_col_ref[at, 1:2]))
        dh2 = dot(pick, back_ref[...]) + dot_tn(dlogits[:, at], router_w_ref[...])
        normed, rstd = normed_of(after_ref[at, :])
        small_out[exps + 2 : exps + 3, :] += jnp.sum(dh2 * normed, axis=0, keepdims=True)
        small_out[exps + 3 : exps + 4, :] += jnp.sum(dh2, axis=0, keepdims=True)
        dafter = cot_ref[at, :].astype(F32) + norm_back_rows(dh2, normed, rstd, norm[2:3])
        dafter_ref[at, :] = dafter
        dattn = dafter.astype(BF)
        dattn_ref[at, :] = dattn
        dctx_ref[at, :] = dot_nt(dattn, w_ref[:, 3 * feat : 4 * feat]).astype(BF)

    def attend(group):
        def image(i, carry):
            lines = rows_at(i * sp, sp)
            for p in range(per):
                col = (group * per + p) * 128
                at_q, at_k, at_v = (slice(col + n * feat, col + n * feat + 128) for n in range(3))
                query, keys, values = mixed_ref[lines, at_q], mixed_ref[lines, at_k], mixed_ref[lines, at_v]
                dctx = dctx_ref[lines, at_q]
                zero = jnp.zeros_like(query)
                dq = dk = dv = 0.0
                for mask in (left, ~left):
                    query_h = jnp.where(mask, query, zero)
                    keys_h = jnp.where(mask, keys, zero)
                    dctx_h = jnp.where(mask, dctx, zero)
                    scores = jnp.where(key_ok, dot_nt(query_h, keys) * SCALE, NEG)
                    top = jnp.max(scores, axis=-1, keepdims=True)
                    grown = jnp.exp(scores - top)
                    probs = grown / jnp.sum(grown, axis=-1, keepdims=True)
                    dv = dv + dot_tn(probs.astype(BF), dctx_h)
                    dweights = dot_nt(dctx_h, values)
                    dscores = (
                        probs * (dweights - jnp.sum(probs * dweights, axis=-1, keepdims=True))
                    ).astype(BF)
                    dq = dq + dot(dscores, keys_h)
                    dk = dk + dot_tn(dscores, query_h)
                dmixed_ref[lines, at_q] = (dq * SCALE).astype(BF)
                dmixed_ref[lines, at_k] = (dk * SCALE).astype(BF)
                dmixed_ref[lines, at_v] = dv.astype(BF)
            return carry

        lax.fori_loop(0, imgs, image, 0)
        for n in range(3):
            grads_ref[1 + group, :, n * width : (n + 1) * width] = dot(
                turned_ref[...], dmixed_ref[:, n * feat + group * width : n * feat + (group + 1) * width]
            ).astype(BF)

    def first_norm(start):
        at = slice(start, start + BIG)
        dh1 = dot_nt(dmixed_ref[at, :], w_ref[:, : 3 * feat])
        normed, rstd = normed_of(x_ref[at, :].astype(F32))
        small_out[exps : exps + 1, :] += jnp.sum(dh1 * normed, axis=0, keepdims=True)
        small_out[exps + 1 : exps + 2, :] += jnp.sum(dh1, axis=0, keepdims=True)
        rows_out_ref[at, :] = (dafter_ref[at, :] + norm_back_rows(dh1, normed, rstd, norm[0:1])).astype(BF)

    def deliver(ref):
        for i in range(imgs):
            ref[i] = rows_out_ref[i * sp : i * sp + seq, :]

    def final_rows(start, source):
        at = slice(start, start + BIG)
        slots = iota((BIG, source.shape[0]), 1)
        final = after_ref[at, :]
        for k in range(2):
            pick = hot(slots == place_col_ref[at, 2 + k : 3 + k])
            final = final + gates_col_ref[at, k : k + 1] * dot(pick, source[...])
        rows_out_ref[at, :] = final.astype(BF)

    dmixed_ref[imgs * sp : nt, :] = jnp.zeros((nt - imgs * sp, 3 * feat), BF)
    turned_ref[...] = ctx_ref[...].T
    for n in range(3):
        at = slice(n * width, (n + 1) * width)
        grads_ref[0, :, at] = dot(turned_ref[...], dattn_ref[:, at]).astype(BF)
    turn(0)
    turned_ref[...] = h1_ref[...].T
    for group in range(groups):
        attend(group)
        turn(1 + group)
    first_norm(0)
    turn(4)
    for start in range(BIG, nt, BIG):
        first_norm(start)
    deliver(input_grad_ref)
    if not reduce:
        out_ref[...] = grads_ref[...]
        for start in range(0, nt, BIG):
            final_rows(start, result_ref)
        deliver(output_ref)
        return
    small_go(0)
    turn(5)
    small_take(0)
    small_go(1)
    outer_copy(1).start()
    result_rows.finish()
    final_rows(0, landed)
    turn(6)
    small_take(1)
    small_go(2)
    for start in range(BIG, nt, BIG):
        final_rows(start, landed)
    deliver(output_ref)
    turn(7)
    small_take(2)
    small_go(3)
    turn(8)
    small_take(3)
    small_go(4)
    turn(9)
    small_take(4)
    outer_copy(0).wait()
    outer_copy(1).wait()
    for k in range(CHUNKS):
        last_copy(k).wait()
        core_copy(k, 0).wait_send()
        core_copy(k, 1).wait_send()
        dp_copy(k).wait_send()
        y_copy(k).wait_send()
        wide_copy(k).wait_send()
        for r in range(DEEP - 1):
            z_copy(k, r).wait_send()
            tall_copy(k, r).wait_send()


def run_back(reduce, imgs, seq, sp, cap, cp, apart, exps, *args):
    nt, feat = args[9].shape
    vmem = pl.BlockSpec(memory_space=pltpu.VMEM)
    small = up(exps + 4, 8)
    quarter = feat // 4
    scratch = [
        pltpu.VMEM((nt, feat), F32),
        pltpu.VMEM((nt, feat), BF),
        pltpu.VMEM((nt, feat), BF),
        pltpu.VMEM((nt, 3 * feat), BF),
        pltpu.VMEM((CHUNKS, feat, feat), BF),
        pltpu.VMEM((feat, nt), BF),
        pltpu.VMEM((nt, feat), BF),
    ]
    if reduce:
        dma = pltpu.SemaphoreType.DMA
        tall, wide = quarter // DEEP, feat // 2
        line = (CHUNKS, DEEP - 1)
        one, many = dma((CHUNKS,)), dma(line)
        scratch += [
            pltpu.VMEM((exps * apart, feat), BF),
            pltpu.VMEM((CHUNKS, 2, quarter, feat), BF),
            pltpu.VMEM((CHUNKS, 2, quarter, feat), BF),
            pltpu.VMEM((CHUNKS, quarter, feat), BF),
            pltpu.VMEM((CHUNKS, quarter, feat), BF),
            pltpu.VMEM((CHUNKS, quarter, wide), BF),
            pltpu.VMEM((CHUNKS, quarter, wide), BF),
            pltpu.VMEM(line + (tall, wide), BF),
            pltpu.VMEM((CHUNKS, tall, wide), BF),
            pltpu.VMEM((5, small, feat), F32),
            dma((exps,)), dma((exps,)), dma, dma((CHUNKS, 2)), dma((CHUNKS, 2)),
            one, one, one, one, many, many, many, many, one, one, one, one, dma((5,)), dma((5,)),
            dma((2,)), dma((2,)),
        ]
    hbm = pl.BlockSpec(memory_space=pl.ANY)
    extra = [shape(args[-1].shape, BF)] if reduce else []
    return pl.pallas_call(
        functools.partial(
            back_kernel, reduce=reduce, imgs=imgs, seq=seq, sp=sp, cap=cap, cp=cp, apart=apart, exps=exps
        ),
        out_shape=(
            shape((CHUNKS, feat // 2 if reduce else feat, feat), BF),
            shape((small, feat), F32),
            shape((imgs, seq, feat), BF),
            shape((imgs, seq, feat), BF),
            *extra,
        ),
        in_specs=[vmem] * (len(args) - 2) + [hbm] * 2 if reduce else [vmem] * len(args),
        out_specs=(vmem,) * 4 + (hbm,) * len(extra),
        scratch_shapes=scratch,
        compiler_params=pltpu.CompilerParams(
            vmem_limit_bytes=VMEM_CAP, collective_id=1 if reduce else None, has_side_effects=reduce
        ),
        cost_estimate=pl.CostEstimate(flops=60_000_000_000, bytes_accessed=60_000_000, transcendentals=0),
    )(*args)


def adam_rows(weight, first, second, grad, rate, decay):
    new_first = BETA_ONE * first + (1.0 - BETA_ONE) * grad
    new_second = BETA_TWO * second + (1.0 - BETA_TWO) * grad * grad
    first_hat = new_first * (1.0 / (1.0 - BETA_ONE**STEP))
    second_hat = new_second * (1.0 / (1.0 - BETA_TWO**STEP))
    new_weight = weight - rate * (first_hat / (jnp.sqrt(second_hat) + ADAM_EPS) + decay * weight)
    return new_weight, new_first, new_second


def total_kernel(dense_ref, small_ref, *refs, shards, exps):
    far = refs[:4]
    norm_ref, part_ref, landed, send_sem, recv_sem = refs[4:]
    feat = dense_ref.shape[-1]
    at_dp, me = lax.axis_index("dp"), lax.axis_index("expert")
    count = shards * exps
    flat = at_dp * exps + me
    devices = [(((flat + r) % count) // exps, ((flat + r) % count) % exps) for r in range(1, count)]
    barrier = pltpu.get_barrier_semaphore()
    for device in devices:
        pl.semaphore_signal(barrier, inc=1, device_id=device, device_id_type=MESH)

    unit = 32

    def squares_of(read, size, width):
        def step(i, total):
            values = read(rows_at(i * unit, unit))
            return total + jnp.sum(values * values, axis=0, keepdims=True)

        return jnp.sum(lax.fori_loop(0, size // unit, step, jnp.zeros((1, width), F32)))

    half = feat // shards
    small = small_ref[:, rows_at(at_dp * half, half, 128)]
    dense_part = jnp.sum(small * small)
    for k in range(CHUNKS):
        dense_part += squares_of(lambda at, k=k: dense_ref[k, at, :].astype(F32), dense_ref.shape[1], feat)
    local = jnp.where(me == 0, dense_part, 0.0)
    for mine, theirs in (far[0:2], far[2:4]):
        local += squares_of(
            lambda at, mine=mine, theirs=theirs: mine[at, :].astype(F32) + theirs[at, :].astype(F32), *mine.shape
        )
    part_ref[...] = jnp.full(part_ref.shape, local, F32)
    pl.semaphore_wait(barrier, count - 1)
    copies = [
        remote(part_ref, landed.at[r], send_sem.at[r], recv_sem.at[r], device) for r, device in enumerate(devices)
    ]
    for made in copies:
        made.start()
    total = part_ref[...]
    for r, made in enumerate(copies):
        made.wait_recv()
        total = total + landed[r]
    norm_ref[...] = jnp.sqrt(total)
    for made in copies:
        made.wait_send()


def run_total(shards, exps, *args):
    count = shards * exps
    vmem = pl.BlockSpec(memory_space=pltpu.VMEM)
    dma = pltpu.SemaphoreType.DMA
    return pl.pallas_call(
        functools.partial(total_kernel, shards=shards, exps=exps),
        out_shape=shape((8, 128), F32),
        in_specs=[vmem] * len(args),
        out_specs=vmem,
        scratch_shapes=[
            pltpu.VMEM((8, 128), F32),
            pltpu.VMEM((count - 1, 8, 128), F32),
            dma((count - 1,)), dma((count - 1,)),
        ],
        compiler_params=pltpu.CompilerParams(
            vmem_limit_bytes=VMEM_CAP, collective_id=2, has_side_effects=True
        ),
        cost_estimate=pl.CostEstimate(flops=100_000_000, bytes_accessed=20_000_000, transcendentals=0),
    )(*args)


def adam_kernel(*refs, exps, jobs):
    refs = list(refs)

    def take(count):
        taken = refs[:count]
        del refs[:count]
        return taken

    norm_ref, small_ref, dense_in = take(3)
    router_in, norm_in = take(3), take(3)
    far_in = take(4)
    state_in = [take(3) for _ in range(4)]
    router_out, vector_out = take(3), take(3)
    state_out = [take(3) for _ in range(4)]
    dense_ref = take(1)[0]
    far = take(4)
    state = [take(3) for _ in range(4)]
    far_sem, load_sem, store_sem = refs
    feat = dense_ref.shape[-1]
    unit = 32

    def piece(ref, i, p):
        size = ref.shape[0] // jobs[i]
        return ref.at[pl.ds(p * size, size), :]

    def load(i, n, p):
        return pltpu.make_async_copy(piece(state_in[i][n], i, p), piece(state[i][n], i, p), load_sem.at[i, n, p])

    def load_far(i, n, p):
        return pltpu.make_async_copy(
            piece(far_in[2 * i + n], i, p), piece(far[2 * i + n], i, p), far_sem.at[i, n, p]
        )

    def store(i, n, p):
        return pltpu.make_async_copy(piece(state[i][n], i, p), piece(state_out[i][n], i, p), store_sem.at[i, n, p])

    load_dense = pltpu.make_async_copy(dense_in, dense_ref, far_sem.at[2, 0, 0])
    for i in range(4):
        if i == 2:
            load_dense.start()
        for p in range(jobs[i]):
            for n in range(3):
                load(i, n, p).start()
            if i < 2:
                load_far(i, 0, p).start()
                load_far(i, 1, p).start()

    clip = CLIP_NORM / jnp.maximum(norm_ref[0:1, 0:1], CLIP_NORM)
    small = small_ref[...]
    router_grad = small[0:exps] * clip
    for ref, new in zip(router_out, adam_rows(*(r[...] for r in router_in), router_grad, RATE_MATRIX, DECAY)):
        ref[...] = new
    vector_grad = small[exps : exps + 4] * clip
    for ref, new in zip(vector_out, adam_rows(*(r[...] for r in norm_in), vector_grad, RATE_VECTOR, 0.0)):
        ref[...] = new

    def expert_grad(i):
        def grad(at):
            return far[2 * i][at, :].astype(F32) + far[2 * i + 1][at, :].astype(F32)

        return grad

    def qkv_grad(at):
        width = feat // (CHUNKS - 1)
        return jnp.concatenate(
            [dense_ref[g, at, n * width : (n + 1) * width] for n in range(3) for g in range(1, CHUNKS)], axis=1
        ).astype(F32)

    def proj_grad(at):
        return dense_ref[0, at, :].astype(F32)

    for i, grad_of in enumerate((expert_grad(0), expert_grad(1), qkv_grad, proj_grad)):
        size = state[i][0].shape[0] // jobs[i]
        if i == 2:
            load_dense.wait()
        for p in range(jobs[i]):
            for n in range(3):
                load(i, n, p).wait()
            if i < 2:
                load_far(i, 0, p).wait()
                load_far(i, 1, p).wait()

            def rows(u, carry, i=i, p=p, size=size, grad_of=grad_of):
                at = rows_at(p * size + u * unit, unit)
                new = adam_rows(*(state[i][n][at, :] for n in range(3)), grad_of(at) * clip, RATE_MATRIX, DECAY)
                for n in range(3):
                    state[i][n][at, :] = new[n]
                return carry

            lax.fori_loop(0, size // unit, rows, 0)
            for n in range(3):
                store(i, n, p).start()
    for i in range(4):
        for p in range(jobs[i]):
            for n in range(3):
                store(i, n, p).wait()


def run_adam(exps, norm, small, dense, router, vector, far, states):
    jobs = (4, 4, 3, 1)
    vmem, hbm = pl.BlockSpec(memory_space=pltpu.VMEM), pl.BlockSpec(memory_space=pl.ANY)
    dma = pltpu.SemaphoreType.DMA
    flat_states = [a for group in states for a in group]
    args = [norm, small, dense, *router, *vector, *far, *flat_states]
    return pl.pallas_call(
        functools.partial(adam_kernel, exps=exps, jobs=jobs),
        out_shape=[shape(a.shape, F32) for a in (*router, *vector, *flat_states)],
        in_specs=[vmem] * 2 + [hbm] + [vmem] * 6 + [hbm] * 16,
        out_specs=[vmem] * 6 + [hbm] * 12,
        scratch_shapes=[pltpu.VMEM(dense.shape, BF)]
        + [pltpu.VMEM(a.shape, BF) for a in far]
        + [pltpu.VMEM(a.shape, F32) for a in flat_states]
        + [dma((3, 2, 4)), dma((4, 3, 4)), dma((4, 3, 4))],
        compiler_params=pltpu.CompilerParams(vmem_limit_bytes=VMEM_CAP),
        cost_estimate=pl.CostEstimate(flops=100_000_000, bytes_accessed=100_000_000, transcendentals=0),
    )(*args)


def adam_step(weight, first, second, grad, rate, decay):
    new_first = BETA_ONE * first + (1.0 - BETA_ONE) * grad
    new_second = BETA_TWO * second + (1.0 - BETA_TWO) * grad * grad
    first_hat = new_first / (1.0 - BETA_ONE**STEP)
    second_hat = new_second / (1.0 - BETA_TWO**STEP)
    new_weight = weight - rate * (first_hat / (jnp.sqrt(second_hat) + ADAM_EPS) + decay * weight)
    return (new_weight, new_first, new_second)


def body(
    images,
    cotangent,
    routes,
    priority,
    qkv_weight,
    qkv_first,
    qkv_second,
    proj_weight,
    proj_first,
    proj_second,
    router_weight,
    router_first,
    router_second,
    norm_params,
    norm_first,
    norm_second,
    inner_weight,
    inner_first,
    inner_second,
    outer_weight,
    outer_first,
    outer_second,
):
    exps = lax.axis_size("expert")
    shards = lax.axis_size("dp")
    imgs, seq, feat = images.shape
    tok = imgs * seq
    cap = (18 * tok + 8 * exps - 1) // (8 * exps)
    cp = up(cap + 1, 8)
    sp = up(seq, 16)
    nt = up(imgs * sp, BLOCK)
    rows = exps * cp
    at_dp, at_exp = lax.axis_index("dp"), lax.axis_index("expert")
    ring = [(0, 1), (1, 0)]
    shard_rows = qkv_weight.shape[0]
    by_kernel = shards == 2 and exps == 4 * DEEP

    def spread(values, fill=0):
        values = jnp.pad(values, ((0, 0), (0, sp - seq), (0, 0)), constant_values=fill)
        values = values.reshape(imgs * sp, values.shape[-1])
        return jnp.pad(values, ((0, nt - imgs * sp), (0, 0)), constant_values=fill)

    def unspread(values):
        return values[: imgs * sp].reshape(imgs, sp, -1)[:, :seq]

    def exchange(values):
        return lax.all_to_all(
            values.reshape(exps, cp, feat), "expert", split_axis=0, concat_axis=0, tiled=True
        ).reshape(rows, feat)

    dense = jnp.concatenate([qkv_weight.astype(BF), proj_weight.astype(BF)], axis=1)
    small = jnp.concatenate([router_weight.astype(BF).T, norm_params.astype(BF)], axis=0)
    small = jnp.pad(small, ((0, up(exps + 4, 16) - exps - 4), (0, 0)))
    inner_b, outer_b = inner_weight[0].astype(BF), outer_weight[0].astype(BF)
    if shards > 2:
        dense = lax.all_gather(dense, "dp", axis=0, tiled=True)
        small = lax.all_gather(small, "dp", axis=1, tiled=True)
    picks = jnp.concatenate([spread(routes, -1).T, jnp.full((6, nt), -1, I32)], axis=0)
    order = priority[0] + (priority[0] // seq) * (sp - seq)
    order = jnp.pad(order, (0, nt - tok), constant_values=-1)
    w_full, small, h1, mixed, context, after, h2, router, gates, place, x, cot, recv, recv_cot, *others = run_front(
        images, cotangent, picks, order[None, :], order[:, None], small, dense,
        (inner_b, outer_b) if shards == 2 else None,
        nt=nt, sp=sp, cap=cap, cp=up(cap + 1, 16), ck=cp, exps=exps,
    )
    if shards == 2:
        small = jnp.concatenate([small[0], small[1]], axis=1)
        own, far = (inner_b, outer_b), tuple(others)
    else:
        own, far = (
            lax.all_gather(inner_b, "dp", axis=1, tiled=True),
            lax.all_gather(outer_b, "dp", axis=0, tiled=True),
        ), None
    router_t, norm_b = small[:exps], small[exps : exps + 4]
    place_col = place[0:4].T
    gates_col = gates[2:4].T

    act, dhid, recv, dres, result, drows = run_expert(recv, recv_cot, own, far, cap, cp, exps)

    def tn(left, right):
        return lax.dot_general(left, right, (((0,), (0,)), ((), ())), preferred_element_type=F32)

    if shards == 2:
        mid = inner_b.shape[1]
        far_inner = tn(recv, dhid[:, mid:]).astype(BF)
        far_inner, drows, act = lax.optimization_barrier((far_inner, drows, act))
        sent_inner = lax.ppermute(far_inner, "dp", ring)
        back_grad = exchange(drows)
        far_outer = tn(act[:, mid:], dres).astype(BF)
        far_outer, recv, act = lax.optimization_barrier((far_outer, recv, act))
        if not by_kernel:
            sent_outer = lax.ppermute(far_outer, "dp", ring)
        own_inner, own_outer = tn(recv, dhid[:, :mid]).astype(BF), tn(act[:, :mid], dres).astype(BF)
        back_grad, own_inner, own_outer = lax.optimization_barrier((back_grad, own_inner, own_outer))
    else:
        back_grad = exchange(drows)
        shard_inner = lax.psum_scatter(
            tn(recv, dhid).astype(BF), "dp", scatter_dimension=1, tiled=True
        ).astype(F32)[None]
        shard_outer = lax.psum_scatter(
            tn(act, dres).astype(BF), "dp", scatter_dimension=0, tiled=True
        ).astype(F32)[None]

    if not by_kernel:
        result = lax.all_to_all(
            result.reshape(exps, -1, feat), "expert", split_axis=0, concat_axis=0, tiled=True
        ).reshape(-1, feat)
    dense_grad, small_grad, input_grad, output, *sent = run_back(
        by_kernel, imgs, seq, sp, cap, cp, up(cap + 1, 16), exps,
        back_grad, place_col, place, picks, gates, gates_col, router, router_t, h2, after, cot, norm_b, w_full,
        mixed, h1, context, x, result, *((far_outer,) if by_kernel else ()),
    )

    if by_kernel:
        far = (own_inner, sent_inner, own_outer, *sent)
        norm = run_total(shards, exps, dense_grad, small_grad, *far)
        small_half = lax.dynamic_slice_in_dim(small_grad, at_dp * shard_rows, shard_rows, 1)
        new = run_adam(
            exps, norm, small_half, dense_grad,
            (router_weight.T, router_first.T, router_second.T),
            (norm_params, norm_first, norm_second),
            far,
            (
                (inner_weight[0], inner_first[0], inner_second[0]),
                (outer_weight[0], outer_first[0], outer_second[0]),
                (qkv_weight, qkv_first, qkv_second),
                (proj_weight, proj_first, proj_second),
            ),
        )
        router_new, norm_new, inner_new, outer_new, qkv_new, proj_new = (new[3 * i : 3 * i + 3] for i in range(6))
        return (
            output,
            input_grad,
            norm[0, 0],
            *qkv_new,
            *proj_new,
            *(a.T for a in router_new),
            *norm_new,
            *(a[None] for a in inner_new),
            *(a[None] for a in outer_new),
        )

    dense_grad = lax.psum(dense_grad, ("dp", "expert"))
    small_grad = lax.psum(small_grad, ("dp", "expert"))
    width = feat // (CHUNKS - 1)
    dense_grad = lax.dynamic_slice_in_dim(dense_grad, at_dp * shard_rows, shard_rows, 1).astype(F32)
    shard_small = lax.dynamic_slice_in_dim(small_grad, at_dp * shard_rows, shard_rows, 1)
    shard_qkv = jnp.concatenate(
        [dense_grad[g, :, n * width : (n + 1) * width] for n in range(3) for g in range(1, CHUNKS)], axis=1
    )
    shard_proj = dense_grad[0]
    shard_router, shard_vector = shard_small[:exps].T, shard_small[exps : exps + 4]
    if shards == 2:
        shard_inner = (own_inner.astype(F32) + sent_inner.astype(F32))[None]
        shard_outer = (own_outer.astype(F32) + sent_outer.astype(F32))[None]
    dense_squares = jnp.sum(dense_grad * dense_grad) + jnp.sum(shard_small * shard_small)
    expert_squares = jnp.sum(shard_inner * shard_inner) + jnp.sum(shard_outer * shard_outer)
    local_squares = expert_squares + jnp.where(at_exp == 0, dense_squares, jnp.float32(0.0))
    grad_norm = jnp.sqrt(lax.psum(local_squares, ("dp", "expert")))
    clip = CLIP_NORM / jnp.maximum(grad_norm, CLIP_NORM)
    qkv_new = adam_step(qkv_weight, qkv_first, qkv_second, shard_qkv * clip, RATE_MATRIX, DECAY)
    proj_new = adam_step(proj_weight, proj_first, proj_second, shard_proj * clip, RATE_MATRIX, DECAY)
    router_new = adam_step(
        router_weight, router_first, router_second, shard_router * clip, RATE_MATRIX, DECAY
    )
    norm_new = adam_step(norm_params, norm_first, norm_second, shard_vector * clip, RATE_VECTOR, 0.0)
    inner_new = adam_step(
        inner_weight, inner_first, inner_second, shard_inner * clip, RATE_MATRIX, DECAY
    )
    outer_new = adam_step(
        outer_weight, outer_first, outer_second, shard_outer * clip, RATE_MATRIX, DECAY
    )
    return (
        output,
        input_grad,
        grad_norm,
        *qkv_new,
        *proj_new,
        *router_new,
        *norm_new,
        *inner_new,
        *outer_new,
    )


def solution(mesh):
    tokens = P(("dp", "expert"), None, None)
    dense = P("dp", None)
    vector = P(None, "dp")
    inner = P("expert", None, "dp")
    outer = P("expert", "dp", None)
    return jax.shard_map(
        body,
        mesh=mesh,
        in_specs=(tokens, tokens, tokens, P(("dp", "expert"), None))
        + (dense,) * 9
        + (vector,) * 3
        + (inner,) * 3
        + (outer,) * 3,
        out_specs=(tokens, tokens, P())
        + (dense,) * 9
        + (vector,) * 3
        + (inner,) * 3
        + (outer,) * 3,
        check_vma=False,
    )
```

```python
import functools

import jax
import jax.numpy as jnp
from jax import lax
from jax.experimental import pallas as pl
from jax.experimental.pallas import tpu as pltpu
from jax.sharding import PartitionSpec as P

HEADS = 12
HDIM = 64
STEP = 10
SCALE = float(HDIM) ** (-0.5)

LN_EPS = 1e-06
BETA_ONE = 0.9
BETA_TWO = 0.999
ADAM_EPS = 1e-08
RATE_MATRIX = 0.06
RATE_VECTOR = 0.4
DECAY = 0.1
CLIP_NORM = 1.0

BF = jnp.bfloat16
F32 = jnp.float32
I32 = jnp.int32
NEG = -1e30
BLOCK = 128
BIG = 320
TILE = 512
EARLY = 2
CHUNKS = 4
DEEP = 4
VMEM_CAP = 60 * 1024 * 1024

LOG2_E = 1.4426950408889634
SQRT_HALF = 0.7071067811865476
INV_SQRT_TAU = 0.3989422804014327


def up(value, step):
    return -(-value // step) * step


def dot(left, right):
    return lax.dot_general(left, right, (((1,), (0,)), ((), ())), preferred_element_type=F32)


def dot_nt(left, right):
    return lax.dot_general(left, right, (((1,), (1,)), ((), ())), preferred_element_type=F32)


def dot_tn(left, right):
    return lax.dot_general(left, right, (((0,), (0,)), ((), ())), preferred_element_type=F32)


def iota(shape, axis):
    return lax.broadcasted_iota(I32, shape, axis)


def hot(mask):
    return jnp.where(mask, 1.0, 0.0).astype(BF)


def normed_of(values):
    centre = jnp.mean(values, axis=-1, keepdims=True)
    centered = values - centre
    rstd = lax.rsqrt(jnp.mean(centered * centered, axis=-1, keepdims=True) + LN_EPS)
    return centered * rstd, rstd


def norm_back_rows(grad, normed, rstd, gain):
    scaled = grad * gain
    inner_mean = jnp.mean(scaled, axis=-1, keepdims=True)
    cross_mean = jnp.mean(scaled * normed, axis=-1, keepdims=True)
    return rstd * (scaled - inner_mean - normed * cross_mean)


def split3(values):
    high = values.astype(BF)
    rest = values - high.astype(F32)
    mid = rest.astype(BF)
    low = (rest - mid.astype(F32)).astype(BF)
    return high, mid, low


def call(kernel, out_shape, *args, scratch=(), specs=None, flops=0, moved=0):
    vmem = pl.BlockSpec(memory_space=pltpu.VMEM)
    single = not isinstance(out_shape, (tuple, list))
    return pl.pallas_call(
        kernel,
        out_shape=out_shape,
        in_specs=[vmem] * len(args) if specs is None else specs,
        out_specs=vmem if single else [vmem] * len(out_shape),
        scratch_shapes=list(scratch),
        compiler_params=pltpu.CompilerParams(vmem_limit_bytes=VMEM_CAP),
        cost_estimate=pl.CostEstimate(flops=int(flops), bytes_accessed=int(moved), transcendentals=0),
    )(*args)


def shape(dims, kind):
    return jax.ShapeDtypeStruct(dims, kind)


MESH = pl.DeviceIdType.MESH


def remote(source, target, send, recv, device):
    return pltpu.make_async_remote_copy(
        src_ref=source, dst_ref=target, send_sem=send, recv_sem=recv, device_id=device, device_id_type=MESH
    )


def rows_at(start, size, unit=16):
    return pl.ds(pl.multiple_of(start, unit), size)


class Exchange:
    def __init__(self, send, recv, send_sem, recv_sem, local_sem, exps):
        self.send, self.recv, self.send_sem, self.recv_sem, self.local_sem = send, recv, send_sem, recv_sem, local_sem
        self.chips = exps // 2
        self.at_dp, self.me = lax.axis_index("dp"), lax.axis_index("expert")
        self.core, self.chip = self.me % 2, self.me // 2

    def out(self, r, j):
        there = ((self.chip + r) % self.chips) * 2 + j
        return remote(
            self.send.at[there], self.recv.at[self.me],
            self.send_sem.at[2 * r + j], self.recv_sem.at[2 * r + self.core], (self.at_dp, there),
        )

    def back(self, r, j):
        there = ((self.chip + self.chips - r) % self.chips) * 2 + j
        return remote(
            self.send.at[self.me], self.recv.at[there],
            self.send_sem.at[2 * r + j], self.recv_sem.at[2 * r + j], (self.at_dp, there),
        )

    def own(self):
        return pltpu.make_async_copy(self.send.at[self.me], self.recv.at[self.me], self.local_sem)

    def start(self, r):
        @pl.when(r == 0)
        def _():
            self.out(0, 1 - self.core).start()
            self.own().start()

        @pl.when(r > 0)
        def _():
            self.out(r, 0).start()
            self.out(r, 1).start()

    def finish(self):
        self.own().wait()
        self.out(0, 1 - self.core).wait_send()
        self.back(0, 1 - self.core).wait_recv()

        def step(r, carry):
            for j in range(2):
                self.out(r, j).wait_send()
                self.back(r, j).wait_recv()
            return carry

        lax.fori_loop(1, self.chips, step, 0)


def front_kernel(*refs, pair, imgs, seq, sp, nt, cap, cp, exps):
    refs = list(refs)

    def take(count):
        taken = refs[:count]
        del refs[:count]
        return taken

    images_ref, cot_in_ref, picks_ref, order_row_ref, order_col_ref, small_ref, qkv_ref, proj_ref = take(8)
    if pair:
        experts_in = take(2)
    w_ref, small_all, h1_ref, mixed_ref, ctx_ref, after_ref, h2_ref, router_out, gates_ref, place_out = take(10)
    x_ref, cot_ref, recv_ref, recv_cot_ref = take(4)
    if pair:
        experts_own, experts_far = take(2), take(2)
    send_ref, send_cot_ref, pad_ref = take(3)
    if pair:
        staged, experts = take(2), take(2)
    cot_ssem, cot_rsem, row_ssem, row_rsem, local_sem = take(5)
    if pair:
        weight_ssem, weight_rsem, side_ssem, side_rsem, stage_sem, own_sem = take(6)
    feat = images_ref.shape[-1]
    at_dp, me = lax.axis_index("dp"), lax.axis_index("expert")
    core, chip = me % 2, me // 2
    chips = exps // 2
    shard = qkv_ref.shape[0]
    half = shard // 2
    groups = CHUNKS - 1
    pairs = feat // 128
    per = pairs // groups

    if pair:
        loads = [pltpu.make_async_copy(experts_in[i], staged[i], stage_sem.at[i]) for i in range(2)]
        for made in loads:
            made.start()
    barrier = pltpu.get_barrier_semaphore()

    def greet(r, carry):
        pl.semaphore_signal(
            barrier, inc=1, device_id=(at_dp, (me + r) % exps), device_id_type=MESH
        )
        return carry

    lax.fori_loop(1, exps, greet, 0)
    if pair:
        pl.semaphore_signal(barrier, inc=1, device_id=(1 - at_dp, me), device_id_type=MESH)
    width = per * 128
    own_rows = rows_at(at_dp * shard if pair else 0, shard)
    for g in range(groups):
        for n in range(3):
            w_ref[own_rows, g * feat + n * width : g * feat + (n + 1) * width] = qkv_ref[
                :, n * feat + g * width : n * feat + (g + 1) * width
            ].astype(BF)
    w_ref[own_rows, 3 * feat : 4 * feat] = proj_ref[...].astype(BF)
    for ref, source in ((x_ref, images_ref), (cot_ref, cot_in_ref)):
        ref[...] = jnp.zeros(ref.shape, BF)
        for i in range(imgs):
            ref[i * sp : i * sp + seq, :] = source[i]
    first, second = picks_ref[0:1, :], picks_ref[1:2, :]
    sub, lane = iota((nt, nt), 0), iota((nt, nt), 1)
    pos_row = jnp.sum(jnp.where(order_col_ref[...] == lane, sub.astype(F32), 0.0), axis=0, keepdims=True)
    pos_col = jnp.sum(jnp.where(order_row_ref[...] == sub, lane.astype(F32), 0.0), axis=1, keepdims=True)
    earlier = hot(pos_col < pos_row)
    exp_id = iota((exps, nt), 0)
    hot0 = jnp.where(exp_id == first, 1.0, 0.0)
    hot1 = jnp.where(exp_id == second, 1.0, 0.0)
    before0 = dot(hot0.astype(BF), earlier)
    before1 = dot(hot1.astype(BF), earlier) + jnp.sum(hot0, axis=1, keepdims=True)
    slot0 = jnp.sum(hot0 * before0, axis=0, keepdims=True).astype(I32)
    slot1 = jnp.sum(hot1 * before1, axis=0, keepdims=True).astype(I32)
    ok0, ok1 = (slot0 < cap) & (first >= 0), (slot1 < cap) & (second >= 0)
    place0, place1 = jnp.where(ok0, first * cp + slot0, -1), jnp.where(ok1, second * cp + slot1, -1)
    place_out[0:1, :] = place0
    place_out[1:2, :] = place1
    place_out[2:8, :] = jnp.full((6, nt), -1, I32)

    pl.semaphore_wait(barrier, exps - 1 + int(pair))

    if pair:
        other_dp, other_core = (1 - at_dp, me), (at_dp, chip * 2 + 1 - core)
        small_copy = remote(
            small_ref, small_all.at[at_dp], weight_ssem.at[0], weight_rsem.at[0], other_dp
        )
        small_copy.start()

        deep, side = chip // 2, chip % 2
        wide = feat // 2
        far_base = (1 - at_dp) * shard

        def same_place(start, size, g, send, recv, device):
            place = w_ref.at[rows_at(start, size), rows_at(g * feat + core * wide, wide, 128)]
            return remote(place, place, send, recv, device)

        def dense_copy(g):
            return same_place(at_dp * shard + side * half, half, g, weight_ssem.at[1 + g], weight_rsem.at[1 + g], other_dp)

        def side_copy(g):
            device = (at_dp, (deep * 2 + 1 - side) * 2 + core)
            return same_place(far_base + side * half, half, g, side_ssem.at[g], side_rsem.at[g], device)

        def swap_copy(g):
            return same_place(far_base, shard, g, weight_ssem.at[5 + g], weight_rsem.at[5 + g], other_core)

        for g in range(CHUNKS):
            dense_copy(g).start()
        far_copies = [
            remote(
                experts[i].at[0 : experts_far[i].shape[0], :], experts_far[i],
                weight_ssem.at[9 + i], weight_rsem.at[9 + i], other_dp,
            )
            for i in range(2)
        ]
        own_copies = [pltpu.make_async_copy(experts[i], experts_own[i], own_sem.at[i]) for i in range(2)]
    cot_rows = Exchange(send_cot_ref, recv_cot_ref, cot_ssem, cot_rsem, local_sem.at[0], exps)

    def cot_chunk(r, carry):
        there = (chip + r) % chips
        row = iota((2 * cp, nt), 0) + there * (2 * cp)
        pick = hot((row == place0) | (row == place1))
        rows = dot(pick, cot_ref[...])
        for j in range(2):
            send_cot_ref[there * 2 + j] = rows[j * cp : (j + 1) * cp].astype(BF)
        cot_rows.start(r)
        return carry

    lax.fori_loop(0, chips, cot_chunk, 0)

    if pair:
        for i in range(2):
            loads[i].wait()
            unit = 64

            def narrow(n, carry, i=i, unit=unit):
                at = rows_at(n * unit, unit)
                experts[i][at, :] = staged[i][at, :].astype(BF)
                return carry

            lax.fori_loop(0, staged[i].shape[0] // unit, narrow, 0)
            far_copies[i].start()
            own_copies[i].start()

    if pair:
        small_all[at_dp] = small_ref[...]
        small_copy.wait_recv()
        small = jnp.concatenate([small_all[0], small_all[1]], axis=1)
    else:
        small_all[...] = small_ref[...]
        small = small_all[...]
    norm = small[exps : exps + 4].astype(F32)
    router_w = small[:exps]

    def first_norm(i, carry):
        at = rows_at(i * BLOCK, BLOCK, BLOCK)
        normed, _ = normed_of(x_ref[at, :].astype(F32))
        h1_ref[at, :] = (normed * norm[0:1] + norm[1:2]).astype(BF)
        return carry

    lax.fori_loop(0, nt // BLOCK, first_norm, 0)

    key_ok = iota((sp, sp), 1) < seq
    left = iota((sp, 128), 1) < HDIM

    def attend(group, i):
        rows = slice(i * sp, (i + 1) * sp)
        for p in range(per):
            cols = [group * feat + n * width + p * 128 for n in range(3)]
            query, keys, values = (mixed_ref[rows, c : c + 128] for c in cols)
            outs = []
            for mask in (left, ~left):
                scores = dot_nt(jnp.where(mask, query, jnp.zeros_like(query)), keys) * SCALE
                scores = jnp.where(key_ok, scores, NEG)
                top = jnp.max(scores, axis=-1, keepdims=True)
                grown = jnp.exp(scores - top)
                probs = grown / jnp.sum(grown, axis=-1, keepdims=True)
                outs.append(dot(probs.astype(BF), values))
            col = (group * per + p) * 128
            ctx_ref[rows, col : col + 128] = jnp.where(left, outs[0], outs[1]).astype(BF)

    ctx_ref[imgs * sp : nt, :] = jnp.zeros((nt - imgs * sp, feat), BF)
    if pair:
        dense_copy(0).wait_recv()
        side_copy(0).start()
        dense_copy(1).wait_recv()
        side_copy(1).start()
        side_copy(0).wait_recv()
        swap_copy(0).start()
        swap_copy(0).wait_recv()
    for group in range(groups):
        for n in range(2):
            at = slice(group * feat + n * (feat // 2), group * feat + (n + 1) * (feat // 2))
            mixed_ref[:, at] = dot(h1_ref[...], w_ref[:, at]).astype(BF)
        for i in range(imgs):
            if pair and i == 0 and group + 2 < CHUNKS:
                dense_copy(group + 2).wait_recv()
                side_copy(group + 2).start()
            if pair and i == imgs - 1:
                side_copy(group + 1).wait_recv()
                swap_copy(group + 1).start()
            attend(group, i)
        if pair:
            swap_copy(group + 1).wait_recv()

    def second_norm(i, carry):
        at = rows_at(i * BIG, BIG)
        after = x_ref[at, :].astype(F32) + dot(ctx_ref[at, :], w_ref[:, 3 * feat : 4 * feat])
        after_ref[at, :] = after
        normed, _ = normed_of(after)
        h2_ref[at, :] = (normed * norm[2:3] + norm[3:4]).astype(BF)
        return carry

    lax.fori_loop(0, nt // BIG, second_norm, 0)

    h2 = h2_ref[...]
    logits = dot_nt(router_w, h2)
    grown = jnp.exp(logits - jnp.max(logits, axis=0, keepdims=True))
    router = grown / jnp.sum(grown, axis=0, keepdims=True)
    router_out[...] = router
    chosen0 = jnp.sum(jnp.where(exp_id == first, router, 0.0), axis=0, keepdims=True)
    chosen1 = jnp.sum(jnp.where(exp_id == second, router, 0.0), axis=0, keepdims=True)
    total = chosen0 + chosen1
    total = jnp.where(total > 0.0, total, 1.0)
    gate0, gate1 = chosen0 / total, chosen1 / total
    for i, row in enumerate((chosen0, chosen1, gate0, gate1)):
        gates_ref[i : i + 1, :] = row
    gates_ref[4:8, :] = jnp.zeros((4, nt), F32)

    zero_rows = jnp.zeros((5, nt), F32)
    parts0 = jnp.concatenate([v.astype(F32) for v in split3(gate0)] + [zero_rows], axis=0).astype(BF)
    parts1 = jnp.concatenate([v.astype(F32) for v in split3(gate1)] + [zero_rows], axis=0).astype(BF)
    pad_ref[...] = jnp.zeros(pad_ref.shape, F32)
    token_rows = Exchange(send_ref, recv_ref, row_ssem, row_rsem, local_sem.at[1], exps)

    def row_chunk(r, carry):
        there = (chip + r) % chips
        row = iota((2 * cp, nt), 0) + there * (2 * cp)
        pick0, pick1 = hot(row == place0), hot(row == place1)
        rows = dot(pick0 + pick1, h2_ref[...])
        spread = dot_nt(parts0, pick0) + dot_nt(parts1, pick1)
        line = iota((cp, feat), 0)
        for j in range(2):
            for k in range(3):
                pad_ref[j : j + 1, k * 128 : k * 128 + cp] = spread[k : k + 1, j * cp : (j + 1) * cp]
            mine = rows[j * cp : (j + 1) * cp] + jnp.where(line == cap, pad_ref[j : j + 1, :], 0.0)
            send_ref[there * 2 + j] = mine.astype(BF)
        token_rows.start(r)
        return carry

    lax.fori_loop(0, chips, row_chunk, 0)

    if pair:
        small_copy.wait_send()
        for g in range(CHUNKS):
            dense_copy(g).wait_send()
            side_copy(g).wait_send()
            swap_copy(g).wait_send()
        for i in range(2):
            far_copies[i].wait()
            own_copies[i].wait()
    cot_rows.finish()
    token_rows.finish()


def run_front(images, cot, picks, order_row, order_col, small, qkv, proj, weights, *, nt, sp, cap, cp, exps):
    imgs, seq, feat = images.shape
    pair = weights is not None
    vmem, hbm = pl.BlockSpec(memory_space=pltpu.VMEM), pl.BlockSpec(memory_space=pl.ANY)
    dma = pltpu.SemaphoreType.DMA
    slabs = (exps, cp, feat)
    outs = [
        shape((feat, 4 * feat), BF),
        shape((2,) + small.shape if pair else small.shape, BF),
        shape((nt, feat), BF),
        shape((nt, 3 * feat), BF),
        shape((nt, feat), BF),
        shape((nt, feat), F32),
        shape((nt, feat), BF),
        shape((exps, nt), F32),
        shape((8, nt), F32),
        shape((8, nt), I32),
        shape((nt, feat), BF),
        shape((nt, feat), BF),
        shape(slabs, BF),
        shape(slabs, BF),
    ]
    ins = [images, cot, picks, order_row, order_col, small, qkv, proj]
    scratch = [pltpu.VMEM(slabs, BF), pltpu.VMEM(slabs, BF), pltpu.VMEM((8, feat), F32)]
    if pair:
        ins += list(weights)
        outs += [shape(w.shape, BF) for w in weights]
        outs += [shape(weights[0].shape, BF), shape((EARLY * TILE, feat), BF)]
        scratch += [pltpu.VMEM(w.shape, F32) for w in weights] + [pltpu.VMEM(w.shape, BF) for w in weights]
    scratch += [dma((exps,)), dma((exps,)), dma((exps,)), dma((exps,)), dma((2,))]
    if pair:
        scratch += [dma((11,)), dma((11,)), dma((CHUNKS,)), dma((CHUNKS,)), dma((2,)), dma((2,))]
    return pl.pallas_call(
        functools.partial(front_kernel, pair=pair, imgs=imgs, seq=seq, sp=sp, nt=nt, cap=cap, cp=cp, exps=exps),
        out_shape=outs,
        in_specs=[vmem] * 8 + [hbm] * (len(ins) - 8),
        out_specs=[vmem] * 12 + [hbm] * (len(outs) - 12),
        scratch_shapes=scratch,
        compiler_params=pltpu.CompilerParams(
            vmem_limit_bytes=VMEM_CAP, collective_id=3, has_side_effects=True
        ),
        cost_estimate=pl.CostEstimate(flops=20_000_000_000, bytes_accessed=60_000_000, transcendentals=0),
    )(*ins)


def gelu_both(hidden):
    bell = jnp.exp2(hidden * hidden * (-0.5 * LOG2_E))
    below = 0.5 + 0.5 * lax.erf(hidden * SQRT_HALF)
    return hidden * below, below + hidden * (bell * INV_SQRT_TAU)


def expert_kernel(*refs, pair, mine, cap, cp, exps, block):
    refs = list(refs)

    def take(count):
        taken = refs[:count]
        del refs[:count]
        return taken

    recv_in, dfin_in, inner_ref, outer_ref = take(4)
    if pair:
        inner_far, outer_far, outer_all = take(3)
    back_out, result_out, own_inner, own_outer = take(4)
    if pair:
        far_outer, sent_inner = take(2)
    recv_ref, dfin_ref, rows_ref, dres_ref, rows_t, dres_t, sum_r, sum_d, wi_ref, wo_ref, act_ref, dhid_ref = take(12)
    slab_sem = take(1)[0]
    if pair:
        landed, far_inner, back_ssem, back_rsem, outer_ssem, outer_rsem, inner_ssem, inner_rsem = take(8)
    j = pl.program_id(0)
    rows, feat = rows_ref.shape
    two = 2 * cp
    sub = iota((two, 128), 0)
    lane = iota((two, 128), 1)
    upper = sub < cp
    diag = lane == jnp.where(upper, sub, sub - cp)
    count = 2 * mine if pair else mine
    tile = wi_ref.shape[1]

    if pair:
        at_dp, me = lax.axis_index("dp"), lax.axis_index("expert")
        other_dp = (1 - at_dp, me)
        outer_copies = [
            remote(
                outer_all.at[t * tile : (t + 1) * tile, :], landed.at[t - EARLY],
                outer_ssem.at[t - EARLY], outer_rsem.at[t - EARLY], other_dp,
            )
            for t in range(EARLY, mine)
        ]
        inner_copies = [
            remote(
                far_inner.at[t], sent_inner.at[:, t * tile : (t + 1) * tile], inner_ssem.at[t], inner_rsem.at[t], other_dp
            )
            for t in range(mine)
        ]
        drows_out = Exchange(recv_ref, back_out, back_ssem, back_rsem, slab_sem.at[2], exps)
    else:
        drows_out = pltpu.make_async_copy(recv_ref, back_out, slab_sem.at[2])
    result_copy = pltpu.make_async_copy(dfin_ref, result_out, slab_sem.at[3])

    @pl.when(j == 0)
    def _():
        slabs = [
            pltpu.make_async_copy(recv_in, recv_ref, slab_sem.at[0]),
            pltpu.make_async_copy(dfin_in, dfin_ref, slab_sem.at[1]),
        ]
        for made in slabs:
            made.start()
        if pair:
            barrier = pltpu.get_barrier_semaphore()

            def greet(r, carry):
                pl.semaphore_signal(barrier, inc=1, device_id=(at_dp, (me + r) % exps), device_id_type=MESH)
                return carry

            lax.fori_loop(1, exps, greet, 0)
            pl.semaphore_signal(barrier, inc=1, device_id=other_dp, device_id_type=MESH)
            pl.semaphore_wait(barrier, exps)
            for made in outer_copies:
                made.start()
        sum_r[...] = jnp.zeros_like(sum_r)
        sum_d[...] = jnp.zeros_like(sum_d)
        for made in slabs:
            made.wait()

        def gate_rows(i, carry):
            at = rows_at(i * two, two)

            def both_of(ref):
                return jnp.concatenate([ref[2 * i].astype(F32), ref[2 * i + 1].astype(F32)], axis=0)

            recv, dfin = both_of(recv_ref), both_of(dfin_ref)
            rows_ref[at, :] = recv.astype(BF)
            lead = recv[:, 0:384]
            place = iota((two, 384), 0)
            spread = []
            for k in range(2):
                row = jnp.sum(jnp.where(place == k * cp + cap, lead, 0.0), axis=0, keepdims=True)
                spread.append(row[:, 0:128] + row[:, 128:256] + row[:, 256:384])
            both = jnp.where(upper, spread[0], spread[1])
            gate = jnp.sum(jnp.where(diag, both, 0.0), axis=1, keepdims=True)
            dres_ref[at, :] = (gate * dfin).astype(BF)
            return carry

        lax.fori_loop(0, exps // 2, gate_rows, 0)

    @pl.when(j < mine)
    def _():
        wi_ref[...] = inner_ref[...]
        wo_ref[...] = outer_ref[...]

    if pair:

        @pl.when((j >= mine) & (j < count))
        def _():
            wi_ref[...] = inner_far[...]

        @pl.when((j >= mine) & (j < mine + EARLY))
        def _():
            wo_ref[...] = outer_far[...]

        for t in range(EARLY, mine):

            @pl.when(j == mine + t)
            def _(t=t):
                outer_copies[t - EARLY].wait()
                wo_ref[...] = landed[t - EARLY]

    @pl.when(j < count)
    def _():
        for i in range(rows // block):
            at = pl.ds(i * block, block)
            hidden = dot(rows_ref[at, :], wi_ref[...])
            act, slope = gelu_both(hidden)
            act = act.astype(BF)
            dact = dot_nt(dres_ref[at, :], wo_ref[...])
            dhid = (slope * dact).astype(BF)
            act_ref[j, at, :] = act
            dhid_ref[j, at, :] = dhid
            sum_r[at, :] += dot(act, wo_ref[...])
            sum_d[at, :] += dot_nt(dhid, wi_ref[...])

    @pl.when(j == count - 1)
    def _():
        def finish(i, carry):
            at = rows_at(i * two, two)
            dfin = jnp.concatenate([dfin_ref[2 * i].astype(F32), dfin_ref[2 * i + 1].astype(F32)], axis=0)
            result = sum_r[at, :].astype(BF).astype(F32)
            dgate = jnp.sum(result * dfin, axis=1, keepdims=True)
            line = iota((two, feat), 0)
            drows = sum_d[at, :]
            for k in range(2):
                chosen = upper if k == 0 else ~upper
                row = jnp.sum(jnp.where(diag & chosen, dgate, 0.0), axis=0, keepdims=True)
                wide = jnp.concatenate(
                    [v.astype(F32) for v in split3(row)] + [jnp.zeros((1, feat - 384), F32)], axis=1
                )
                drows = drows + jnp.where(line == k * cp + cap, wide, 0.0)
            for k in range(2):
                recv_ref[2 * i + k] = drows[k * cp : (k + 1) * cp].astype(BF)
                dfin_ref[2 * i + k] = result[k * cp : (k + 1) * cp].astype(BF)
            return carry

        lax.fori_loop(0, exps // 2, finish, 0)
        if pair:

            def drows_go(r, carry):
                drows_out.start(r)
                return carry

            lax.fori_loop(0, exps // 2, drows_go, 0)
        else:
            drows_out.start()
        result_copy.start()
        rows_t[...] = rows_ref[...].T
        dres_t[...] = dres_ref[...].T

    def grads_of(n):
        inner = dot(rows_t[...], dhid_ref[n]).astype(BF)
        outer = dot(dres_t[...], act_ref[n]).astype(BF).T
        return inner, outer

    if pair:

        @pl.when((j >= count) & (j < count + mine))
        def _():
            inner, outer = grads_of(j - count + mine)
            far_inner[j - count] = inner
            far_outer[...] = outer

        for t in range(mine):

            @pl.when(j == count + t)
            def _(t=t):
                inner_copies[t].start()

    @pl.when(j >= 2 * count - mine)
    def _():
        inner, outer = grads_of(j - (2 * count - mine))
        own_inner[...] = inner
        own_outer[...] = outer

    @pl.when(j == 2 * count - 1)
    def _():
        result_copy.wait()
        if pair:
            drows_out.finish()
            for made in inner_copies:
                made.wait()
        else:
            drows_out.wait()


def run_expert(recv, dfin, own, far, cap, cp, exps):
    slabs = recv.shape
    feat = slabs[-1]
    rows = exps * cp
    inner, outer = own
    tile = min(TILE, inner.shape[1])
    mine = inner.shape[1] // tile
    pair = far is not None
    count = 2 * mine if pair else mine
    start = 2 * count - mine
    hbm = pl.BlockSpec(memory_space=pl.ANY)
    dma = pltpu.SemaphoreType.DMA

    def across(first, size=mine):
        return pl.BlockSpec((feat, tile), lambda j: (0, jnp.clip(j - first, 0, size - 1)))

    def down(first, size=mine):
        return pl.BlockSpec((tile, feat), lambda j: (jnp.clip(j - first, 0, size - 1), 0))

    in_specs = [hbm, hbm, across(0), down(0)]
    args = [recv, dfin, inner, outer]
    out_specs = [hbm, hbm, across(start), down(start)]
    out_shape = [shape(slabs, BF), shape(slabs, BF), shape(inner.shape, BF), shape(outer.shape, BF)]
    scratch = [
        pltpu.VMEM(slabs, BF),
        pltpu.VMEM(slabs, BF),
        pltpu.VMEM((rows, feat), BF),
        pltpu.VMEM((rows, feat), BF),
        pltpu.VMEM((feat, rows), BF),
        pltpu.VMEM((feat, rows), BF),
        pltpu.VMEM((rows, feat), F32),
        pltpu.VMEM((rows, feat), F32),
        pltpu.VMEM((feat, tile), BF),
        pltpu.VMEM((tile, feat), BF),
        pltpu.VMEM((count, rows, tile), BF),
        pltpu.VMEM((count, rows, tile), BF),
        dma((4,)),
    ]
    if pair:
        in_specs += [across(mine), down(mine, EARLY), hbm]
        args += [*far, outer]
        out_specs += [down(count), hbm]
        out_shape += [shape(outer.shape, BF), shape(inner.shape, BF)]
        scratch += [
            pltpu.VMEM((mine - EARLY, tile, feat), BF),
            pltpu.VMEM((mine, feat, tile), BF),
            dma((exps,)), dma((exps,)), dma((mine - EARLY,)), dma((mine - EARLY,)), dma((mine,)), dma((mine,)),
        ]
    block = next(b for b in (352, 384, 256, 128, 16) if rows % b == 0)
    return pl.pallas_call(
        functools.partial(expert_kernel, pair=pair, mine=mine, cap=cap, cp=cp, exps=exps, block=block),
        grid=(2 * count,),
        in_specs=in_specs,
        out_specs=out_specs,
        out_shape=out_shape,
        scratch_shapes=scratch,
        compiler_params=pltpu.CompilerParams(
            vmem_limit_bytes=VMEM_CAP,
            dimension_semantics=("arbitrary",),
            collective_id=4 if pair else None,
            has_side_effects=pair,
        ),
        cost_estimate=pl.CostEstimate(
            flops=12 * rows * feat * count * tile, bytes_accessed=30_000_000, transcendentals=0
        ),
    )(*args)


def back_kernel(*refs, reduce, imgs, seq, sp, cap, cp, exps):
    refs = list(refs)

    def take(count):
        taken = refs[:count]
        del refs[:count]
        return taken

    back_ref, place_col_ref, place_ref, picks_ref, gates_ref, gates_col_ref, router_ref, router_w_ref = take(8)
    h2_ref, after_ref, cot_ref, norm_ref, w_ref, mixed_ref, h1_ref, ctx_ref, x_ref, result_ref = take(10)
    if reduce:
        outer_ref = take(1)[0]
    out_ref, small_out, input_grad_ref, output_ref = take(4)
    if reduce:
        outer_out = take(1)[0]
    dafter_ref, dattn_ref, dctx_ref, dmixed_ref, grads_ref, turned_ref, rows_out_ref, results_ref = take(8)
    nt, feat = cot_ref.shape
    rows = exps * cp
    pairs = feat // 128
    groups = CHUNKS - 1
    per = pairs // groups
    width = per * 128
    key_ok = iota((sp, sp), 1) < seq
    left = iota((sp, 128), 1) < HDIM

    if reduce:
        landed, from_core, pair_sum, from_dp, dp_sum, from_y, y_sum, from_z, mine, small_in = take(10)
        (row_ssem, row_rsem, local_sem, core_send, core_recv, dp_send, dp_recv, y_send, y_recv, z_send, z_recv,
         tall_send, tall_recv, wide_send, wide_recv, last_send, last_recv, small_send, small_recv,
         outer_send, outer_recv) = take(21)
        at_dp, me = lax.axis_index("dp"), lax.axis_index("expert")
        core, chip = me % 2, me // 2
        half, quarter = feat // 2, feat // 4
        tall, wide = quarter // DEEP, feat // 2
        deep, side = chip // 2, chip % 2
        other_core, other_dp = (at_dp, chip * 2 + 1 - core), (1 - at_dp, me)
        other_side = (at_dp, (deep * 2 + 1 - side) * 2 + core)
        line = [(deep + r) % DEEP for r in range(1, DEEP)]
        peers = [(at_dp, (there * 2 + side) * 2 + core) for there in line]
        barrier = pltpu.get_barrier_semaphore()

        def greet(r, carry):
            pl.semaphore_signal(barrier, inc=1, device_id=(at_dp, (me + r) % exps), device_id_type=MESH)
            return carry

        lax.fori_loop(1, exps, greet, 0)
        pl.semaphore_signal(barrier, inc=1, device_id=other_dp, device_id_type=MESH)
        pl.semaphore_wait(barrier, exps)
        result_rows = Exchange(result_ref, landed, row_ssem, row_rsem, local_sem, exps)

        def result_go(r, carry):
            result_rows.start(r)
            return carry

        lax.fori_loop(0, exps // 2, result_go, 0)

        def core_copy(k, part):
            return remote(
                grads_ref.at[k, rows_at(part * half + (1 - core) * quarter, quarter), :],
                from_core.at[k, part], core_send.at[k, part], core_recv.at[k, part], other_core,
            )

        my_rows = rows_at(core * quarter, quarter)
        my_part = rows_at(core * quarter + deep * tall, tall)
        my_side, far_side = rows_at(side * wide, wide, 128), rows_at((1 - side) * wide, wide, 128)

        def dp_copy(k):
            return remote(pair_sum.at[k, 1 - at_dp], from_dp.at[k], dp_send.at[k], dp_recv.at[k], other_dp)

        def y_copy(k):
            return remote(dp_sum.at[k, :, far_side], from_y.at[k], y_send.at[k], y_recv.at[k], other_side)

        def z_copy(k, r):
            return remote(
                y_sum.at[k, rows_at(line[r] * tall, tall), :], from_z.at[k, r], z_send.at[k, r], z_recv.at[k, r], peers[r]
            )

        def tall_copy(k, r):
            return remote(
                mine.at[k], out_ref.at[k, my_part, my_side], tall_send.at[k, r], tall_recv.at[k, r], peers[r]
            )

        def wide_copy(k):
            place = out_ref.at[k, my_rows, my_side]
            return remote(place, place, wide_send.at[k], wide_recv.at[k], other_side)

        def last_copy(k):
            place = out_ref.at[k, my_rows, :]
            return remote(place, place, last_send.at[k], last_recv.at[k], other_core)

        def outer_copy(i):
            size = outer_ref.shape[0] // 2
            at = pl.ds(i * size, size)
            return remote(outer_ref.at[at, :], outer_out.at[at, :], outer_send.at[i], outer_recv.at[i], other_dp)

        outer_copy(0).start()
        steps = [other_core, other_dp] + [(at_dp, (chip ^ bit) * 2 + core) for bit in (1, 2, 4)]

        def small_copy(i):
            return remote(small_out, small_in.at[i], small_send.at[i], small_recv.at[i], steps[i])

    def core_start(k):
        core_copy(k, 0).start()
        core_copy(k, 1).start()

    def core_done(k):
        for part in range(2):
            core_copy(k, part).wait_recv()
            pair_sum[k, part] = (
                grads_ref[k, rows_at(part * half + core * quarter, quarter), :].astype(F32)
                + from_core[k, part].astype(F32)
            ).astype(BF)
        dp_copy(k).start()

    def dp_done(k):
        dp_copy(k).wait_recv()
        dp_sum[k] = (pair_sum[k, at_dp].astype(F32) + from_dp[k].astype(F32)).astype(BF)
        y_copy(k).start()

    def y_done(k):
        y_copy(k).wait_recv()
        y_sum[k] = (dp_sum[k, :, my_side].astype(F32) + from_y[k].astype(F32)).astype(BF)
        for r in range(DEEP - 1):
            z_copy(k, r).start()

    def z_done(k):
        total = y_sum[k, rows_at(deep * tall, tall), :].astype(F32)
        for r in range(DEEP - 1):
            z_copy(k, r).wait_recv()
            total = total + from_z[k, r].astype(F32)
        mine[k] = total.astype(BF)
        out_ref[k, my_part, my_side] = mine[k]
        for r in range(DEEP - 1):
            tall_copy(k, r).start()

    def tall_done(k):
        for r in range(DEEP - 1):
            tall_copy(k, r).wait_recv()
        wide_copy(k).start()

    def wide_done(k):
        wide_copy(k).wait_recv()
        last_copy(k).start()

    stages = (core_start, core_done, dp_done, y_done, z_done, tall_done, wide_done)

    def turn(number):
        if reduce:
            for k in reversed(range(CHUNKS)):
                if 0 <= number - k < len(stages):
                    stages[number - k](k)

    def small_go(i):
        if reduce:
            small_copy(i).start()

    def small_take(i):
        if reduce:
            small_copy(i).wait()
            small_out[...] = small_out[...] + small_in[i]

    def line_up(source):
        def step(i, carry):
            both = [source[2 * i + k].astype(F32) for k in range(2)]
            results_ref[rows_at(i * 2 * cp, 2 * cp), :] = jnp.concatenate(both, axis=0).astype(BF)
            return carry

        lax.fori_loop(0, exps // 2, step, 0)

    line_up(back_ref)
    spare = hot(iota((exps, rows), 1) == iota((exps, rows), 0) * cp + cap)
    lines = dot(spare, results_ref[:, 0:384])
    exp_id = iota((exps, nt), 0)
    dgate, match = [], []
    for k in range(2):
        pick = picks_ref[k : k + 1, :]
        place = place_ref[k : k + 1, :]
        slot = jnp.where(place >= 0, place - pick * cp, -1)
        slot_hot = hot(iota((128, nt), 0) == slot)
        found = (
            dot(lines[:, 0:128].astype(BF), slot_hot)
            + dot(lines[:, 128:256].astype(BF), slot_hot)
            + dot(lines[:, 256:384].astype(BF), slot_hot)
        )
        match.append(jnp.where(exp_id == pick, 1.0, 0.0))
        dgate.append(jnp.sum(match[k] * found, axis=0, keepdims=True))
    chosen = (gates_ref[0:1, :], gates_ref[1:2, :])
    total = chosen[0] + chosen[1]
    total = jnp.where(total > 0.0, total, 1.0)
    cross = (dgate[0] * chosen[0] + dgate[1] * chosen[1]) / (total * total)
    drouter = match[0] * (dgate[0] / total - cross) + match[1] * (dgate[1] / total - cross)
    router = router_ref[...]
    dlogits = (router * (drouter - jnp.sum(router * drouter, axis=0, keepdims=True))).astype(BF)
    norm = norm_ref[...].astype(F32)
    small_out[0:exps, :] = dot(dlogits, h2_ref[...])
    small_out[exps:, :] = jnp.zeros((small_out.shape[0] - exps, feat), F32)

    for start in range(0, nt, BIG):
        at = slice(start, start + BIG)
        slots = iota((BIG, rows), 1)
        pick = hot((slots == place_col_ref[at, 0:1]) | (slots == place_col_ref[at, 1:2]))
        dh2 = dot(pick, results_ref[...]) + dot_tn(dlogits[:, at], router_w_ref[...])
        normed, rstd = normed_of(after_ref[at, :])
        small_out[exps + 2 : exps + 3, :] += jnp.sum(dh2 * normed, axis=0, keepdims=True)
        small_out[exps + 3 : exps + 4, :] += jnp.sum(dh2, axis=0, keepdims=True)
        dafter = cot_ref[at, :].astype(F32) + norm_back_rows(dh2, normed, rstd, norm[2:3])
        dafter_ref[at, :] = dafter
        dattn = dafter.astype(BF)
        dattn_ref[at, :] = dattn
        dctx_ref[at, :] = dot_nt(dattn, w_ref[:, 3 * feat : 4 * feat]).astype(BF)

    def attend(group):
        def image(i, carry):
            lines = rows_at(i * sp, sp)
            for p in range(per):
                col = (group * per + p) * 128
                at_q, at_k, at_v = (
                    slice(c, c + 128) for c in (group * feat + n * width + p * 128 for n in range(3))
                )
                query, keys, values = mixed_ref[lines, at_q], mixed_ref[lines, at_k], mixed_ref[lines, at_v]
                dctx = dctx_ref[lines, col : col + 128]
                zero = jnp.zeros_like(query)
                dq = dk = dv = 0.0
                for mask in (left, ~left):
                    query_h = jnp.where(mask, query, zero)
                    keys_h = jnp.where(mask, keys, zero)
                    dctx_h = jnp.where(mask, dctx, zero)
                    scores = jnp.where(key_ok, dot_nt(query_h, keys) * SCALE, NEG)
                    top = jnp.max(scores, axis=-1, keepdims=True)
                    grown = jnp.exp(scores - top)
                    probs = grown / jnp.sum(grown, axis=-1, keepdims=True)
                    dv = dv + dot_tn(probs.astype(BF), dctx_h)
                    dweights = dot_nt(dctx_h, values)
                    dscores = (
                        probs * (dweights - jnp.sum(probs * dweights, axis=-1, keepdims=True))
                    ).astype(BF)
                    dq = dq + dot(dscores, keys_h)
                    dk = dk + dot_tn(dscores, query_h)
                dmixed_ref[lines, at_q] = (dq * SCALE).astype(BF)
                dmixed_ref[lines, at_k] = (dk * SCALE).astype(BF)
                dmixed_ref[lines, at_v] = dv.astype(BF)
            return carry

        lax.fori_loop(0, imgs, image, 0)
        for n in range(2):
            at = slice(n * (feat // 2), (n + 1) * (feat // 2))
            grads_ref[1 + group, :, at] = dot(
                turned_ref[...], dmixed_ref[:, group * feat + at.start : group * feat + at.stop]
            ).astype(BF)

    def first_norm(start):
        at = slice(start, start + BIG)
        dh1 = dot_nt(dmixed_ref[at, :], w_ref[:, : 3 * feat])
        normed, rstd = normed_of(x_ref[at, :].astype(F32))
        small_out[exps : exps + 1, :] += jnp.sum(dh1 * normed, axis=0, keepdims=True)
        small_out[exps + 1 : exps + 2, :] += jnp.sum(dh1, axis=0, keepdims=True)
        rows_out_ref[at, :] = (dafter_ref[at, :] + norm_back_rows(dh1, normed, rstd, norm[0:1])).astype(BF)

    def deliver(ref):
        for i in range(imgs):
            ref[i] = rows_out_ref[i * sp : i * sp + seq, :]

    def final_rows(start):
        at = slice(start, start + BIG)
        slots = iota((BIG, rows), 1)
        final = after_ref[at, :]
        for k in range(2):
            pick = hot(slots == place_col_ref[at, k : k + 1])
            final = final + gates_col_ref[at, k : k + 1] * dot(pick, results_ref[...])
        rows_out_ref[at, :] = final.astype(BF)

    dmixed_ref[imgs * sp : nt, :] = jnp.zeros((nt - imgs * sp, 3 * feat), BF)
    turned_ref[...] = ctx_ref[...].T
    for n in range(2):
        at = slice(n * (feat // 2), (n + 1) * (feat // 2))
        grads_ref[0, :, at] = dot(turned_ref[...], dattn_ref[:, at]).astype(BF)
    turn(0)
    turned_ref[...] = h1_ref[...].T
    for group in range(groups):
        attend(group)
        turn(1 + group)
    first_norm(0)
    turn(4)
    for start in range(BIG, nt, BIG):
        first_norm(start)
    deliver(input_grad_ref)
    if not reduce:
        out_ref[...] = grads_ref[...]
        line_up(result_ref)
        for start in range(0, nt, BIG):
            final_rows(start)
        deliver(output_ref)
        return
    small_go(0)
    turn(5)
    small_take(0)
    small_go(1)
    outer_copy(1).start()
    result_rows.finish()
    line_up(landed)
    final_rows(0)
    turn(6)
    small_take(1)
    small_go(2)
    for start in range(BIG, nt, BIG):
        final_rows(start)
    deliver(output_ref)
    turn(7)
    small_take(2)
    small_go(3)
    turn(8)
    small_take(3)
    small_go(4)
    turn(9)
    small_take(4)
    outer_copy(0).wait()
    outer_copy(1).wait()
    for k in range(CHUNKS):
        last_copy(k).wait()
        core_copy(k, 0).wait_send()
        core_copy(k, 1).wait_send()
        dp_copy(k).wait_send()
        y_copy(k).wait_send()
        wide_copy(k).wait_send()
        for r in range(DEEP - 1):
            z_copy(k, r).wait_send()
            tall_copy(k, r).wait_send()


def run_back(reduce, imgs, seq, sp, cap, cp, exps, *args):
    nt, feat = args[9].shape
    vmem = pl.BlockSpec(memory_space=pltpu.VMEM)
    small = up(exps + 4, 8)
    quarter = feat // 4
    scratch = [
        pltpu.VMEM((nt, feat), F32),
        pltpu.VMEM((nt, feat), BF),
        pltpu.VMEM((nt, feat), BF),
        pltpu.VMEM((nt, 3 * feat), BF),
        pltpu.VMEM((CHUNKS, feat, feat), BF),
        pltpu.VMEM((feat, nt), BF),
        pltpu.VMEM((nt, feat), BF),
        pltpu.VMEM((exps * cp, feat), BF),
    ]
    if reduce:
        dma = pltpu.SemaphoreType.DMA
        tall, wide = quarter // DEEP, feat // 2
        line = (CHUNKS, DEEP - 1)
        one, many = dma((CHUNKS,)), dma(line)
        scratch += [
            pltpu.VMEM((exps, cp, feat), BF),
            pltpu.VMEM((CHUNKS, 2, quarter, feat), BF),
            pltpu.VMEM((CHUNKS, 2, quarter, feat), BF),
            pltpu.VMEM((CHUNKS, quarter, feat), BF),
            pltpu.VMEM((CHUNKS, quarter, feat), BF),
            pltpu.VMEM((CHUNKS, quarter, wide), BF),
            pltpu.VMEM((CHUNKS, quarter, wide), BF),
            pltpu.VMEM(line + (tall, wide), BF),
            pltpu.VMEM((CHUNKS, tall, wide), BF),
            pltpu.VMEM((5, small, feat), F32),
            dma((exps,)), dma((exps,)), dma, dma((CHUNKS, 2)), dma((CHUNKS, 2)),
            one, one, one, one, many, many, many, many, one, one, one, one, dma((5,)), dma((5,)),
            dma((2,)), dma((2,)),
        ]
    hbm = pl.BlockSpec(memory_space=pl.ANY)
    extra = [shape(args[-1].shape, BF)] if reduce else []
    return pl.pallas_call(
        functools.partial(
            back_kernel, reduce=reduce, imgs=imgs, seq=seq, sp=sp, cap=cap, cp=cp, exps=exps
        ),
        out_shape=(
            shape((CHUNKS, feat // 2 if reduce else feat, feat), BF),
            shape((small, feat), F32),
            shape((imgs, seq, feat), BF),
            shape((imgs, seq, feat), BF),
            *extra,
        ),
        in_specs=[vmem] * (len(args) - 2) + [hbm] * 2 if reduce else [vmem] * len(args),
        out_specs=(vmem,) * 4 + (hbm,) * len(extra),
        scratch_shapes=scratch,
        compiler_params=pltpu.CompilerParams(
            vmem_limit_bytes=50 * 1024 * 1024, collective_id=1 if reduce else None, has_side_effects=reduce
        ),
        cost_estimate=pl.CostEstimate(flops=60_000_000_000, bytes_accessed=60_000_000, transcendentals=0),
    )(*args)


def adam_rows(weight, first, second, grad, rate, decay):
    new_first = BETA_ONE * first + (1.0 - BETA_ONE) * grad
    new_second = BETA_TWO * second + (1.0 - BETA_TWO) * grad * grad
    first_hat = new_first * (1.0 / (1.0 - BETA_ONE**STEP))
    second_hat = new_second * (1.0 / (1.0 - BETA_TWO**STEP))
    new_weight = weight - rate * (first_hat / (jnp.sqrt(second_hat) + ADAM_EPS) + decay * weight)
    return new_weight, new_first, new_second


def total_kernel(dense_ref, small_ref, *refs, shards, exps):
    far = refs[:4]
    norm_ref, part_ref, landed, send_sem, recv_sem = refs[4:]
    feat = dense_ref.shape[-1]
    at_dp, me = lax.axis_index("dp"), lax.axis_index("expert")
    count = shards * exps
    flat = at_dp * exps + me
    devices = [(((flat + r) % count) // exps, ((flat + r) % count) % exps) for r in range(1, count)]
    barrier = pltpu.get_barrier_semaphore()
    for device in devices:
        pl.semaphore_signal(barrier, inc=1, device_id=device, device_id_type=MESH)

    unit = 32

    def squares_of(read, size, width):
        def step(i, total):
            values = read(rows_at(i * unit, unit))
            return total + jnp.sum(values * values, axis=0, keepdims=True)

        return jnp.sum(lax.fori_loop(0, size // unit, step, jnp.zeros((1, width), F32)))

    half = feat // shards
    small = small_ref[:, rows_at(at_dp * half, half, 128)]
    dense_part = jnp.sum(small * small)
    for k in range(CHUNKS):
        dense_part += squares_of(lambda at, k=k: dense_ref[k, at, :].astype(F32), dense_ref.shape[1], feat)
    local = jnp.where(me == 0, dense_part, 0.0)
    for mine, theirs in (far[0:2], far[2:4]):
        local += squares_of(
            lambda at, mine=mine, theirs=theirs: mine[at, :].astype(F32) + theirs[at, :].astype(F32), *mine.shape
        )
    part_ref[...] = jnp.full(part_ref.shape, local, F32)
    pl.semaphore_wait(barrier, count - 1)
    copies = [
        remote(part_ref, landed.at[r], send_sem.at[r], recv_sem.at[r], device) for r, device in enumerate(devices)
    ]
    for made in copies:
        made.start()
    total = part_ref[...]
    for r, made in enumerate(copies):
        made.wait_recv()
        total = total + landed[r]
    norm_ref[...] = jnp.sqrt(total)
    for made in copies:
        made.wait_send()


def run_total(shards, exps, *args):
    count = shards * exps
    vmem = pl.BlockSpec(memory_space=pltpu.VMEM)
    dma = pltpu.SemaphoreType.DMA
    return pl.pallas_call(
        functools.partial(total_kernel, shards=shards, exps=exps),
        out_shape=shape((8, 128), F32),
        in_specs=[vmem] * len(args),
        out_specs=vmem,
        scratch_shapes=[
            pltpu.VMEM((8, 128), F32),
            pltpu.VMEM((count - 1, 8, 128), F32),
            dma((count - 1,)), dma((count - 1,)),
        ],
        compiler_params=pltpu.CompilerParams(
            vmem_limit_bytes=16 * 1024 * 1024, collective_id=2, has_side_effects=True
        ),
        cost_estimate=pl.CostEstimate(flops=100_000_000, bytes_accessed=20_000_000, transcendentals=0),
    )(*args)


SLOTS = 4


def adam_kernel(*refs, exps, pieces):
    refs = list(refs)

    def take(count):
        taken = refs[:count]
        del refs[:count]
        return taken

    norm_ref, small_ref, dense_ref = take(3)
    router_in, norm_in = take(3), take(3)
    far_in = take(4)
    state_in = [take(3) for _ in range(4)]
    norm_out, router_out, vector_out = take(1)[0], take(3), take(3)
    state_out = [take(3) for _ in range(4)]
    far, state, far_sem, load_sem, store_sem = refs
    tall, feat = far.shape[-2:]
    unit = 32

    def part(ref, t):
        _, down, right = pieces[t]
        return ref.at[pl.ds(down * tall, tall), pl.ds(right * feat, feat)]

    def loads(t):
        i, slot = pieces[t][0], t % SLOTS
        made = [
            pltpu.make_async_copy(part(state_in[i][n], t), state.at[slot, n], load_sem.at[slot, n]) for n in range(3)
        ]
        if i < 2:
            made += [
                pltpu.make_async_copy(part(far_in[2 * i + n], t), far.at[slot, n], far_sem.at[slot, n])
                for n in range(2)
            ]
        return made

    def stores(t):
        i, slot = pieces[t][0], t % SLOTS
        return [
            pltpu.make_async_copy(state.at[slot, n], part(state_out[i][n], t), store_sem.at[slot, n]) for n in range(3)
        ]

    def each(copies, what):
        for made in copies:
            getattr(made, what)()

    for t in range(SLOTS - 1):
        each(loads(t), "start")
    norm_out[...] = norm_ref[0:1, 0:1]
    clip = CLIP_NORM / jnp.maximum(norm_ref[0:1, 0:1], CLIP_NORM)
    small = small_ref[...]
    router_grad = small[0:exps] * clip
    for ref, new in zip(router_out, adam_rows(*(r[...] for r in router_in), router_grad, RATE_MATRIX, DECAY)):
        ref[...] = new
    vector_grad = small[exps : exps + 4] * clip
    for ref, new in zip(vector_out, adam_rows(*(r[...] for r in norm_in), vector_grad, RATE_VECTOR, 0.0)):
        ref[...] = new

    for t, (i, _, right) in enumerate(pieces):
        slot = t % SLOTS
        each(loads(t), "wait")

        def rows(u, carry, i=i, right=right, slot=slot):
            at = rows_at(u * unit, unit)
            if i < 2:
                grad = far[slot, 0, at, :].astype(F32) + far[slot, 1, at, :].astype(F32)
            elif i == 2:
                width = feat // (CHUNKS - 1)
                grad = jnp.concatenate(
                    [dense_ref[g, at, right * width : (right + 1) * width] for g in range(1, CHUNKS)], axis=1
                ).astype(F32)
            else:
                grad = dense_ref[0, at, :].astype(F32)
            new = adam_rows(*(state[slot, n, at, :] for n in range(3)), grad * clip, RATE_MATRIX, DECAY)
            for n in range(3):
                state[slot, n, at, :] = new[n]
            return carry

        lax.fori_loop(0, tall // unit, rows, 0)
        each(stores(t), "start")
        if t + SLOTS - 1 < len(pieces):
            if t >= 1:
                each(stores(t - 1), "wait")
            each(loads(t + SLOTS - 1), "start")
    for t in range(len(pieces) - SLOTS, len(pieces)):
        each(stores(t), "wait")


def run_adam(exps, norm, small, dense, router, vector, far, states):
    vmem, hbm = pl.BlockSpec(memory_space=pltpu.VMEM), pl.BlockSpec(memory_space=pl.ANY)
    dma = pltpu.SemaphoreType.DMA
    tall, feat = dense.shape[1:]
    pieces = [
        (i, down, right)
        for i, group in enumerate(states)
        for down in range(group[0].shape[0] // tall)
        for right in range(group[0].shape[1] // feat)
    ]
    flat_states = [a for group in states for a in group]
    args = [norm, small, dense, *router, *vector, *far, *flat_states]
    return pl.pallas_call(
        functools.partial(adam_kernel, exps=exps, pieces=pieces),
        out_shape=[shape((1, 1), F32)] + [shape(a.shape, F32) for a in (*router, *vector, *flat_states)],
        in_specs=[vmem] * 9 + [hbm] * 16,
        out_specs=[vmem] * 7 + [hbm] * 12,
        scratch_shapes=[
            pltpu.VMEM((SLOTS, 2, tall, feat), BF),
            pltpu.VMEM((SLOTS, 3, tall, feat), F32),
            dma((SLOTS, 2)), dma((SLOTS, 3)), dma((SLOTS, 3)),
        ],
        compiler_params=pltpu.CompilerParams(vmem_limit_bytes=26 * 1024 * 1024),
        cost_estimate=pl.CostEstimate(flops=100_000_000, bytes_accessed=100_000_000, transcendentals=0),
    )(*args)


def adam_step(weight, first, second, grad, rate, decay):
    new_first = BETA_ONE * first + (1.0 - BETA_ONE) * grad
    new_second = BETA_TWO * second + (1.0 - BETA_TWO) * grad * grad
    first_hat = new_first / (1.0 - BETA_ONE**STEP)
    second_hat = new_second / (1.0 - BETA_TWO**STEP)
    new_weight = weight - rate * (first_hat / (jnp.sqrt(second_hat) + ADAM_EPS) + decay * weight)
    return (new_weight, new_first, new_second)


def body(
    images,
    cotangent,
    routes,
    priority,
    qkv_weight,
    qkv_first,
    qkv_second,
    proj_weight,
    proj_first,
    proj_second,
    router_weight,
    router_first,
    router_second,
    norm_params,
    norm_first,
    norm_second,
    inner_weight,
    inner_first,
    inner_second,
    outer_weight,
    outer_first,
    outer_second,
):
    exps = lax.axis_size("expert")
    shards = lax.axis_size("dp")
    imgs, seq, feat = images.shape
    tok = imgs * seq
    cap = (18 * tok + 8 * exps - 1) // (8 * exps)
    cp = up(cap + 1, 8)
    sp = up(seq, 16)
    nt = up(imgs * sp, BLOCK)
    rows = exps * cp
    at_dp, at_exp = lax.axis_index("dp"), lax.axis_index("expert")
    shard_rows = qkv_weight.shape[0]
    by_kernel = shards == 2 and exps == 4 * DEEP

    def spread(values, fill=0):
        values = jnp.pad(values, ((0, 0), (0, sp - seq), (0, 0)), constant_values=fill)
        values = values.reshape(imgs * sp, values.shape[-1])
        return jnp.pad(values, ((0, nt - imgs * sp), (0, 0)), constant_values=fill)

    def unspread(values):
        return values[: imgs * sp].reshape(imgs, sp, -1)[:, :seq]

    qkv_in, proj_in = qkv_weight, proj_weight
    small = jnp.concatenate([router_weight.astype(BF).T, norm_params.astype(BF)], axis=0)
    small = jnp.pad(small, ((0, up(exps + 4, 16) - exps - 4), (0, 0)))
    if not by_kernel:
        qkv_in = lax.all_gather(qkv_weight.astype(BF), "dp", axis=0, tiled=True)
        proj_in = lax.all_gather(proj_weight.astype(BF), "dp", axis=0, tiled=True)
        small = lax.all_gather(small, "dp", axis=1, tiled=True)
    picks = jnp.concatenate([spread(routes, -1).T, jnp.full((6, nt), -1, I32)], axis=0)
    order = priority[0] + (priority[0] // seq) * (sp - seq)
    order = jnp.pad(order, (0, nt - tok), constant_values=-1)
    w_full, small, h1, mixed, context, after, h2, router, gates, place, x, cot, recv, recv_cot, *others = run_front(
        images, cotangent, picks, order[None, :], order[:, None], small, qkv_in, proj_in,
        (inner_weight[0], outer_weight[0]) if by_kernel else None,
        nt=nt, sp=sp, cap=cap, cp=cp, exps=exps,
    )
    if by_kernel:
        small = jnp.concatenate([small[0], small[1]], axis=1)
        own, far = tuple(others[:2]), tuple(others[2:])
    else:
        own, far = (
            lax.all_gather(inner_weight[0].astype(BF), "dp", axis=1, tiled=True),
            lax.all_gather(outer_weight[0].astype(BF), "dp", axis=0, tiled=True),
        ), None
    router_t, norm_b = small[:exps], small[exps : exps + 4]
    place_col = place[0:2].T
    gates_col = gates[2:4].T

    back_grad, result, own_inner, own_outer, *rest = run_expert(recv, recv_cot, own, far, cap, cp, exps)
    if by_kernel:
        far_outer, sent_inner = rest
    else:
        back_grad = lax.all_to_all(back_grad, "expert", split_axis=0, concat_axis=0, tiled=True)
        shard_inner = lax.psum_scatter(own_inner, "dp", scatter_dimension=1, tiled=True).astype(F32)[None]
        shard_outer = lax.psum_scatter(own_outer, "dp", scatter_dimension=0, tiled=True).astype(F32)[None]

    if not by_kernel:
        result = lax.all_to_all(result, "expert", split_axis=0, concat_axis=0, tiled=True)
    dense_grad, small_grad, input_grad, output, *sent = run_back(
        by_kernel, imgs, seq, sp, cap, cp, exps,
        back_grad, place_col, place, picks, gates, gates_col, router, router_t, h2, after, cot, norm_b, w_full,
        mixed, h1, context, x, result, *((far_outer,) if by_kernel else ()),
    )

    if by_kernel:
        far = (own_inner, sent_inner, own_outer, *sent)
        norm = run_total(shards, exps, dense_grad, small_grad, *far)
        small_half = lax.dynamic_slice_in_dim(small_grad, at_dp * shard_rows, shard_rows, 1)
        norm, *new = run_adam(
            exps, norm, small_half, dense_grad,
            (router_weight.T, router_first.T, router_second.T),
            (norm_params, norm_first, norm_second),
            far,
            (
                (inner_weight[0], inner_first[0], inner_second[0]),
                (outer_weight[0], outer_first[0], outer_second[0]),
                (qkv_weight, qkv_first, qkv_second),
                (proj_weight, proj_first, proj_second),
            ),
        )
        router_new, norm_new, inner_new, outer_new, qkv_new, proj_new = (new[3 * i : 3 * i + 3] for i in range(6))
        return (
            output,
            input_grad,
            norm[0, 0],
            *qkv_new,
            *proj_new,
            *(a.T for a in router_new),
            *norm_new,
            *(a[None] for a in inner_new),
            *(a[None] for a in outer_new),
        )

    dense_grad = lax.psum(dense_grad, ("dp", "expert"))
    small_grad = lax.psum(small_grad, ("dp", "expert"))
    width = feat // (CHUNKS - 1)
    dense_grad = lax.dynamic_slice_in_dim(dense_grad, at_dp * shard_rows, shard_rows, 1).astype(F32)
    shard_small = lax.dynamic_slice_in_dim(small_grad, at_dp * shard_rows, shard_rows, 1)
    shard_qkv = jnp.concatenate(
        [dense_grad[g, :, n * width : (n + 1) * width] for n in range(3) for g in range(1, CHUNKS)], axis=1
    )
    shard_proj = dense_grad[0]
    shard_router, shard_vector = shard_small[:exps].T, shard_small[exps : exps + 4]
    dense_squares = jnp.sum(dense_grad * dense_grad) + jnp.sum(shard_small * shard_small)
    expert_squares = jnp.sum(shard_inner * shard_inner) + jnp.sum(shard_outer * shard_outer)
    local_squares = expert_squares + jnp.where(at_exp == 0, dense_squares, jnp.float32(0.0))
    grad_norm = jnp.sqrt(lax.psum(local_squares, ("dp", "expert")))
    clip = CLIP_NORM / jnp.maximum(grad_norm, CLIP_NORM)
    qkv_new = adam_step(qkv_weight, qkv_first, qkv_second, shard_qkv * clip, RATE_MATRIX, DECAY)
    proj_new = adam_step(proj_weight, proj_first, proj_second, shard_proj * clip, RATE_MATRIX, DECAY)
    router_new = adam_step(
        router_weight, router_first, router_second, shard_router * clip, RATE_MATRIX, DECAY
    )
    norm_new = adam_step(norm_params, norm_first, norm_second, shard_vector * clip, RATE_VECTOR, 0.0)
    inner_new = adam_step(
        inner_weight, inner_first, inner_second, shard_inner * clip, RATE_MATRIX, DECAY
    )
    outer_new = adam_step(
        outer_weight, outer_first, outer_second, shard_outer * clip, RATE_MATRIX, DECAY
    )
    return (
        output,
        input_grad,
        grad_norm,
        *qkv_new,
        *proj_new,
        *router_new,
        *norm_new,
        *inner_new,
        *outer_new,
    )


def solution(mesh):
    tokens = P(("dp", "expert"), None, None)
    dense = P("dp", None)
    vector = P(None, "dp")
    inner = P("expert", None, "dp")
    outer = P("expert", "dp", None)
    return jax.shard_map(
        body,
        mesh=mesh,
        in_specs=(tokens, tokens, tokens, P(("dp", "expert"), None))
        + (dense,) * 9
        + (vector,) * 3
        + (inner,) * 3
        + (outer,) * 3,
        out_specs=(tokens, tokens, P())
        + (dense,) * 9
        + (vector,) * 3
        + (inner,) * 3
        + (outer,) * 3,
        check_vma=False,
    )
```

```python
import functools

import jax
import jax.numpy as jnp
from jax import lax
from jax.experimental import pallas as pl
from jax.experimental.pallas import tpu as pltpu
from jax.sharding import PartitionSpec as P

HEADS = 12
HDIM = 64
STEP = 10
SCALE = float(HDIM) ** (-0.5)

LN_EPS = 1e-06
BETA_ONE = 0.9
BETA_TWO = 0.999
ADAM_EPS = 1e-08
RATE_MATRIX = 0.06
RATE_VECTOR = 0.4
DECAY = 0.1
CLIP_NORM = 1.0

BF = jnp.bfloat16
F32 = jnp.float32
I32 = jnp.int32
NEG = -1e30
BLOCK = 128
BIG = 320
TILE = 512
EARLY = 2
CHUNKS = 4
DEEP = 4
VMEM_CAP = 60 * 1024 * 1024

LOG2_E = 1.4426950408889634
SQRT_HALF = 0.7071067811865476
INV_SQRT_TAU = 0.3989422804014327


def up(value, step):
    return -(-value // step) * step


def dot(left, right):
    return lax.dot_general(left, right, (((1,), (0,)), ((), ())), preferred_element_type=F32)


def dot_nt(left, right):
    return lax.dot_general(left, right, (((1,), (1,)), ((), ())), preferred_element_type=F32)


def dot_tn(left, right):
    return lax.dot_general(left, right, (((0,), (0,)), ((), ())), preferred_element_type=F32)


def iota(shape, axis):
    return lax.broadcasted_iota(I32, shape, axis)


def hot(mask):
    return jnp.where(mask, 1.0, 0.0).astype(BF)


def normed_of(values):
    centre = jnp.mean(values, axis=-1, keepdims=True)
    centered = values - centre
    rstd = lax.rsqrt(jnp.mean(centered * centered, axis=-1, keepdims=True) + LN_EPS)
    return centered * rstd, rstd


def norm_back_rows(grad, normed, rstd, gain):
    scaled = grad * gain
    inner_mean = jnp.mean(scaled, axis=-1, keepdims=True)
    cross_mean = jnp.mean(scaled * normed, axis=-1, keepdims=True)
    return rstd * (scaled - inner_mean - normed * cross_mean)


def split3(values):
    high = values.astype(BF)
    rest = values - high.astype(F32)
    mid = rest.astype(BF)
    low = (rest - mid.astype(F32)).astype(BF)
    return high, mid, low


def call(kernel, out_shape, *args, scratch=(), specs=None, flops=0, moved=0):
    vmem = pl.BlockSpec(memory_space=pltpu.VMEM)
    single = not isinstance(out_shape, (tuple, list))
    return pl.pallas_call(
        kernel,
        out_shape=out_shape,
        in_specs=[vmem] * len(args) if specs is None else specs,
        out_specs=vmem if single else [vmem] * len(out_shape),
        scratch_shapes=list(scratch),
        compiler_params=pltpu.CompilerParams(vmem_limit_bytes=VMEM_CAP),
        cost_estimate=pl.CostEstimate(flops=int(flops), bytes_accessed=int(moved), transcendentals=0),
    )(*args)


def shape(dims, kind):
    return jax.ShapeDtypeStruct(dims, kind)


MESH = pl.DeviceIdType.MESH


def remote(source, target, send, recv, device):
    return pltpu.make_async_remote_copy(
        src_ref=source, dst_ref=target, send_sem=send, recv_sem=recv, device_id=device, device_id_type=MESH
    )


def rows_at(start, size, unit=16):
    return pl.ds(pl.multiple_of(start, unit), size)


class Exchange:
    def __init__(self, send, recv, send_sem, recv_sem, local_sem, exps):
        self.send, self.recv, self.send_sem, self.recv_sem, self.local_sem = send, recv, send_sem, recv_sem, local_sem
        self.chips = exps // 2
        self.at_dp, self.me = lax.axis_index("dp"), lax.axis_index("expert")
        self.core, self.chip = self.me % 2, self.me // 2

    def out(self, r, j):
        there = ((self.chip + r) % self.chips) * 2 + j
        return remote(
            self.send.at[there], self.recv.at[self.me],
            self.send_sem.at[2 * r + j], self.recv_sem.at[2 * r + self.core], (self.at_dp, there),
        )

    def back(self, r, j):
        there = ((self.chip + self.chips - r) % self.chips) * 2 + j
        return remote(
            self.send.at[self.me], self.recv.at[there],
            self.send_sem.at[2 * r + j], self.recv_sem.at[2 * r + j], (self.at_dp, there),
        )

    def own(self):
        return pltpu.make_async_copy(self.send.at[self.me], self.recv.at[self.me], self.local_sem)

    def start(self, r):
        @pl.when(r == 0)
        def _():
            self.out(0, 1 - self.core).start()
            self.own().start()

        @pl.when(r > 0)
        def _():
            self.out(r, 0).start()
            self.out(r, 1).start()

    def finish(self):
        self.own().wait()
        self.out(0, 1 - self.core).wait_send()
        self.back(0, 1 - self.core).wait_recv()

        def step(r, carry):
            for j in range(2):
                self.out(r, j).wait_send()
                self.back(r, j).wait_recv()
            return carry

        lax.fori_loop(1, self.chips, step, 0)


def front_kernel(*refs, pair, imgs, seq, sp, nt, cap, cp, exps):
    refs = list(refs)

    def take(count):
        taken = refs[:count]
        del refs[:count]
        return taken

    images_ref, cot_in_ref, picks_ref, order_ref, small_ref, qkv_in, proj_in = take(7)
    if pair:
        experts_in = take(2)
    w_ref, small_out, h1_ref, mixed_ref, ctx_ref, after_ref, h2_ref, router_out, gates_ref, place_out = take(10)
    gates_col, place_col = take(2)
    x_ref, cot_ref, recv_ref, recv_cot_ref = take(4)
    if pair:
        experts_own, experts_far = take(2), take(2)
    send_ref, send_cot_ref, pad_ref, qkv_ref, proj_ref, dense_sem = take(6)
    if pair:
        small_all = take(1)[0]
        staged, experts = take(2), take(2)
    cot_ssem, cot_rsem, row_ssem, row_rsem, local_sem = take(5)
    if pair:
        weight_ssem, weight_rsem, side_ssem, side_rsem, stage_sem, own_sem = take(6)
    feat = images_ref.shape[-1]
    at_dp, me = lax.axis_index("dp"), lax.axis_index("expert")
    core, chip = me % 2, me // 2
    chips = exps // 2
    shard = qkv_ref.shape[0]
    half = shard // 2
    groups = CHUNKS - 1
    pairs = feat // 128
    per = pairs // groups

    if pair:
        loads = [pltpu.make_async_copy(experts_in[i], staged[i], stage_sem.at[i]) for i in range(2)]
        for made in loads:
            made.start()
    dense_loads = [
        pltpu.make_async_copy(qkv_in, qkv_ref, dense_sem.at[0]), pltpu.make_async_copy(proj_in, proj_ref, dense_sem.at[1])
    ]
    for made in dense_loads:
        made.start()
    barrier = pltpu.get_barrier_semaphore()

    def greet(r, carry):
        pl.semaphore_signal(
            barrier, inc=1, device_id=(at_dp, (me + r) % exps), device_id_type=MESH
        )
        return carry

    lax.fori_loop(1, exps, greet, 0)
    if pair:
        pl.semaphore_signal(barrier, inc=1, device_id=(1 - at_dp, me), device_id_type=MESH)
    width = per * 128
    own_rows = rows_at(at_dp * shard if pair else 0, shard)
    for made in dense_loads:
        made.wait()
    for g in range(groups):
        for n in range(3):
            w_ref[own_rows, g * feat + n * width : g * feat + (n + 1) * width] = qkv_ref[
                :, n * feat + g * width : n * feat + (g + 1) * width
            ].astype(BF)
    w_ref[own_rows, 3 * feat : 4 * feat] = proj_ref[...].astype(BF)
    pl.semaphore_wait(barrier, exps - 1 + int(pair))

    if pair:
        other_dp, other_core = (1 - at_dp, me), (at_dp, chip * 2 + 1 - core)
        small_copy = remote(
            small_ref, small_all.at[at_dp], weight_ssem.at[0], weight_rsem.at[0], other_dp
        )
        small_copy.start()

        deep, side = chip // 2, chip % 2
        wide = feat // 2
        far_base = (1 - at_dp) * shard

        def same_place(start, size, g, send, recv, device):
            place = w_ref.at[rows_at(start, size), rows_at(g * feat + core * wide, wide, 128)]
            return remote(place, place, send, recv, device)

        def dense_copy(g):
            return same_place(at_dp * shard + side * half, half, g, weight_ssem.at[1 + g], weight_rsem.at[1 + g], other_dp)

        def side_copy(g):
            device = (at_dp, (deep * 2 + 1 - side) * 2 + core)
            return same_place(far_base + side * half, half, g, side_ssem.at[g], side_rsem.at[g], device)

        def swap_copy(g):
            return same_place(far_base, shard, g, weight_ssem.at[5 + g], weight_rsem.at[5 + g], other_core)

        for g in range(CHUNKS):
            dense_copy(g).start()
        far_copies = [
            remote(
                experts[i].at[0 : experts_far[i].shape[0], :], experts_far[i],
                weight_ssem.at[9 + i], weight_rsem.at[9 + i], other_dp,
            )
            for i in range(2)
        ]
        own_copies = [pltpu.make_async_copy(experts[i], experts_own[i], own_sem.at[i]) for i in range(2)]
    for ref, source in ((x_ref, images_ref), (cot_ref, cot_in_ref)):
        ref[...] = jnp.zeros(ref.shape, BF)
        for i in range(imgs):
            ref[i * sp : i * sp + seq, :] = source[i]
    first, second = picks_ref[0:1, :], picks_ref[1:2, :]
    sub, lane = iota((nt, nt), 0), iota((nt, nt), 1)
    order_row = order_ref[...]
    order_col = jnp.broadcast_to(order_row.astype(F32), (8, nt)).T[:, 0:1].astype(I32)
    pos_row = jnp.sum(jnp.where(order_col == lane, sub.astype(F32), 0.0), axis=0, keepdims=True)
    pos_col = jnp.sum(jnp.where(order_row == sub, lane.astype(F32), 0.0), axis=1, keepdims=True)
    earlier = hot(pos_col < pos_row)
    exp_id = iota((exps, nt), 0)
    hot0 = jnp.where(exp_id == first, 1.0, 0.0)
    hot1 = jnp.where(exp_id == second, 1.0, 0.0)
    before0 = dot(hot0.astype(BF), earlier)
    before1 = dot(hot1.astype(BF), earlier) + jnp.sum(hot0, axis=1, keepdims=True)
    slot0 = jnp.sum(hot0 * before0, axis=0, keepdims=True).astype(I32)
    slot1 = jnp.sum(hot1 * before1, axis=0, keepdims=True).astype(I32)
    ok0, ok1 = (slot0 < cap) & (first >= 0), (slot1 < cap) & (second >= 0)
    place0, place1 = jnp.where(ok0, first * cp + slot0, -1), jnp.where(ok1, second * cp + slot1, -1)
    place_out[0:1, :] = place0
    place_out[1:2, :] = place1
    place_out[2:8, :] = jnp.full((6, nt), -1, I32)
    place_col[...] = place_out[...].astype(F32).T.astype(I32)

    cot_rows = Exchange(send_cot_ref, recv_cot_ref, cot_ssem, cot_rsem, local_sem.at[0], exps)

    def cot_chunk(r, carry):
        there = (chip + r) % chips
        row = iota((2 * cp, nt), 0) + there * (2 * cp)
        pick = hot((row == place0) | (row == place1))
        rows = dot(pick, cot_ref[...])
        for j in range(2):
            send_cot_ref[there * 2 + j] = rows[j * cp : (j + 1) * cp].astype(BF)
        cot_rows.start(r)
        return carry

    lax.fori_loop(0, chips, cot_chunk, 0)

    if pair:
        for i in range(2):
            loads[i].wait()
            unit = 64

            def narrow(n, carry, i=i, unit=unit):
                at = rows_at(n * unit, unit)
                experts[i][at, :] = staged[i][at, :].astype(BF)
                return carry

            lax.fori_loop(0, staged[i].shape[0] // unit, narrow, 0)
            far_copies[i].start()
            own_copies[i].start()

    if pair:
        small_all[at_dp] = small_ref[...]
        small_copy.wait_recv()
        small = jnp.concatenate([small_all[0], small_all[1]], axis=1)
    else:
        small = small_ref[...]
    small_out[...] = small
    norm = small[exps : exps + 4].astype(F32)
    router_w = small[:exps]

    def first_norm(i, carry):
        at = rows_at(i * BLOCK, BLOCK, BLOCK)
        normed, _ = normed_of(x_ref[at, :].astype(F32))
        h1_ref[at, :] = (normed * norm[0:1] + norm[1:2]).astype(BF)
        return carry

    lax.fori_loop(0, nt // BLOCK, first_norm, 0)

    key_ok = iota((sp, sp), 1) < seq
    left = iota((sp, 128), 1) < HDIM

    def attend(group, i):
        rows = slice(i * sp, (i + 1) * sp)
        for p in range(per):
            cols = [group * feat + n * width + p * 128 for n in range(3)]
            query, keys, values = (mixed_ref[rows, c : c + 128] for c in cols)
            outs = []
            for mask in (left, ~left):
                scores = dot_nt(jnp.where(mask, query, jnp.zeros_like(query)), keys) * SCALE
                scores = jnp.where(key_ok, scores, NEG)
                top = jnp.max(scores, axis=-1, keepdims=True)
                grown = jnp.exp(scores - top)
                probs = grown / jnp.sum(grown, axis=-1, keepdims=True)
                outs.append(dot(probs.astype(BF), values))
            col = (group * per + p) * 128
            ctx_ref[rows, col : col + 128] = jnp.where(left, outs[0], outs[1]).astype(BF)

    ctx_ref[imgs * sp : nt, :] = jnp.zeros((nt - imgs * sp, feat), BF)
    if pair:
        dense_copy(0).wait_recv()
        side_copy(0).start()
        dense_copy(1).wait_recv()
        side_copy(1).start()
        side_copy(0).wait_recv()
        swap_copy(0).start()
        swap_copy(0).wait_recv()
    for group in range(groups):
        for n in range(2):
            at = slice(group * feat + n * (feat // 2), group * feat + (n + 1) * (feat // 2))
            mixed_ref[:, at] = dot(h1_ref[...], w_ref[:, at]).astype(BF)
        for i in range(imgs):
            if pair and i == 0 and group + 2 < CHUNKS:
                dense_copy(group + 2).wait_recv()
                side_copy(group + 2).start()
            if pair and i == imgs - 1:
                side_copy(group + 1).wait_recv()
                swap_copy(group + 1).start()
            attend(group, i)
        if pair:
            swap_copy(group + 1).wait_recv()

    def second_norm(i, carry):
        at = rows_at(i * BIG, BIG)
        after = x_ref[at, :].astype(F32) + dot(ctx_ref[at, :], w_ref[:, 3 * feat : 4 * feat])
        after_ref[at, :] = after
        normed, _ = normed_of(after)
        h2_ref[at, :] = (normed * norm[2:3] + norm[3:4]).astype(BF)
        return carry

    lax.fori_loop(0, nt // BIG, second_norm, 0)

    h2 = h2_ref[...]
    logits = dot_nt(router_w, h2)
    grown = jnp.exp(logits - jnp.max(logits, axis=0, keepdims=True))
    router = grown / jnp.sum(grown, axis=0, keepdims=True)
    router_out[...] = router
    chosen0 = jnp.sum(jnp.where(exp_id == first, router, 0.0), axis=0, keepdims=True)
    chosen1 = jnp.sum(jnp.where(exp_id == second, router, 0.0), axis=0, keepdims=True)
    total = chosen0 + chosen1
    total = jnp.where(total > 0.0, total, 1.0)
    gate0, gate1 = chosen0 / total, chosen1 / total
    for i, row in enumerate((chosen0, chosen1, gate0, gate1)):
        gates_ref[i : i + 1, :] = row
    gates_ref[4:8, :] = jnp.zeros((4, nt), F32)
    gates_col[...] = gates_ref[...].T

    zero_rows = jnp.zeros((5, nt), F32)
    parts0 = jnp.concatenate([v.astype(F32) for v in split3(gate0)] + [zero_rows], axis=0).astype(BF)
    parts1 = jnp.concatenate([v.astype(F32) for v in split3(gate1)] + [zero_rows], axis=0).astype(BF)
    pad_ref[...] = jnp.zeros(pad_ref.shape, F32)
    token_rows = Exchange(send_ref, recv_ref, row_ssem, row_rsem, local_sem.at[1], exps)

    def row_chunk(r, carry):
        there = (chip + r) % chips
        row = iota((2 * cp, nt), 0) + there * (2 * cp)
        pick0, pick1 = hot(row == place0), hot(row == place1)
        rows = dot(pick0 + pick1, h2_ref[...])
        spread = dot_nt(parts0, pick0) + dot_nt(parts1, pick1)
        line = iota((cp, feat), 0)
        for j in range(2):
            for k in range(3):
                pad_ref[j : j + 1, k * 128 : k * 128 + cp] = spread[k : k + 1, j * cp : (j + 1) * cp]
            mine = rows[j * cp : (j + 1) * cp] + jnp.where(line == cap, pad_ref[j : j + 1, :], 0.0)
            send_ref[there * 2 + j] = mine.astype(BF)
        token_rows.start(r)
        return carry

    lax.fori_loop(0, chips, row_chunk, 0)

    if pair:
        small_copy.wait_send()
        for g in range(CHUNKS):
            dense_copy(g).wait_send()
            side_copy(g).wait_send()
            swap_copy(g).wait_send()
        for i in range(2):
            far_copies[i].wait()
            own_copies[i].wait()
    cot_rows.finish()
    token_rows.finish()


def run_front(images, cot, picks, order, small, qkv, proj, weights, *, nt, sp, cap, cp, exps):
    imgs, seq, feat = images.shape
    pair = weights is not None
    vmem, hbm = pl.BlockSpec(memory_space=pltpu.VMEM), pl.BlockSpec(memory_space=pl.ANY)
    dma = pltpu.SemaphoreType.DMA
    slabs = (exps, cp, feat)
    outs = [
        shape((feat, 4 * feat), BF),
        shape((small.shape[0], feat), BF),
        shape((nt, feat), BF),
        shape((nt, 3 * feat), BF),
        shape((nt, feat), BF),
        shape((nt, feat), F32),
        shape((nt, feat), BF),
        shape((exps, nt), F32),
        shape((8, nt), F32),
        shape((8, nt), I32),
        shape((nt, 8), F32),
        shape((nt, 8), I32),
        shape((nt, feat), BF),
        shape((nt, feat), BF),
        shape(slabs, BF),
        shape(slabs, BF),
    ]
    ins = [images, cot, picks, order, small, qkv, proj]
    scratch = [pltpu.VMEM(slabs, BF), pltpu.VMEM(slabs, BF), pltpu.VMEM((8, feat), F32)]
    scratch += [pltpu.VMEM(qkv.shape, qkv.dtype), pltpu.VMEM(proj.shape, proj.dtype), dma((2,))]
    if pair:
        ins += list(weights)
        outs += [shape(w.shape, BF) for w in weights]
        outs += [shape(weights[0].shape, BF), shape((EARLY * TILE, feat), BF)]
        scratch += [pltpu.VMEM((2,) + small.shape, BF)]
        scratch += [pltpu.VMEM(w.shape, F32) for w in weights] + [pltpu.VMEM(w.shape, BF) for w in weights]
    scratch += [dma((exps,)), dma((exps,)), dma((exps,)), dma((exps,)), dma((2,))]
    if pair:
        scratch += [dma((11,)), dma((11,)), dma((CHUNKS,)), dma((CHUNKS,)), dma((2,)), dma((2,))]
    return pl.pallas_call(
        functools.partial(front_kernel, pair=pair, imgs=imgs, seq=seq, sp=sp, nt=nt, cap=cap, cp=cp, exps=exps),
        out_shape=outs,
        in_specs=[vmem] * 5 + [hbm] * (len(ins) - 5),
        out_specs=[vmem] * 14 + [hbm] * (len(outs) - 14),
        scratch_shapes=scratch,
        compiler_params=pltpu.CompilerParams(
            vmem_limit_bytes=VMEM_CAP, collective_id=3, has_side_effects=True
        ),
        cost_estimate=pl.CostEstimate(flops=20_000_000_000, bytes_accessed=60_000_000, transcendentals=0),
    )(*ins)


def gelu_both(hidden):
    bell = jnp.exp2(hidden * hidden * (-0.5 * LOG2_E))
    below = 0.5 + 0.5 * lax.erf(hidden * SQRT_HALF)
    return hidden * below, below + hidden * (bell * INV_SQRT_TAU)


def expert_kernel(*refs, pair, mine, cap, cp, exps, block):
    refs = list(refs)

    def take(count):
        taken = refs[:count]
        del refs[:count]
        return taken

    recv_in, dfin_in, inner_ref, outer_ref = take(4)
    if pair:
        inner_far, outer_far, outer_all = take(3)
    back_out, result_out, own_inner, own_outer = take(4)
    if pair:
        far_outer, sent_inner = take(2)
    recv_ref, dfin_ref, rows_ref, dres_ref, rows_t, dres_t, sum_r, sum_d, wi_ref, wo_ref, act_ref, dhid_ref = take(12)
    slab_sem = take(1)[0]
    if pair:
        landed, far_inner, back_ssem, back_rsem, outer_ssem, outer_rsem, inner_ssem, inner_rsem = take(8)
    j = pl.program_id(0)
    rows, feat = rows_ref.shape
    two = 2 * cp
    sub = iota((two, 128), 0)
    lane = iota((two, 128), 1)
    upper = sub < cp
    diag = lane == jnp.where(upper, sub, sub - cp)
    count = 2 * mine if pair else mine
    tile = wi_ref.shape[1]

    if pair:
        at_dp, me = lax.axis_index("dp"), lax.axis_index("expert")
        other_dp = (1 - at_dp, me)
        outer_copies = [
            remote(
                outer_all.at[t * tile : (t + 1) * tile, :], landed.at[t - EARLY],
                outer_ssem.at[t - EARLY], outer_rsem.at[t - EARLY], other_dp,
            )
            for t in range(EARLY, mine)
        ]
        inner_copies = [
            remote(
                far_inner.at[t], sent_inner.at[:, t * tile : (t + 1) * tile], inner_ssem.at[t], inner_rsem.at[t], other_dp
            )
            for t in range(mine)
        ]
        drows_out = Exchange(recv_ref, back_out, back_ssem, back_rsem, slab_sem.at[2], exps)
    else:
        drows_out = pltpu.make_async_copy(recv_ref, back_out, slab_sem.at[2])
    result_copy = pltpu.make_async_copy(dfin_ref, result_out, slab_sem.at[3])

    @pl.when(j == 0)
    def _():
        slabs = [
            pltpu.make_async_copy(recv_in, recv_ref, slab_sem.at[0]),
            pltpu.make_async_copy(dfin_in, dfin_ref, slab_sem.at[1]),
        ]
        for made in slabs:
            made.start()
        if pair:
            barrier = pltpu.get_barrier_semaphore()

            def greet(r, carry):
                pl.semaphore_signal(barrier, inc=1, device_id=(at_dp, (me + r) % exps), device_id_type=MESH)
                return carry

            lax.fori_loop(1, exps, greet, 0)
            pl.semaphore_signal(barrier, inc=1, device_id=other_dp, device_id_type=MESH)
            pl.semaphore_wait(barrier, exps)
            for made in outer_copies:
                made.start()
        sum_r[...] = jnp.zeros_like(sum_r)
        sum_d[...] = jnp.zeros_like(sum_d)
        for made in slabs:
            made.wait()

        def gate_rows(i, carry):
            at = rows_at(i * two, two)

            def both_of(ref):
                return jnp.concatenate([ref[2 * i].astype(F32), ref[2 * i + 1].astype(F32)], axis=0)

            recv, dfin = both_of(recv_ref), both_of(dfin_ref)
            rows_ref[at, :] = recv.astype(BF)
            lead = recv[:, 0:384]
            place = iota((two, 384), 0)
            spread = []
            for k in range(2):
                row = jnp.sum(jnp.where(place == k * cp + cap, lead, 0.0), axis=0, keepdims=True)
                spread.append(row[:, 0:128] + row[:, 128:256] + row[:, 256:384])
            both = jnp.where(upper, spread[0], spread[1])
            gate = jnp.sum(jnp.where(diag, both, 0.0), axis=1, keepdims=True)
            dres_ref[at, :] = (gate * dfin).astype(BF)
            return carry

        lax.fori_loop(0, exps // 2, gate_rows, 0)

    @pl.when(j < mine)
    def _():
        wi_ref[...] = inner_ref[...]
        wo_ref[...] = outer_ref[...]

    if pair:

        @pl.when((j >= mine) & (j < count))
        def _():
            wi_ref[...] = inner_far[...]

        @pl.when((j >= mine) & (j < mine + EARLY))
        def _():
            wo_ref[...] = outer_far[...]

        for t in range(EARLY, mine):

            @pl.when(j == mine + t)
            def _(t=t):
                outer_copies[t - EARLY].wait()
                wo_ref[...] = landed[t - EARLY]

    @pl.when(j < count)
    def _():
        for i in range(rows // block):
            at = pl.ds(i * block, block)
            hidden = dot(rows_ref[at, :], wi_ref[...])
            act, slope = gelu_both(hidden)
            act = act.astype(BF)
            dact = dot_nt(dres_ref[at, :], wo_ref[...])
            dhid = (slope * dact).astype(BF)
            act_ref[j, at, :] = act
            dhid_ref[j, at, :] = dhid
            sum_r[at, :] += dot(act, wo_ref[...])
            sum_d[at, :] += dot_nt(dhid, wi_ref[...])

    @pl.when(j == count - 1)
    def _():
        def finish(i, carry):
            at = rows_at(i * two, two)
            dfin = jnp.concatenate([dfin_ref[2 * i].astype(F32), dfin_ref[2 * i + 1].astype(F32)], axis=0)
            result = sum_r[at, :].astype(BF).astype(F32)
            dgate = jnp.sum(result * dfin, axis=1, keepdims=True)
            line = iota((two, feat), 0)
            drows = sum_d[at, :]
            for k in range(2):
                chosen = upper if k == 0 else ~upper
                row = jnp.sum(jnp.where(diag & chosen, dgate, 0.0), axis=0, keepdims=True)
                wide = jnp.concatenate(
                    [v.astype(F32) for v in split3(row)] + [jnp.zeros((1, feat - 384), F32)], axis=1
                )
                drows = drows + jnp.where(line == k * cp + cap, wide, 0.0)
            for k in range(2):
                recv_ref[2 * i + k] = drows[k * cp : (k + 1) * cp].astype(BF)
                dfin_ref[2 * i + k] = result[k * cp : (k + 1) * cp].astype(BF)
            return carry

        lax.fori_loop(0, exps // 2, finish, 0)
        if pair:

            def drows_go(r, carry):
                drows_out.start(r)
                return carry

            lax.fori_loop(0, exps // 2, drows_go, 0)
        else:
            drows_out.start()
        result_copy.start()
        rows_t[...] = rows_ref[...].T
        dres_t[...] = dres_ref[...].T

    def grads_of(n):
        inner = dot(rows_t[...], dhid_ref[n]).astype(BF)
        outer = dot(dres_t[...], act_ref[n]).astype(BF).T
        return inner, outer

    if pair:

        @pl.when((j >= count) & (j < count + mine))
        def _():
            inner, outer = grads_of(j - count + mine)
            far_inner[j - count] = inner
            far_outer[...] = outer

        for t in range(mine):

            @pl.when(j == count + t)
            def _(t=t):
                inner_copies[t].start()

    @pl.when(j >= 2 * count - mine)
    def _():
        inner, outer = grads_of(j - (2 * count - mine))
        own_inner[...] = inner
        own_outer[...] = outer

    @pl.when(j == 2 * count - 1)
    def _():
        result_copy.wait()
        if pair:
            drows_out.finish()
            for made in inner_copies:
                made.wait()
        else:
            drows_out.wait()


def run_expert(recv, dfin, own, far, cap, cp, exps):
    slabs = recv.shape
    feat = slabs[-1]
    rows = exps * cp
    inner, outer = own
    tile = min(TILE, inner.shape[1])
    mine = inner.shape[1] // tile
    pair = far is not None
    count = 2 * mine if pair else mine
    start = 2 * count - mine
    hbm = pl.BlockSpec(memory_space=pl.ANY)
    dma = pltpu.SemaphoreType.DMA

    def across(first, size=mine):
        return pl.BlockSpec((feat, tile), lambda j: (0, jnp.clip(j - first, 0, size - 1)))

    def down(first, size=mine):
        return pl.BlockSpec((tile, feat), lambda j: (jnp.clip(j - first, 0, size - 1), 0))

    in_specs = [hbm, hbm, across(0), down(0)]
    args = [recv, dfin, inner, outer]
    out_specs = [hbm, hbm, across(start), down(start)]
    out_shape = [shape(slabs, BF), shape(slabs, BF), shape(inner.shape, BF), shape(outer.shape, BF)]
    scratch = [
        pltpu.VMEM(slabs, BF),
        pltpu.VMEM(slabs, BF),
        pltpu.VMEM((rows, feat), BF),
        pltpu.VMEM((rows, feat), BF),
        pltpu.VMEM((feat, rows), BF),
        pltpu.VMEM((feat, rows), BF),
        pltpu.VMEM((rows, feat), F32),
        pltpu.VMEM((rows, feat), F32),
        pltpu.VMEM((feat, tile), BF),
        pltpu.VMEM((tile, feat), BF),
        pltpu.VMEM((count, rows, tile), BF),
        pltpu.VMEM((count, rows, tile), BF),
        dma((4,)),
    ]
    if pair:
        in_specs += [across(mine), down(mine, EARLY), hbm]
        args += [*far, outer]
        out_specs += [down(count), hbm]
        out_shape += [shape(outer.shape, BF), shape(inner.shape, BF)]
        scratch += [
            pltpu.VMEM((mine - EARLY, tile, feat), BF),
            pltpu.VMEM((mine, feat, tile), BF),
            dma((exps,)), dma((exps,)), dma((mine - EARLY,)), dma((mine - EARLY,)), dma((mine,)), dma((mine,)),
        ]
    block = next(b for b in (352, 384, 256, 128, 16) if rows % b == 0)
    return pl.pallas_call(
        functools.partial(expert_kernel, pair=pair, mine=mine, cap=cap, cp=cp, exps=exps, block=block),
        grid=(2 * count,),
        in_specs=in_specs,
        out_specs=out_specs,
        out_shape=out_shape,
        scratch_shapes=scratch,
        compiler_params=pltpu.CompilerParams(
            vmem_limit_bytes=VMEM_CAP,
            dimension_semantics=("arbitrary",),
            collective_id=4 if pair else None,
            has_side_effects=pair,
        ),
        cost_estimate=pl.CostEstimate(
            flops=12 * rows * feat * count * tile, bytes_accessed=30_000_000, transcendentals=0
        ),
    )(*args)


def back_kernel(*refs, reduce, imgs, seq, sp, cap, cp, exps):
    refs = list(refs)

    def take(count):
        taken = refs[:count]
        del refs[:count]
        return taken

    back_ref, place_col_ref, place_ref, picks_ref, gates_ref, gates_col_ref, router_ref = take(7)
    h2_ref, after_ref, cot_ref, small_ref, w_ref, mixed_ref, h1_ref, ctx_ref, x_ref, result_ref = take(10)
    if reduce:
        outer_ref = take(1)[0]
    out_ref, small_out, input_grad_ref, output_ref = take(4)
    if reduce:
        outer_out = take(1)[0]
    dafter_ref, dattn_ref, dctx_ref, dmixed_ref, grads_ref, turned_ref, rows_out_ref, results_ref = take(8)
    nt, feat = cot_ref.shape
    rows = exps * cp
    pairs = feat // 128
    groups = CHUNKS - 1
    per = pairs // groups
    width = per * 128
    key_ok = iota((sp, sp), 1) < seq
    left = iota((sp, 128), 1) < HDIM

    if reduce:
        landed, from_core, pair_sum, from_dp, dp_sum, from_y, y_sum, from_z, mine, small_in = take(10)
        (row_ssem, row_rsem, local_sem, core_send, core_recv, dp_send, dp_recv, y_send, y_recv, z_send, z_recv,
         tall_send, tall_recv, wide_send, wide_recv, last_send, last_recv, small_send, small_recv,
         outer_send, outer_recv) = take(21)
        at_dp, me = lax.axis_index("dp"), lax.axis_index("expert")
        core, chip = me % 2, me // 2
        half, quarter = feat // 2, feat // 4
        tall, wide = quarter // DEEP, feat // 2
        deep, side = chip // 2, chip % 2
        other_core, other_dp = (at_dp, chip * 2 + 1 - core), (1 - at_dp, me)
        other_side = (at_dp, (deep * 2 + 1 - side) * 2 + core)
        line = [(deep + r) % DEEP for r in range(1, DEEP)]
        peers = [(at_dp, (there * 2 + side) * 2 + core) for there in line]
        barrier = pltpu.get_barrier_semaphore()

        def greet(r, carry):
            pl.semaphore_signal(barrier, inc=1, device_id=(at_dp, (me + r) % exps), device_id_type=MESH)
            return carry

        lax.fori_loop(1, exps, greet, 0)
        pl.semaphore_signal(barrier, inc=1, device_id=other_dp, device_id_type=MESH)
        pl.semaphore_wait(barrier, exps)
        result_rows = Exchange(result_ref, landed, row_ssem, row_rsem, local_sem, exps)

        def result_go(r, carry):
            result_rows.start(r)
            return carry

        lax.fori_loop(0, exps // 2, result_go, 0)

        def core_copy(k, part):
            return remote(
                grads_ref.at[k, rows_at(part * half + (1 - core) * quarter, quarter), :],
                from_core.at[k, part], core_send.at[k, part], core_recv.at[k, part], other_core,
            )

        my_rows = rows_at(core * quarter, quarter)
        my_part = rows_at(core * quarter + deep * tall, tall)
        my_side, far_side = rows_at(side * wide, wide, 128), rows_at((1 - side) * wide, wide, 128)

        def dp_copy(k):
            return remote(pair_sum.at[k, 1 - at_dp], from_dp.at[k], dp_send.at[k], dp_recv.at[k], other_dp)

        def y_copy(k):
            return remote(dp_sum.at[k, :, far_side], from_y.at[k], y_send.at[k], y_recv.at[k], other_side)

        def z_copy(k, r):
            return remote(
                y_sum.at[k, rows_at(line[r] * tall, tall), :], from_z.at[k, r], z_send.at[k, r], z_recv.at[k, r], peers[r]
            )

        def tall_copy(k, r):
            return remote(
                mine.at[k], out_ref.at[k, my_part, my_side], tall_send.at[k, r], tall_recv.at[k, r], peers[r]
            )

        def wide_copy(k):
            place = out_ref.at[k, my_rows, my_side]
            return remote(place, place, wide_send.at[k], wide_recv.at[k], other_side)

        def last_copy(k):
            place = out_ref.at[k, my_rows, :]
            return remote(place, place, last_send.at[k], last_recv.at[k], other_core)

        def outer_copy(i):
            size = outer_ref.shape[0] // 2
            at = pl.ds(i * size, size)
            return remote(outer_ref.at[at, :], outer_out.at[at, :], outer_send.at[i], outer_recv.at[i], other_dp)

        outer_copy(0).start()
        steps = [other_core, other_dp] + [(at_dp, (chip ^ bit) * 2 + core) for bit in (1, 2, 4)]

        def small_copy(i):
            return remote(small_out, small_in.at[i], small_send.at[i], small_recv.at[i], steps[i])

    def core_start(k):
        core_copy(k, 0).start()
        core_copy(k, 1).start()

    def core_done(k):
        for part in range(2):
            core_copy(k, part).wait_recv()
            pair_sum[k, part] = (
                grads_ref[k, rows_at(part * half + core * quarter, quarter), :].astype(F32)
                + from_core[k, part].astype(F32)
            ).astype(BF)
        dp_copy(k).start()

    def dp_done(k):
        dp_copy(k).wait_recv()
        dp_sum[k] = (pair_sum[k, at_dp].astype(F32) + from_dp[k].astype(F32)).astype(BF)
        y_copy(k).start()

    def y_done(k):
        y_copy(k).wait_recv()
        y_sum[k] = (dp_sum[k, :, my_side].astype(F32) + from_y[k].astype(F32)).astype(BF)
        for r in range(DEEP - 1):
            z_copy(k, r).start()

    def z_done(k):
        total = y_sum[k, rows_at(deep * tall, tall), :].astype(F32)
        for r in range(DEEP - 1):
            z_copy(k, r).wait_recv()
            total = total + from_z[k, r].astype(F32)
        mine[k] = total.astype(BF)
        out_ref[k, my_part, my_side] = mine[k]
        for r in range(DEEP - 1):
            tall_copy(k, r).start()

    def tall_done(k):
        for r in range(DEEP - 1):
            tall_copy(k, r).wait_recv()
        wide_copy(k).start()

    def wide_done(k):
        wide_copy(k).wait_recv()
        last_copy(k).start()

    stages = (core_start, core_done, dp_done, y_done, z_done, tall_done, wide_done)

    def turn(number):
        if reduce:
            for k in reversed(range(CHUNKS)):
                if 0 <= number - k < len(stages):
                    stages[number - k](k)

    def small_go(i):
        if reduce:
            small_copy(i).start()

    def small_take(i):
        if reduce:
            small_copy(i).wait()
            small_out[...] = small_out[...] + small_in[i]

    def line_up(source):
        def step(i, carry):
            both = [source[2 * i + k].astype(F32) for k in range(2)]
            results_ref[rows_at(i * 2 * cp, 2 * cp), :] = jnp.concatenate(both, axis=0).astype(BF)
            return carry

        lax.fori_loop(0, exps // 2, step, 0)

    line_up(back_ref)
    spare = hot(iota((exps, rows), 1) == iota((exps, rows), 0) * cp + cap)
    lines = dot(spare, results_ref[:, 0:384])
    exp_id = iota((exps, nt), 0)
    dgate, match = [], []
    for k in range(2):
        pick = picks_ref[k : k + 1, :]
        place = place_ref[k : k + 1, :]
        slot = jnp.where(place >= 0, place - pick * cp, -1)
        slot_hot = hot(iota((128, nt), 0) == slot)
        found = (
            dot(lines[:, 0:128].astype(BF), slot_hot)
            + dot(lines[:, 128:256].astype(BF), slot_hot)
            + dot(lines[:, 256:384].astype(BF), slot_hot)
        )
        match.append(jnp.where(exp_id == pick, 1.0, 0.0))
        dgate.append(jnp.sum(match[k] * found, axis=0, keepdims=True))
    chosen = (gates_ref[0:1, :], gates_ref[1:2, :])
    total = chosen[0] + chosen[1]
    total = jnp.where(total > 0.0, total, 1.0)
    cross = (dgate[0] * chosen[0] + dgate[1] * chosen[1]) / (total * total)
    drouter = match[0] * (dgate[0] / total - cross) + match[1] * (dgate[1] / total - cross)
    router = router_ref[...]
    dlogits = (router * (drouter - jnp.sum(router * drouter, axis=0, keepdims=True))).astype(BF)
    norm = small_ref[exps : exps + 4, :].astype(F32)
    small_out[0:exps, :] = dot(dlogits, h2_ref[...])
    small_out[exps:, :] = jnp.zeros((small_out.shape[0] - exps, feat), F32)

    for start in range(0, nt, BIG):
        at = slice(start, start + BIG)
        slots = iota((BIG, rows), 1)
        pick = hot((slots == place_col_ref[at, 0:1]) | (slots == place_col_ref[at, 1:2]))
        dh2 = dot(pick, results_ref[...]) + dot_tn(dlogits[:, at], small_ref[0:exps, :])
        normed, rstd = normed_of(after_ref[at, :])
        small_out[exps + 2 : exps + 3, :] += jnp.sum(dh2 * normed, axis=0, keepdims=True)
        small_out[exps + 3 : exps + 4, :] += jnp.sum(dh2, axis=0, keepdims=True)
        dafter = cot_ref[at, :].astype(F32) + norm_back_rows(dh2, normed, rstd, norm[2:3])
        dafter_ref[at, :] = dafter
        dattn = dafter.astype(BF)
        dattn_ref[at, :] = dattn
        dctx_ref[at, :] = dot_nt(dattn, w_ref[:, 3 * feat : 4 * feat]).astype(BF)

    def attend(group):
        def image(i, carry):
            lines = rows_at(i * sp, sp)
            for p in range(per):
                col = (group * per + p) * 128
                at_q, at_k, at_v = (
                    slice(c, c + 128) for c in (group * feat + n * width + p * 128 for n in range(3))
                )
                query, keys, values = mixed_ref[lines, at_q], mixed_ref[lines, at_k], mixed_ref[lines, at_v]
                dctx = dctx_ref[lines, col : col + 128]
                zero = jnp.zeros_like(query)
                dq = dk = dv = 0.0
                for mask in (left, ~left):
                    query_h = jnp.where(mask, query, zero)
                    keys_h = jnp.where(mask, keys, zero)
                    dctx_h = jnp.where(mask, dctx, zero)
                    scores = jnp.where(key_ok, dot_nt(query_h, keys) * SCALE, NEG)
                    top = jnp.max(scores, axis=-1, keepdims=True)
                    grown = jnp.exp(scores - top)
                    probs = grown / jnp.sum(grown, axis=-1, keepdims=True)
                    dv = dv + dot_tn(probs.astype(BF), dctx_h)
                    dweights = dot_nt(dctx_h, values)
                    dscores = (
                        probs * (dweights - jnp.sum(probs * dweights, axis=-1, keepdims=True))
                    ).astype(BF)
                    dq = dq + dot(dscores, keys_h)
                    dk = dk + dot_tn(dscores, query_h)
                dmixed_ref[lines, at_q] = (dq * SCALE).astype(BF)
                dmixed_ref[lines, at_k] = (dk * SCALE).astype(BF)
                dmixed_ref[lines, at_v] = dv.astype(BF)
            return carry

        lax.fori_loop(0, imgs, image, 0)
        for n in range(2):
            at = slice(n * (feat // 2), (n + 1) * (feat // 2))
            grads_ref[1 + group, :, at] = dot(
                turned_ref[...], dmixed_ref[:, group * feat + at.start : group * feat + at.stop]
            ).astype(BF)

    def first_norm(start):
        at = slice(start, start + BIG)
        dh1 = dot_nt(dmixed_ref[at, :], w_ref[:, : 3 * feat])
        normed, rstd = normed_of(x_ref[at, :].astype(F32))
        small_out[exps : exps + 1, :] += jnp.sum(dh1 * normed, axis=0, keepdims=True)
        small_out[exps + 1 : exps + 2, :] += jnp.sum(dh1, axis=0, keepdims=True)
        rows_out_ref[at, :] = (dafter_ref[at, :] + norm_back_rows(dh1, normed, rstd, norm[0:1])).astype(BF)

    def deliver(ref):
        for i in range(imgs):
            ref[i] = rows_out_ref[i * sp : i * sp + seq, :]

    def final_rows(start):
        at = slice(start, start + BIG)
        slots = iota((BIG, rows), 1)
        final = after_ref[at, :]
        for k in range(2):
            pick = hot(slots == place_col_ref[at, k : k + 1])
            final = final + gates_col_ref[at, 2 + k : 3 + k] * dot(pick, results_ref[...])
        rows_out_ref[at, :] = final.astype(BF)

    dmixed_ref[imgs * sp : nt, :] = jnp.zeros((nt - imgs * sp, 3 * feat), BF)
    turned_ref[...] = ctx_ref[...].T
    for n in range(2):
        at = slice(n * (feat // 2), (n + 1) * (feat // 2))
        grads_ref[0, :, at] = dot(turned_ref[...], dattn_ref[:, at]).astype(BF)
    turn(0)
    turned_ref[...] = h1_ref[...].T
    for group in range(groups):
        attend(group)
        turn(1 + group)
    first_norm(0)
    if reduce:
        core_done(3)
        dp_done(2)
        y_done(1)
    for start in range(BIG, nt, BIG):
        first_norm(start)
    deliver(input_grad_ref)
    if not reduce:
        out_ref[...] = grads_ref[...]
        line_up(result_ref)
        for start in range(0, nt, BIG):
            final_rows(start)
        deliver(output_ref)
        return
    small_go(0)
    dp_done(3)
    y_done(2)
    small_take(0)
    small_go(1)
    outer_copy(1).start()
    y_done(3)
    z_done(0)
    z_done(1)
    small_take(1)
    small_go(2)
    z_done(2)
    z_done(3)
    result_rows.finish()
    line_up(landed)
    final_rows(0)
    tall_done(0)
    small_take(2)
    small_go(3)
    tall_done(1)
    tall_done(2)
    for start in range(BIG, nt, BIG):
        final_rows(start)
    deliver(output_ref)
    small_take(3)
    small_go(4)
    tall_done(3)
    for k in range(CHUNKS):
        wide_done(k)
    small_take(4)
    outer_copy(0).wait()
    outer_copy(1).wait()
    for k in range(CHUNKS):
        last_copy(k).wait()
        core_copy(k, 0).wait_send()
        core_copy(k, 1).wait_send()
        dp_copy(k).wait_send()
        y_copy(k).wait_send()
        wide_copy(k).wait_send()
        for r in range(DEEP - 1):
            z_copy(k, r).wait_send()
            tall_copy(k, r).wait_send()


def run_back(reduce, imgs, seq, sp, cap, cp, exps, *args):
    nt, feat = args[8].shape
    vmem = pl.BlockSpec(memory_space=pltpu.VMEM)
    small = up(exps + 4, 8)
    quarter = feat // 4
    scratch = [
        pltpu.VMEM((nt, feat), F32),
        pltpu.VMEM((nt, feat), BF),
        pltpu.VMEM((nt, feat), BF),
        pltpu.VMEM((nt, 3 * feat), BF),
        pltpu.VMEM((CHUNKS, feat, feat), BF),
        pltpu.VMEM((feat, nt), BF),
        pltpu.VMEM((nt, feat), BF),
        pltpu.VMEM((exps * cp, feat), BF),
    ]
    if reduce:
        dma = pltpu.SemaphoreType.DMA
        tall, wide = quarter // DEEP, feat // 2
        line = (CHUNKS, DEEP - 1)
        one, many = dma((CHUNKS,)), dma(line)
        scratch += [
            pltpu.VMEM((exps, cp, feat), BF),
            pltpu.VMEM((CHUNKS, 2, quarter, feat), BF),
            pltpu.VMEM((CHUNKS, 2, quarter, feat), BF),
            pltpu.VMEM((CHUNKS, quarter, feat), BF),
            pltpu.VMEM((CHUNKS, quarter, feat), BF),
            pltpu.VMEM((CHUNKS, quarter, wide), BF),
            pltpu.VMEM((CHUNKS, quarter, wide), BF),
            pltpu.VMEM(line + (tall, wide), BF),
            pltpu.VMEM((CHUNKS, tall, wide), BF),
            pltpu.VMEM((5, small, feat), F32),
            dma((exps,)), dma((exps,)), dma, dma((CHUNKS, 2)), dma((CHUNKS, 2)),
            one, one, one, one, many, many, many, many, one, one, one, one, dma((5,)), dma((5,)),
            dma((2,)), dma((2,)),
        ]
    hbm = pl.BlockSpec(memory_space=pl.ANY)
    extra = [shape(args[-1].shape, BF)] if reduce else []
    return pl.pallas_call(
        functools.partial(
            back_kernel, reduce=reduce, imgs=imgs, seq=seq, sp=sp, cap=cap, cp=cp, exps=exps
        ),
        out_shape=(
            shape((CHUNKS, feat // 2 if reduce else feat, feat), BF),
            shape((small, feat), F32),
            shape((imgs, seq, feat), BF),
            shape((imgs, seq, feat), BF),
            *extra,
        ),
        in_specs=[vmem] * (len(args) - 2) + [hbm] * 2 if reduce else [vmem] * len(args),
        out_specs=(vmem,) * 4 + (hbm,) * len(extra),
        scratch_shapes=scratch,
        compiler_params=pltpu.CompilerParams(
            vmem_limit_bytes=50 * 1024 * 1024, collective_id=1 if reduce else None, has_side_effects=reduce
        ),
        cost_estimate=pl.CostEstimate(flops=60_000_000_000, bytes_accessed=60_000_000, transcendentals=0),
    )(*args)


def adam_rows(weight, first, second, grad, rate, decay):
    new_first = BETA_ONE * first + (1.0 - BETA_ONE) * grad
    new_second = BETA_TWO * second + (1.0 - BETA_TWO) * grad * grad
    first_hat = new_first * (1.0 / (1.0 - BETA_ONE**STEP))
    second_hat = new_second * (1.0 / (1.0 - BETA_TWO**STEP))
    new_weight = weight - rate * (first_hat / (jnp.sqrt(second_hat) + ADAM_EPS) + decay * weight)
    return new_weight, new_first, new_second


def total_kernel(small_ref, dense_in, *refs, shards, exps):
    far_in = refs[:4]
    norm_ref, dense_ref, far, part_ref, landed, dense_sem, far_sem, send_sem, recv_sem = refs[4:]
    tall, feat = dense_ref.shape[1:]
    at_dp, me = lax.axis_index("dp"), lax.axis_index("expert")
    count = shards * exps
    flat = at_dp * exps + me
    devices = [(((flat + r) % count) // exps, ((flat + r) % count) % exps) for r in range(1, count)]
    pieces = [
        (2 * i, down, right)
        for i in range(2)
        for down in range(far_in[2 * i].shape[0] // tall)
        for right in range(far_in[2 * i].shape[1] // feat)
    ]

    def load(t, n):
        i, down, right = pieces[t]
        source = far_in[i + n].at[pl.ds(down * tall, tall), pl.ds(right * feat, feat)]
        return pltpu.make_async_copy(source, far.at[t, n], far_sem.at[t, n])

    def load_dense(k):
        return pltpu.make_async_copy(dense_in.at[k], dense_ref.at[k], dense_sem.at[k])

    for k in range(CHUNKS):
        load_dense(k).start()
    for t in range(len(pieces)):
        load(t, 0).start()
        load(t, 1).start()
    barrier = pltpu.get_barrier_semaphore()

    def greet(r, carry):
        there = (flat + r) % count
        pl.semaphore_signal(barrier, inc=1, device_id=(there // exps, there % exps), device_id_type=MESH)
        return carry

    lax.fori_loop(1, count, greet, 0)
    unit = 32

    def squares_of(read):
        def step(i, total):
            values = read(rows_at(i * unit, unit))
            return total + jnp.sum((values * values).reshape(unit // 8, 8, feat), axis=0)

        return lax.fori_loop(0, tall // unit, step, jnp.zeros((8, feat), F32))

    half = feat // shards
    small = small_ref[:, rows_at(at_dp * half, half, 128)]
    dense_part = jnp.zeros((8, feat), F32)
    for k in range(CHUNKS):
        load_dense(k).wait()
        dense_part += squares_of(lambda at, k=k: dense_ref[k, at, :].astype(F32))
    local = jnp.where(me == 0, jnp.sum(dense_part) + jnp.sum(small * small), 0.0)
    part = jnp.zeros((8, feat), F32)
    for t in range(len(pieces)):
        load(t, 0).wait()
        load(t, 1).wait()
        part += squares_of(lambda at, t=t: far[t, 0, at, :].astype(F32) + far[t, 1, at, :].astype(F32))
    part_ref[...] = jnp.full(part_ref.shape, local + jnp.sum(part), F32)
    pl.semaphore_wait(barrier, count - 1)
    copies = [
        remote(part_ref, landed.at[r], send_sem.at[r], recv_sem.at[r], device) for r, device in enumerate(devices)
    ]
    for made in copies:
        made.start()
    total = part_ref[...]
    for r, made in enumerate(copies):
        made.wait_recv()
        total = total + landed[r]
    norm_ref[...] = jnp.sqrt(total)
    for made in copies:
        made.wait_send()


def run_total(shards, exps, small, dense, *far):
    count = shards * exps
    vmem, hbm = pl.BlockSpec(memory_space=pltpu.VMEM), pl.BlockSpec(memory_space=pl.ANY)
    dma = pltpu.SemaphoreType.DMA
    tall, feat = dense.shape[1:]
    pieces = sum(a.size for a in far) // (2 * tall * feat)
    return pl.pallas_call(
        functools.partial(total_kernel, shards=shards, exps=exps),
        out_shape=shape((8, 128), F32),
        in_specs=[vmem] + [hbm] * (1 + len(far)),
        out_specs=vmem,
        scratch_shapes=[
            pltpu.VMEM(dense.shape, BF),
            pltpu.VMEM((pieces, 2, tall, feat), BF),
            pltpu.VMEM((8, 128), F32),
            pltpu.VMEM((count - 1, 8, 128), F32),
            dma((CHUNKS,)), dma((pieces, 2)), dma((count - 1,)), dma((count - 1,)),
        ],
        compiler_params=pltpu.CompilerParams(
            vmem_limit_bytes=60 * 1024 * 1024, collective_id=2, has_side_effects=True
        ),
        cost_estimate=pl.CostEstimate(flops=100_000_000, bytes_accessed=20_000_000, transcendentals=0),
    )(small, dense, *far)


SLOTS = 4


def adam_kernel(*refs, exps, pieces):
    refs = list(refs)

    def take(count):
        taken = refs[:count]
        del refs[:count]
        return taken

    norm_ref, small_ref, dense_ref = take(3)
    router_in, norm_in = take(3), take(3)
    far_in = take(4)
    state_in = [take(3) for _ in range(4)]
    norm_out, router_out, vector_out = take(1)[0], take(3), take(3)
    state_out = [take(3) for _ in range(4)]
    far, state, far_sem, load_sem, store_sem = refs
    tall, feat = far.shape[-2:]
    unit = 32

    def part(ref, t):
        _, down, right = pieces[t]
        return ref.at[pl.ds(down * tall, tall), pl.ds(right * feat, feat)]

    def loads(t):
        i, slot = pieces[t][0], t % SLOTS
        made = [
            pltpu.make_async_copy(part(state_in[i][n], t), state.at[slot, n], load_sem.at[slot, n]) for n in range(3)
        ]
        if i < 2:
            made += [
                pltpu.make_async_copy(part(far_in[2 * i + n], t), far.at[slot, n], far_sem.at[slot, n])
                for n in range(2)
            ]
        return made

    def stores(t):
        i, slot = pieces[t][0], t % SLOTS
        return [
            pltpu.make_async_copy(state.at[slot, n], part(state_out[i][n], t), store_sem.at[slot, n]) for n in range(3)
        ]

    def each(copies, what):
        for made in copies:
            getattr(made, what)()

    for t in range(SLOTS - 1):
        each(loads(t), "start")
    norm_out[...] = norm_ref[0:1, 0:1]
    clip = CLIP_NORM / jnp.maximum(norm_ref[0:1, 0:1], CLIP_NORM)
    small = small_ref[...]
    router_grad = small[0:exps] * clip
    for ref, new in zip(router_out, adam_rows(*(r[...] for r in router_in), router_grad, RATE_MATRIX, DECAY)):
        ref[...] = new
    vector_grad = small[exps : exps + 4] * clip
    for ref, new in zip(vector_out, adam_rows(*(r[...] for r in norm_in), vector_grad, RATE_VECTOR, 0.0)):
        ref[...] = new

    for t, (i, _, right) in enumerate(pieces):
        slot = t % SLOTS
        each(loads(t), "wait")

        def rows(u, carry, i=i, right=right, slot=slot):
            at = rows_at(u * unit, unit)
            if i < 2:
                grad = far[slot, 0, at, :].astype(F32) + far[slot, 1, at, :].astype(F32)
            elif i == 2:
                width = feat // (CHUNKS - 1)
                grad = jnp.concatenate(
                    [dense_ref[g, at, right * width : (right + 1) * width] for g in range(1, CHUNKS)], axis=1
                ).astype(F32)
            else:
                grad = dense_ref[0, at, :].astype(F32)
            new = adam_rows(*(state[slot, n, at, :] for n in range(3)), grad * clip, RATE_MATRIX, DECAY)
            for n in range(3):
                state[slot, n, at, :] = new[n]
            return carry

        lax.fori_loop(0, tall // unit, rows, 0)
        each(stores(t), "start")
        if t + SLOTS - 1 < len(pieces):
            if t >= 1:
                each(stores(t - 1), "wait")
            each(loads(t + SLOTS - 1), "start")
    for t in range(len(pieces) - SLOTS, len(pieces)):
        each(stores(t), "wait")


def run_adam(exps, norm, small, dense, router, vector, far, states):
    vmem, hbm = pl.BlockSpec(memory_space=pltpu.VMEM), pl.BlockSpec(memory_space=pl.ANY)
    dma = pltpu.SemaphoreType.DMA
    tall, feat = dense.shape[1:]
    pieces = [
        (i, down, right)
        for i, group in enumerate(states)
        for down in range(group[0].shape[0] // tall)
        for right in range(group[0].shape[1] // feat)
    ]
    flat_states = [a for group in states for a in group]
    args = [norm, small, dense, *router, *vector, *far, *flat_states]
    return pl.pallas_call(
        functools.partial(adam_kernel, exps=exps, pieces=pieces),
        out_shape=[shape((1, 1), F32)] + [shape(a.shape, F32) for a in (*router, *vector, *flat_states)],
        in_specs=[vmem] * 9 + [hbm] * 16,
        out_specs=[vmem] * 7 + [hbm] * 12,
        scratch_shapes=[
            pltpu.VMEM((SLOTS, 2, tall, feat), BF),
            pltpu.VMEM((SLOTS, 3, tall, feat), F32),
            dma((SLOTS, 2)), dma((SLOTS, 3)), dma((SLOTS, 3)),
        ],
        compiler_params=pltpu.CompilerParams(vmem_limit_bytes=60 * 1024 * 1024),
        cost_estimate=pl.CostEstimate(flops=100_000_000, bytes_accessed=100_000_000, transcendentals=0),
    )(*args)


def adam_step(weight, first, second, grad, rate, decay):
    new_first = BETA_ONE * first + (1.0 - BETA_ONE) * grad
    new_second = BETA_TWO * second + (1.0 - BETA_TWO) * grad * grad
    first_hat = new_first / (1.0 - BETA_ONE**STEP)
    second_hat = new_second / (1.0 - BETA_TWO**STEP)
    new_weight = weight - rate * (first_hat / (jnp.sqrt(second_hat) + ADAM_EPS) + decay * weight)
    return (new_weight, new_first, new_second)


def body(
    images,
    cotangent,
    routes,
    priority,
    qkv_weight,
    qkv_first,
    qkv_second,
    proj_weight,
    proj_first,
    proj_second,
    router_weight,
    router_first,
    router_second,
    norm_params,
    norm_first,
    norm_second,
    inner_weight,
    inner_first,
    inner_second,
    outer_weight,
    outer_first,
    outer_second,
):
    exps = lax.axis_size("expert")
    shards = lax.axis_size("dp")
    imgs, seq, feat = images.shape
    tok = imgs * seq
    cap = (18 * tok + 8 * exps - 1) // (8 * exps)
    cp = up(cap + 1, 8)
    sp = up(seq, 16)
    nt = up(imgs * sp, BLOCK)
    rows = exps * cp
    at_dp, at_exp = lax.axis_index("dp"), lax.axis_index("expert")
    shard_rows = qkv_weight.shape[0]
    by_kernel = shards == 2 and exps == 4 * DEEP

    qkv_in, proj_in = qkv_weight, proj_weight
    small = jnp.concatenate([router_weight.astype(BF).T, norm_params.astype(BF)], axis=0)
    small = jnp.pad(small, ((0, up(exps + 4, 16) - exps - 4), (0, 0)))
    if not by_kernel:
        qkv_in = lax.all_gather(qkv_weight.astype(BF), "dp", axis=0, tiled=True)
        proj_in = lax.all_gather(proj_weight.astype(BF), "dp", axis=0, tiled=True)
        small = lax.all_gather(small, "dp", axis=1, tiled=True)
    picks = jnp.pad(routes.transpose(2, 0, 1), ((0, 0), (0, 0), (0, sp - seq)), constant_values=-1)
    picks = jnp.pad(picks.reshape(2, imgs * sp), ((0, 0), (0, nt - imgs * sp)), constant_values=-1)
    order = priority[0] + (priority[0] // seq) * (sp - seq)
    order = jnp.pad(order, (0, nt - tok), constant_values=-1)
    w_full, small, h1, mixed, context, after, h2, router, gates, place, gates_col, place_col, x, cot, recv, recv_cot, *others = (
        run_front(
        images, cotangent, picks, order[None, :], small, qkv_in, proj_in,
        (inner_weight[0], outer_weight[0]) if by_kernel else None,
        nt=nt, sp=sp, cap=cap, cp=cp, exps=exps,
    ))
    if by_kernel:
        own, far = tuple(others[:2]), tuple(others[2:])
    else:
        own, far = (
            lax.all_gather(inner_weight[0].astype(BF), "dp", axis=1, tiled=True),
            lax.all_gather(outer_weight[0].astype(BF), "dp", axis=0, tiled=True),
        ), None

    back_grad, result, own_inner, own_outer, *rest = run_expert(recv, recv_cot, own, far, cap, cp, exps)
    if by_kernel:
        far_outer, sent_inner = rest
    else:
        back_grad = lax.all_to_all(back_grad, "expert", split_axis=0, concat_axis=0, tiled=True)
        shard_inner = lax.psum_scatter(own_inner, "dp", scatter_dimension=1, tiled=True).astype(F32)[None]
        shard_outer = lax.psum_scatter(own_outer, "dp", scatter_dimension=0, tiled=True).astype(F32)[None]

    if not by_kernel:
        result = lax.all_to_all(result, "expert", split_axis=0, concat_axis=0, tiled=True)
    dense_grad, small_grad, input_grad, output, *sent = run_back(
        by_kernel, imgs, seq, sp, cap, cp, exps,
        back_grad, place_col, place, picks, gates, gates_col, router, h2, after, cot, small, w_full,
        mixed, h1, context, x, result, *((far_outer,) if by_kernel else ()),
    )

    if by_kernel:
        far = (own_inner, sent_inner, own_outer, *sent)
        norm = run_total(shards, exps, small_grad, dense_grad, *far)
        small_half = lax.dynamic_slice_in_dim(small_grad, at_dp * shard_rows, shard_rows, 1)
        norm, *new = run_adam(
            exps, norm, small_half, dense_grad,
            (router_weight.T, router_first.T, router_second.T),
            (norm_params, norm_first, norm_second),
            far,
            (
                (inner_weight[0], inner_first[0], inner_second[0]),
                (outer_weight[0], outer_first[0], outer_second[0]),
                (qkv_weight, qkv_first, qkv_second),
                (proj_weight, proj_first, proj_second),
            ),
        )
        router_new, norm_new, inner_new, outer_new, qkv_new, proj_new = (new[3 * i : 3 * i + 3] for i in range(6))
        return (
            output,
            input_grad,
            norm[0, 0],
            *qkv_new,
            *proj_new,
            *(a.T for a in router_new),
            *norm_new,
            *(a[None] for a in inner_new),
            *(a[None] for a in outer_new),
        )

    dense_grad = lax.psum(dense_grad, ("dp", "expert"))
    small_grad = lax.psum(small_grad, ("dp", "expert"))
    width = feat // (CHUNKS - 1)
    dense_grad = lax.dynamic_slice_in_dim(dense_grad, at_dp * shard_rows, shard_rows, 1).astype(F32)
    shard_small = lax.dynamic_slice_in_dim(small_grad, at_dp * shard_rows, shard_rows, 1)
    shard_qkv = jnp.concatenate(
        [dense_grad[g, :, n * width : (n + 1) * width] for n in range(3) for g in range(1, CHUNKS)], axis=1
    )
    shard_proj = dense_grad[0]
    shard_router, shard_vector = shard_small[:exps].T, shard_small[exps : exps + 4]
    dense_squares = jnp.sum(dense_grad * dense_grad) + jnp.sum(shard_small * shard_small)
    expert_squares = jnp.sum(shard_inner * shard_inner) + jnp.sum(shard_outer * shard_outer)
    local_squares = expert_squares + jnp.where(at_exp == 0, dense_squares, jnp.float32(0.0))
    grad_norm = jnp.sqrt(lax.psum(local_squares, ("dp", "expert")))
    clip = CLIP_NORM / jnp.maximum(grad_norm, CLIP_NORM)
    qkv_new = adam_step(qkv_weight, qkv_first, qkv_second, shard_qkv * clip, RATE_MATRIX, DECAY)
    proj_new = adam_step(proj_weight, proj_first, proj_second, shard_proj * clip, RATE_MATRIX, DECAY)
    router_new = adam_step(
        router_weight, router_first, router_second, shard_router * clip, RATE_MATRIX, DECAY
    )
    norm_new = adam_step(norm_params, norm_first, norm_second, shard_vector * clip, RATE_VECTOR, 0.0)
    inner_new = adam_step(
        inner_weight, inner_first, inner_second, shard_inner * clip, RATE_MATRIX, DECAY
    )
    outer_new = adam_step(
        outer_weight, outer_first, outer_second, shard_outer * clip, RATE_MATRIX, DECAY
    )
    return (
        output,
        input_grad,
        grad_norm,
        *qkv_new,
        *proj_new,
        *router_new,
        *norm_new,
        *inner_new,
        *outer_new,
    )


def solution(mesh):
    tokens = P(("dp", "expert"), None, None)
    dense = P("dp", None)
    vector = P(None, "dp")
    inner = P("expert", None, "dp")
    outer = P("expert", "dp", None)
    return jax.shard_map(
        body,
        mesh=mesh,
        in_specs=(tokens, tokens, tokens, P(("dp", "expert"), None))
        + (dense,) * 9
        + (vector,) * 3
        + (inner,) * 3
        + (outer,) * 3,
        out_specs=(tokens, tokens, P())
        + (dense,) * 9
        + (vector,) * 3
        + (inner,) * 3
        + (outer,) * 3,
        check_vma=False,
    )
```

```python
import functools

import jax
import jax.numpy as jnp
from jax import lax
from jax.experimental import pallas as pl
from jax.experimental.pallas import tpu as pltpu
from jax.sharding import PartitionSpec as P

HEADS = 12
HDIM = 64
STEP = 10
SCALE = float(HDIM) ** (-0.5)

LN_EPS = 1e-06
BETA_ONE = 0.9
BETA_TWO = 0.999
ADAM_EPS = 1e-08
RATE_MATRIX = 0.06
RATE_VECTOR = 0.4
DECAY = 0.1
CLIP_NORM = 1.0

BF = jnp.bfloat16
F32 = jnp.float32
I32 = jnp.int32
NEG = -1e30
BLOCK = 128
BIG = 320
TILE = 512
EARLY = 2
CHUNKS = 4
DEEP = 4
VMEM_CAP = 60 * 1024 * 1024

LOG2_E = 1.4426950408889634
SQRT_HALF = 0.7071067811865476
INV_SQRT_TAU = 0.3989422804014327


def up(value, step):
    return -(-value // step) * step


def dot(left, right):
    return lax.dot_general(left, right, (((1,), (0,)), ((), ())), preferred_element_type=F32)


def dot_nt(left, right):
    return lax.dot_general(left, right, (((1,), (1,)), ((), ())), preferred_element_type=F32)


def dot_tn(left, right):
    return lax.dot_general(left, right, (((0,), (0,)), ((), ())), preferred_element_type=F32)


def iota(shape, axis):
    return lax.broadcasted_iota(I32, shape, axis)


def hot(mask):
    return jnp.where(mask, 1.0, 0.0).astype(BF)


def normed_of(values):
    centre = jnp.mean(values, axis=-1, keepdims=True)
    centered = values - centre
    rstd = lax.rsqrt(jnp.mean(centered * centered, axis=-1, keepdims=True) + LN_EPS)
    return centered * rstd, rstd


def norm_back_rows(grad, normed, rstd, gain):
    scaled = grad * gain
    inner_mean = jnp.mean(scaled, axis=-1, keepdims=True)
    cross_mean = jnp.mean(scaled * normed, axis=-1, keepdims=True)
    return rstd * (scaled - inner_mean - normed * cross_mean)


def split3(values):
    high = values.astype(BF)
    rest = values - high.astype(F32)
    mid = rest.astype(BF)
    low = (rest - mid.astype(F32)).astype(BF)
    return high, mid, low


def call(kernel, out_shape, *args, scratch=(), specs=None, flops=0, moved=0):
    vmem = pl.BlockSpec(memory_space=pltpu.VMEM)
    single = not isinstance(out_shape, (tuple, list))
    return pl.pallas_call(
        kernel,
        out_shape=out_shape,
        in_specs=[vmem] * len(args) if specs is None else specs,
        out_specs=vmem if single else [vmem] * len(out_shape),
        scratch_shapes=list(scratch),
        compiler_params=pltpu.CompilerParams(vmem_limit_bytes=VMEM_CAP),
        cost_estimate=pl.CostEstimate(flops=int(flops), bytes_accessed=int(moved), transcendentals=0),
    )(*args)


def shape(dims, kind):
    return jax.ShapeDtypeStruct(dims, kind)


MESH = pl.DeviceIdType.MESH


def remote(source, target, send, recv, device):
    return pltpu.make_async_remote_copy(
        src_ref=source, dst_ref=target, send_sem=send, recv_sem=recv, device_id=device, device_id_type=MESH
    )


def rows_at(start, size, unit=16):
    return pl.ds(pl.multiple_of(start, unit), size)


class Exchange:
    def __init__(self, send, recv, send_sem, recv_sem, local_sem, exps):
        self.send, self.recv, self.send_sem, self.recv_sem, self.local_sem = send, recv, send_sem, recv_sem, local_sem
        self.chips = exps // 2
        self.at_dp, self.me = lax.axis_index("dp"), lax.axis_index("expert")
        self.core, self.chip = self.me % 2, self.me // 2

    def out(self, r, j):
        there = ((self.chip + r) % self.chips) * 2 + j
        return remote(
            self.send.at[there], self.recv.at[self.me],
            self.send_sem.at[2 * r + j], self.recv_sem.at[2 * r + self.core], (self.at_dp, there),
        )

    def back(self, r, j):
        there = ((self.chip + self.chips - r) % self.chips) * 2 + j
        return remote(
            self.send.at[self.me], self.recv.at[there],
            self.send_sem.at[2 * r + j], self.recv_sem.at[2 * r + j], (self.at_dp, there),
        )

    def own(self):
        return pltpu.make_async_copy(self.send.at[self.me], self.recv.at[self.me], self.local_sem)

    def start(self, r):
        @pl.when(r == 0)
        def _():
            self.out(0, 1 - self.core).start()
            self.own().start()

        @pl.when(r > 0)
        def _():
            self.out(r, 0).start()
            self.out(r, 1).start()

    def finish(self):
        self.own().wait()
        self.out(0, 1 - self.core).wait_send()
        self.back(0, 1 - self.core).wait_recv()

        def step(r, carry):
            for j in range(2):
                self.out(r, j).wait_send()
                self.back(r, j).wait_recv()
            return carry

        lax.fori_loop(1, self.chips, step, 0)


def front_kernel(*refs, pair, imgs, seq, sp, nt, cap, cp, exps):
    refs = list(refs)

    def take(count):
        taken = refs[:count]
        del refs[:count]
        return taken

    images_ref, cot_in_ref, picks_ref, order_ref, small_ref, qkv_in, proj_in = take(7)
    if pair:
        experts_in = take(2)
    w_ref, small_out, h1_ref, mixed_ref, ctx_ref, after_ref, h2_ref, router_out, gates_ref, place_out = take(10)
    gates_col, place_col = take(2)
    x_ref, cot_ref, recv_ref, recv_cot_ref = take(4)
    if pair:
        experts_own, experts_far = take(2), take(2)
    send_ref, send_cot_ref, pad_ref, qkv_ref, proj_ref, dense_sem = take(6)
    if pair:
        small_all = take(1)[0]
        staged, experts = take(2), take(2)
    cot_ssem, cot_rsem, row_ssem, row_rsem, local_sem = take(5)
    if pair:
        weight_ssem, weight_rsem, side_ssem, side_rsem, stage_sem, own_sem = take(6)
    feat = images_ref.shape[-1]
    at_dp, me = lax.axis_index("dp"), lax.axis_index("expert")
    core, chip = me % 2, me // 2
    chips = exps // 2
    shard = qkv_ref.shape[0]
    half = shard // 2
    groups = CHUNKS - 1
    pairs = feat // 128
    per = pairs // groups

    if pair:
        loads = [pltpu.make_async_copy(experts_in[i], staged[i], stage_sem.at[i]) for i in range(2)]
        for made in loads:
            made.start()
    dense_loads = [
        pltpu.make_async_copy(qkv_in, qkv_ref, dense_sem.at[0]), pltpu.make_async_copy(proj_in, proj_ref, dense_sem.at[1])
    ]
    for made in dense_loads:
        made.start()
    barrier = pltpu.get_barrier_semaphore()

    def greet(r, carry):
        pl.semaphore_signal(
            barrier, inc=1, device_id=(at_dp, (me + r) % exps), device_id_type=MESH
        )
        return carry

    lax.fori_loop(1, exps, greet, 0)
    if pair:
        pl.semaphore_signal(barrier, inc=1, device_id=(1 - at_dp, me), device_id_type=MESH)
    width = per * 128
    own_rows = rows_at(at_dp * shard if pair else 0, shard)
    for made in dense_loads:
        made.wait()
    for g in range(groups):
        for n in range(3):
            w_ref[own_rows, g * feat + n * width : g * feat + (n + 1) * width] = qkv_ref[
                :, n * feat + g * width : n * feat + (g + 1) * width
            ].astype(BF)
    w_ref[own_rows, 3 * feat : 4 * feat] = proj_ref[...].astype(BF)
    pl.semaphore_wait(barrier, exps - 1 + int(pair))

    if pair:
        other_dp, other_core = (1 - at_dp, me), (at_dp, chip * 2 + 1 - core)
        small_copy = remote(
            small_ref, small_all.at[at_dp], weight_ssem.at[0], weight_rsem.at[0], other_dp
        )
        small_copy.start()

        deep, side = chip // 2, chip % 2
        wide = feat // 2
        far_base = (1 - at_dp) * shard

        def same_place(start, size, g, send, recv, device):
            place = w_ref.at[rows_at(start, size), rows_at(g * feat + core * wide, wide, 128)]
            return remote(place, place, send, recv, device)

        def dense_copy(g):
            return same_place(at_dp * shard + side * half, half, g, weight_ssem.at[1 + g], weight_rsem.at[1 + g], other_dp)

        def side_copy(g):
            device = (at_dp, (deep * 2 + 1 - side) * 2 + core)
            return same_place(far_base + side * half, half, g, side_ssem.at[g], side_rsem.at[g], device)

        def swap_copy(g):
            return same_place(far_base, shard, g, weight_ssem.at[5 + g], weight_rsem.at[5 + g], other_core)

        for g in range(CHUNKS):
            dense_copy(g).start()
        far_copies = [
            remote(
                experts[i].at[0 : experts_far[i].shape[0], :], experts_far[i],
                weight_ssem.at[9 + i], weight_rsem.at[9 + i], other_dp,
            )
            for i in range(2)
        ]
        own_copies = [pltpu.make_async_copy(experts[i], experts_own[i], own_sem.at[i]) for i in range(2)]
    for ref, source in ((x_ref, images_ref), (cot_ref, cot_in_ref)):
        ref[...] = jnp.zeros(ref.shape, BF)
        for i in range(imgs):
            ref[i * sp : i * sp + seq, :] = source[i]
    first, second = picks_ref[0:1, :], picks_ref[1:2, :]
    sub, lane = iota((nt, nt), 0), iota((nt, nt), 1)
    order_row = order_ref[...]
    order_col = jnp.broadcast_to(order_row.astype(F32), (8, nt)).T[:, 0:1].astype(I32)
    pos_row = jnp.sum(jnp.where(order_col == lane, sub.astype(F32), 0.0), axis=0, keepdims=True)
    pos_col = jnp.sum(jnp.where(order_row == sub, lane.astype(F32), 0.0), axis=1, keepdims=True)
    earlier = hot(pos_col < pos_row)
    exp_id = iota((exps, nt), 0)
    hot0 = jnp.where(exp_id == first, 1.0, 0.0)
    hot1 = jnp.where(exp_id == second, 1.0, 0.0)
    before0 = dot(hot0.astype(BF), earlier)
    before1 = dot(hot1.astype(BF), earlier) + jnp.sum(hot0, axis=1, keepdims=True)
    slot0 = jnp.sum(hot0 * before0, axis=0, keepdims=True).astype(I32)
    slot1 = jnp.sum(hot1 * before1, axis=0, keepdims=True).astype(I32)
    ok0, ok1 = (slot0 < cap) & (first >= 0), (slot1 < cap) & (second >= 0)
    place0, place1 = jnp.where(ok0, first * cp + slot0, -1), jnp.where(ok1, second * cp + slot1, -1)
    place_out[0:1, :] = place0
    place_out[1:2, :] = place1
    place_out[2:8, :] = jnp.full((6, nt), -1, I32)
    place_col[...] = place_out[...].astype(F32).T.astype(I32)

    cot_rows = Exchange(send_cot_ref, recv_cot_ref, cot_ssem, cot_rsem, local_sem.at[0], exps)

    def cot_chunk(r, carry):
        there = (chip + r) % chips
        row = iota((2 * cp, nt), 0) + there * (2 * cp)
        pick = hot((row == place0) | (row == place1))
        rows = dot(pick, cot_ref[...])
        for j in range(2):
            send_cot_ref[there * 2 + j] = rows[j * cp : (j + 1) * cp].astype(BF)
        cot_rows.start(r)
        return carry

    lax.fori_loop(0, chips, cot_chunk, 0)

    if pair:
        for i in range(2):
            loads[i].wait()
            unit = 64

            def narrow(n, carry, i=i, unit=unit):
                at = rows_at(n * unit, unit)
                experts[i][at, :] = staged[i][at, :].astype(BF)
                return carry

            lax.fori_loop(0, staged[i].shape[0] // unit, narrow, 0)
            far_copies[i].start()
            own_copies[i].start()

    if pair:
        small_all[at_dp] = small_ref[...]
        small_copy.wait_recv()
        small = jnp.concatenate([small_all[0], small_all[1]], axis=1)
    else:
        small = small_ref[...]
    small_out[...] = small
    norm = small[exps : exps + 4].astype(F32)
    router_w = small[:exps]

    def first_norm(i, carry):
        at = rows_at(i * BLOCK, BLOCK, BLOCK)
        normed, _ = normed_of(x_ref[at, :].astype(F32))
        h1_ref[at, :] = (normed * norm[0:1] + norm[1:2]).astype(BF)
        return carry

    lax.fori_loop(0, nt // BLOCK, first_norm, 0)

    key_ok = iota((sp, sp), 1) < seq
    left = iota((sp, 128), 1) < HDIM

    def attend(group, i):
        rows = slice(i * sp, (i + 1) * sp)
        for p in range(per):
            cols = [group * feat + n * width + p * 128 for n in range(3)]
            query, keys, values = (mixed_ref[rows, c : c + 128] for c in cols)
            outs = []
            for mask in (left, ~left):
                scores = dot_nt(jnp.where(mask, query, jnp.zeros_like(query)), keys) * SCALE
                scores = jnp.where(key_ok, scores, NEG)
                top = jnp.max(scores, axis=-1, keepdims=True)
                grown = jnp.exp(scores - top)
                probs = grown / jnp.sum(grown, axis=-1, keepdims=True)
                outs.append(dot(probs.astype(BF), values))
            col = (group * per + p) * 128
            ctx_ref[rows, col : col + 128] = jnp.where(left, outs[0], outs[1]).astype(BF)

    ctx_ref[imgs * sp : nt, :] = jnp.zeros((nt - imgs * sp, feat), BF)
    if pair:
        dense_copy(0).wait_recv()
        side_copy(0).start()
        dense_copy(1).wait_recv()
        side_copy(1).start()
        side_copy(0).wait_recv()
        swap_copy(0).start()
        swap_copy(0).wait_recv()
    for group in range(groups):
        for n in range(2):
            at = slice(group * feat + n * (feat // 2), group * feat + (n + 1) * (feat // 2))
            mixed_ref[:, at] = dot(h1_ref[...], w_ref[:, at]).astype(BF)
        for i in range(imgs):
            if pair and i == 0 and group + 2 < CHUNKS:
                dense_copy(group + 2).wait_recv()
                side_copy(group + 2).start()
            if pair and i == imgs - 1:
                side_copy(group + 1).wait_recv()
                swap_copy(group + 1).start()
            attend(group, i)
        if pair:
            swap_copy(group + 1).wait_recv()

    def second_norm(i, carry):
        at = rows_at(i * BIG, BIG)
        after = x_ref[at, :].astype(F32) + dot(ctx_ref[at, :], w_ref[:, 3 * feat : 4 * feat])
        after_ref[at, :] = after
        normed, _ = normed_of(after)
        h2_ref[at, :] = (normed * norm[2:3] + norm[3:4]).astype(BF)
        return carry

    lax.fori_loop(0, nt // BIG, second_norm, 0)

    h2 = h2_ref[...]
    logits = dot_nt(router_w, h2)
    grown = jnp.exp(logits - jnp.max(logits, axis=0, keepdims=True))
    router = grown / jnp.sum(grown, axis=0, keepdims=True)
    router_out[...] = router
    chosen0 = jnp.sum(jnp.where(exp_id == first, router, 0.0), axis=0, keepdims=True)
    chosen1 = jnp.sum(jnp.where(exp_id == second, router, 0.0), axis=0, keepdims=True)
    total = chosen0 + chosen1
    total = jnp.where(total > 0.0, total, 1.0)
    gate0, gate1 = chosen0 / total, chosen1 / total
    for i, row in enumerate((chosen0, chosen1, gate0, gate1)):
        gates_ref[i : i + 1, :] = row
    gates_ref[4:8, :] = jnp.zeros((4, nt), F32)
    gates_col[...] = gates_ref[...].T

    zero_rows = jnp.zeros((5, nt), F32)
    parts0 = jnp.concatenate([v.astype(F32) for v in split3(gate0)] + [zero_rows], axis=0).astype(BF)
    parts1 = jnp.concatenate([v.astype(F32) for v in split3(gate1)] + [zero_rows], axis=0).astype(BF)
    pad_ref[...] = jnp.zeros(pad_ref.shape, F32)
    token_rows = Exchange(send_ref, recv_ref, row_ssem, row_rsem, local_sem.at[1], exps)

    def row_chunk(r, carry):
        there = (chip + r) % chips
        row = iota((2 * cp, nt), 0) + there * (2 * cp)
        pick0, pick1 = hot(row == place0), hot(row == place1)
        rows = dot(pick0 + pick1, h2_ref[...])
        spread = dot_nt(parts0, pick0) + dot_nt(parts1, pick1)
        line = iota((cp, feat), 0)
        for j in range(2):
            for k in range(3):
                pad_ref[j : j + 1, k * 128 : k * 128 + cp] = spread[k : k + 1, j * cp : (j + 1) * cp]
            mine = rows[j * cp : (j + 1) * cp] + jnp.where(line == cap, pad_ref[j : j + 1, :], 0.0)
            send_ref[there * 2 + j] = mine.astype(BF)
        token_rows.start(r)
        return carry

    lax.fori_loop(0, chips, row_chunk, 0)

    if pair:
        small_copy.wait_send()
        for g in range(CHUNKS):
            dense_copy(g).wait_send()
            side_copy(g).wait_send()
            swap_copy(g).wait_send()
        for i in range(2):
            far_copies[i].wait()
            own_copies[i].wait()
    cot_rows.finish()
    token_rows.finish()


def run_front(images, cot, picks, order, small, qkv, proj, weights, *, nt, sp, cap, cp, exps):
    imgs, seq, feat = images.shape
    pair = weights is not None
    vmem, hbm = pl.BlockSpec(memory_space=pltpu.VMEM), pl.BlockSpec(memory_space=pl.ANY)
    dma = pltpu.SemaphoreType.DMA
    slabs = (exps, cp, feat)
    outs = [
        shape((feat, 4 * feat), BF),
        shape((small.shape[0], feat), BF),
        shape((nt, feat), BF),
        shape((nt, 3 * feat), BF),
        shape((nt, feat), BF),
        shape((nt, feat), F32),
        shape((nt, feat), BF),
        shape((exps, nt), F32),
        shape((8, nt), F32),
        shape((8, nt), I32),
        shape((nt, 8), F32),
        shape((nt, 8), I32),
        shape((nt, feat), BF),
        shape((nt, feat), BF),
        shape(slabs, BF),
        shape(slabs, BF),
    ]
    ins = [images, cot, picks, order, small, qkv, proj]
    scratch = [pltpu.VMEM(slabs, BF), pltpu.VMEM(slabs, BF), pltpu.VMEM((8, feat), F32)]
    scratch += [pltpu.VMEM(qkv.shape, qkv.dtype), pltpu.VMEM(proj.shape, proj.dtype), dma((2,))]
    if pair:
        ins += list(weights)
        outs += [shape(w.shape, BF) for w in weights]
        outs += [shape(weights[0].shape, BF), shape((EARLY * TILE, feat), BF)]
        scratch += [pltpu.VMEM((2,) + small.shape, BF)]
        scratch += [pltpu.VMEM(w.shape, F32) for w in weights] + [pltpu.VMEM(w.shape, BF) for w in weights]
    scratch += [dma((exps,)), dma((exps,)), dma((exps,)), dma((exps,)), dma((2,))]
    if pair:
        scratch += [dma((11,)), dma((11,)), dma((CHUNKS,)), dma((CHUNKS,)), dma((2,)), dma((2,))]
    return pl.pallas_call(
        functools.partial(front_kernel, pair=pair, imgs=imgs, seq=seq, sp=sp, nt=nt, cap=cap, cp=cp, exps=exps),
        out_shape=outs,
        in_specs=[vmem] * 5 + [hbm] * (len(ins) - 5),
        out_specs=[vmem] * 14 + [hbm] * (len(outs) - 14),
        scratch_shapes=scratch,
        compiler_params=pltpu.CompilerParams(
            vmem_limit_bytes=VMEM_CAP, collective_id=3, has_side_effects=True
        ),
        cost_estimate=pl.CostEstimate(flops=20_000_000_000, bytes_accessed=60_000_000, transcendentals=0),
    )(*ins)


def gelu_both(hidden):
    bell = jnp.exp2(hidden * hidden * (-0.5 * LOG2_E))
    below = 0.5 + 0.5 * lax.erf(hidden * SQRT_HALF)
    return hidden * below, below + hidden * (bell * INV_SQRT_TAU)


def expert_kernel(*refs, pair, mine, cap, cp, exps, block):
    refs = list(refs)

    def take(count):
        taken = refs[:count]
        del refs[:count]
        return taken

    recv_in, dfin_in, inner_ref, outer_ref = take(4)
    if pair:
        inner_far, outer_far, outer_all = take(3)
    back_out, result_out, own_inner, own_outer = take(4)
    if pair:
        far_outer, sent_inner = take(2)
    recv_ref, dfin_ref, rows_ref, dres_ref, rows_t, dres_t, sum_r, sum_d, wi_ref, wo_ref, act_ref, dhid_ref = take(12)
    slab_sem = take(1)[0]
    if pair:
        landed, far_inner, back_ssem, back_rsem, outer_ssem, outer_rsem, inner_ssem, inner_rsem = take(8)
    j = pl.program_id(0)
    rows, feat = rows_ref.shape
    two = 2 * cp
    sub = iota((two, 128), 0)
    lane = iota((two, 128), 1)
    upper = sub < cp
    diag = lane == jnp.where(upper, sub, sub - cp)
    count = 2 * mine if pair else mine
    tile = wi_ref.shape[1]

    if pair:
        at_dp, me = lax.axis_index("dp"), lax.axis_index("expert")
        other_dp = (1 - at_dp, me)
        outer_copies = [
            remote(
                outer_all.at[t * tile : (t + 1) * tile, :], landed.at[t - EARLY],
                outer_ssem.at[t - EARLY], outer_rsem.at[t - EARLY], other_dp,
            )
            for t in range(EARLY, mine)
        ]
        inner_copies = [
            remote(
                far_inner.at[t], sent_inner.at[:, t * tile : (t + 1) * tile], inner_ssem.at[t], inner_rsem.at[t], other_dp
            )
            for t in range(mine)
        ]
        drows_out = Exchange(recv_ref, back_out, back_ssem, back_rsem, slab_sem.at[2], exps)
    else:
        drows_out = pltpu.make_async_copy(recv_ref, back_out, slab_sem.at[2])
    result_copy = pltpu.make_async_copy(dfin_ref, result_out, slab_sem.at[3])

    @pl.when(j == 0)
    def _():
        slabs = [
            pltpu.make_async_copy(recv_in, recv_ref, slab_sem.at[0]),
            pltpu.make_async_copy(dfin_in, dfin_ref, slab_sem.at[1]),
        ]
        for made in slabs:
            made.start()
        if pair:
            barrier = pltpu.get_barrier_semaphore()

            def greet(r, carry):
                pl.semaphore_signal(barrier, inc=1, device_id=(at_dp, (me + r) % exps), device_id_type=MESH)
                return carry

            lax.fori_loop(1, exps, greet, 0)
            pl.semaphore_signal(barrier, inc=1, device_id=other_dp, device_id_type=MESH)
            pl.semaphore_wait(barrier, exps)
            for made in outer_copies:
                made.start()
        sum_r[...] = jnp.zeros_like(sum_r)
        sum_d[...] = jnp.zeros_like(sum_d)
        for made in slabs:
            made.wait()

        def gate_rows(i, carry):
            at = rows_at(i * two, two)

            def both_of(ref):
                return jnp.concatenate([ref[2 * i].astype(F32), ref[2 * i + 1].astype(F32)], axis=0)

            recv, dfin = both_of(recv_ref), both_of(dfin_ref)
            rows_ref[at, :] = recv.astype(BF)
            lead = recv[:, 0:384]
            place = iota((two, 384), 0)
            spread = []
            for k in range(2):
                row = jnp.sum(jnp.where(place == k * cp + cap, lead, 0.0), axis=0, keepdims=True)
                spread.append(row[:, 0:128] + row[:, 128:256] + row[:, 256:384])
            both = jnp.where(upper, spread[0], spread[1])
            gate = jnp.sum(jnp.where(diag, both, 0.0), axis=1, keepdims=True)
            dres_ref[at, :] = (gate * dfin).astype(BF)
            return carry

        lax.fori_loop(0, exps // 2, gate_rows, 0)

    @pl.when(j < mine)
    def _():
        wi_ref[...] = inner_ref[...]
        wo_ref[...] = outer_ref[...]

    if pair:

        @pl.when((j >= mine) & (j < count))
        def _():
            wi_ref[...] = inner_far[...]

        @pl.when((j >= mine) & (j < mine + EARLY))
        def _():
            wo_ref[...] = outer_far[...]

        for t in range(EARLY, mine):

            @pl.when(j == mine + t)
            def _(t=t):
                outer_copies[t - EARLY].wait()
                wo_ref[...] = landed[t - EARLY]

    @pl.when(j < count)
    def _():
        for i in range(rows // block):
            at = pl.ds(i * block, block)
            hidden = dot(rows_ref[at, :], wi_ref[...])
            act, slope = gelu_both(hidden)
            act = act.astype(BF)
            dact = dot_nt(dres_ref[at, :], wo_ref[...])
            dhid = (slope * dact).astype(BF)
            act_ref[j, at, :] = act
            dhid_ref[j, at, :] = dhid
            sum_r[at, :] += dot(act, wo_ref[...])
            sum_d[at, :] += dot_nt(dhid, wi_ref[...])

    @pl.when(j == count - 1)
    def _():
        def finish(i, carry):
            at = rows_at(i * two, two)
            dfin = jnp.concatenate([dfin_ref[2 * i].astype(F32), dfin_ref[2 * i + 1].astype(F32)], axis=0)
            result = sum_r[at, :].astype(BF).astype(F32)
            dgate = jnp.sum(result * dfin, axis=1, keepdims=True)
            line = iota((two, feat), 0)
            drows = sum_d[at, :]
            for k in range(2):
                chosen = upper if k == 0 else ~upper
                row = jnp.sum(jnp.where(diag & chosen, dgate, 0.0), axis=0, keepdims=True)
                wide = jnp.concatenate(
                    [v.astype(F32) for v in split3(row)] + [jnp.zeros((1, feat - 384), F32)], axis=1
                )
                drows = drows + jnp.where(line == k * cp + cap, wide, 0.0)
            for k in range(2):
                recv_ref[2 * i + k] = drows[k * cp : (k + 1) * cp].astype(BF)
                dfin_ref[2 * i + k] = result[k * cp : (k + 1) * cp].astype(BF)
            return carry

        lax.fori_loop(0, exps // 2, finish, 0)
        if pair:

            def drows_go(r, carry):
                drows_out.start(r)
                return carry

            lax.fori_loop(0, exps // 2, drows_go, 0)
        else:
            drows_out.start()
        result_copy.start()
        rows_t[...] = rows_ref[...].T
        dres_t[...] = dres_ref[...].T

    def grads_of(n):
        inner = dot(rows_t[...], dhid_ref[n]).astype(BF)
        outer = dot(dres_t[...], act_ref[n]).astype(BF).T
        return inner, outer

    if pair:

        @pl.when((j >= count) & (j < count + mine))
        def _():
            inner, outer = grads_of(j - count + mine)
            far_inner[j - count] = inner
            far_outer[...] = outer

        for t in range(mine):

            @pl.when(j == count + t)
            def _(t=t):
                inner_copies[t].start()

    @pl.when(j >= 2 * count - mine)
    def _():
        inner, outer = grads_of(j - (2 * count - mine))
        own_inner[...] = inner
        own_outer[...] = outer

    @pl.when(j == 2 * count - 1)
    def _():
        result_copy.wait()
        if pair:
            drows_out.finish()
            for made in inner_copies:
                made.wait()
        else:
            drows_out.wait()


def run_expert(recv, dfin, own, far, cap, cp, exps):
    slabs = recv.shape
    feat = slabs[-1]
    rows = exps * cp
    inner, outer = own
    tile = min(TILE, inner.shape[1])
    mine = inner.shape[1] // tile
    pair = far is not None
    count = 2 * mine if pair else mine
    start = 2 * count - mine
    hbm = pl.BlockSpec(memory_space=pl.ANY)
    dma = pltpu.SemaphoreType.DMA

    def across(first, size=mine):
        return pl.BlockSpec((feat, tile), lambda j: (0, jnp.clip(j - first, 0, size - 1)))

    def down(first, size=mine):
        return pl.BlockSpec((tile, feat), lambda j: (jnp.clip(j - first, 0, size - 1), 0))

    in_specs = [hbm, hbm, across(0), down(0)]
    args = [recv, dfin, inner, outer]
    out_specs = [hbm, hbm, across(start), down(start)]
    out_shape = [shape(slabs, BF), shape(slabs, BF), shape(inner.shape, BF), shape(outer.shape, BF)]
    scratch = [
        pltpu.VMEM(slabs, BF),
        pltpu.VMEM(slabs, BF),
        pltpu.VMEM((rows, feat), BF),
        pltpu.VMEM((rows, feat), BF),
        pltpu.VMEM((feat, rows), BF),
        pltpu.VMEM((feat, rows), BF),
        pltpu.VMEM((rows, feat), F32),
        pltpu.VMEM((rows, feat), F32),
        pltpu.VMEM((feat, tile), BF),
        pltpu.VMEM((tile, feat), BF),
        pltpu.VMEM((count, rows, tile), BF),
        pltpu.VMEM((count, rows, tile), BF),
        dma((4,)),
    ]
    if pair:
        in_specs += [across(mine), down(mine, EARLY), hbm]
        args += [*far, outer]
        out_specs += [down(count), hbm]
        out_shape += [shape(outer.shape, BF), shape(inner.shape, BF)]
        scratch += [
            pltpu.VMEM((mine - EARLY, tile, feat), BF),
            pltpu.VMEM((mine, feat, tile), BF),
            dma((exps,)), dma((exps,)), dma((mine - EARLY,)), dma((mine - EARLY,)), dma((mine,)), dma((mine,)),
        ]
    block = next(b for b in (352, 384, 256, 128, 16) if rows % b == 0)
    return pl.pallas_call(
        functools.partial(expert_kernel, pair=pair, mine=mine, cap=cap, cp=cp, exps=exps, block=block),
        grid=(2 * count,),
        in_specs=in_specs,
        out_specs=out_specs,
        out_shape=out_shape,
        scratch_shapes=scratch,
        compiler_params=pltpu.CompilerParams(
            vmem_limit_bytes=VMEM_CAP,
            dimension_semantics=("arbitrary",),
            collective_id=4 if pair else None,
            has_side_effects=pair,
        ),
        cost_estimate=pl.CostEstimate(
            flops=12 * rows * feat * count * tile, bytes_accessed=30_000_000, transcendentals=0
        ),
    )(*args)


def back_kernel(*refs, reduce, imgs, seq, sp, cap, cp, exps):
    refs = list(refs)

    def take(count):
        taken = refs[:count]
        del refs[:count]
        return taken

    back_ref, place_col_ref, place_ref, picks_ref, gates_ref, gates_col_ref, router_ref = take(7)
    h2_ref, after_ref, cot_ref, small_ref, w_ref, mixed_ref, h1_ref, ctx_ref, x_ref, result_ref = take(10)
    if reduce:
        outer_ref = take(1)[0]
    out_ref, small_out, input_grad_ref, output_ref = take(4)
    if reduce:
        outer_out = take(1)[0]
    dafter_ref, dattn_ref, dctx_ref, dmixed_ref, grads_ref, turned_ref, rows_out_ref, results_ref = take(8)
    nt, feat = cot_ref.shape
    rows = exps * cp
    pairs = feat // 128
    groups = CHUNKS - 1
    per = pairs // groups
    width = per * 128
    key_ok = iota((sp, sp), 1) < seq
    left = iota((sp, 128), 1) < HDIM

    if reduce:
        landed, from_core, pair_sum, from_dp, dp_sum, from_y, y_sum, from_z, mine, small_in = take(10)
        (row_ssem, row_rsem, local_sem, core_send, core_recv, dp_send, dp_recv, y_send, y_recv, z_send, z_recv,
         tall_send, tall_recv, wide_send, wide_recv, last_send, last_recv, small_send, small_recv,
         outer_send, outer_recv) = take(21)
        at_dp, me = lax.axis_index("dp"), lax.axis_index("expert")
        core, chip = me % 2, me // 2
        half, quarter = feat // 2, feat // 4
        tall, wide = quarter // DEEP, feat // 2
        deep, side = chip // 2, chip % 2
        other_core, other_dp = (at_dp, chip * 2 + 1 - core), (1 - at_dp, me)
        other_side = (at_dp, (deep * 2 + 1 - side) * 2 + core)
        line = [(deep + r) % DEEP for r in range(1, DEEP)]
        peers = [(at_dp, (there * 2 + side) * 2 + core) for there in line]
        barrier = pltpu.get_barrier_semaphore()

        def greet(r, carry):
            pl.semaphore_signal(barrier, inc=1, device_id=(at_dp, (me + r) % exps), device_id_type=MESH)
            return carry

        lax.fori_loop(1, exps, greet, 0)
        pl.semaphore_signal(barrier, inc=1, device_id=other_dp, device_id_type=MESH)
        pl.semaphore_wait(barrier, exps)
        result_rows = Exchange(result_ref, landed, row_ssem, row_rsem, local_sem, exps)

        def result_go(r, carry):
            result_rows.start(r)
            return carry

        lax.fori_loop(0, exps // 2, result_go, 0)

        def core_copy(k, part):
            return remote(
                grads_ref.at[k, rows_at(part * half + (1 - core) * quarter, quarter), :],
                from_core.at[k, part], core_send.at[k, part], core_recv.at[k, part], other_core,
            )

        my_rows = rows_at(core * quarter, quarter)
        my_part = rows_at(core * quarter + deep * tall, tall)
        my_side, far_side = rows_at(side * wide, wide, 128), rows_at((1 - side) * wide, wide, 128)

        def dp_copy(k):
            return remote(pair_sum.at[k, 1 - at_dp], from_dp.at[k], dp_send.at[k], dp_recv.at[k], other_dp)

        def y_copy(k):
            return remote(dp_sum.at[k, :, far_side], from_y.at[k], y_send.at[k], y_recv.at[k], other_side)

        def z_copy(k, r):
            return remote(
                y_sum.at[k, rows_at(line[r] * tall, tall), :], from_z.at[k, r], z_send.at[k, r], z_recv.at[k, r], peers[r]
            )

        def tall_copy(k, r):
            return remote(
                mine.at[k], out_ref.at[k, my_part, my_side], tall_send.at[k, r], tall_recv.at[k, r], peers[r]
            )

        def wide_copy(k):
            place = out_ref.at[k, my_rows, my_side]
            return remote(place, place, wide_send.at[k], wide_recv.at[k], other_side)

        def last_copy(k):
            place = out_ref.at[k, my_rows, :]
            return remote(place, place, last_send.at[k], last_recv.at[k], other_core)

        def outer_copy(i):
            size = outer_ref.shape[0] // 2
            at = pl.ds(i * size, size)
            return remote(outer_ref.at[at, :], outer_out.at[at, :], outer_send.at[i], outer_recv.at[i], other_dp)

        outer_copy(0).start()
        steps = [other_core, other_dp] + [(at_dp, (chip ^ bit) * 2 + core) for bit in (1, 2, 4)]

        def small_copy(i):
            return remote(small_out, small_in.at[i], small_send.at[i], small_recv.at[i], steps[i])

    def core_start(k):
        core_copy(k, 0).start()
        core_copy(k, 1).start()

    def core_done(k):
        for part in range(2):
            core_copy(k, part).wait_recv()
            pair_sum[k, part] = (
                grads_ref[k, rows_at(part * half + core * quarter, quarter), :].astype(F32)
                + from_core[k, part].astype(F32)
            ).astype(BF)
        dp_copy(k).start()

    def dp_done(k):
        dp_copy(k).wait_recv()
        dp_sum[k] = (pair_sum[k, at_dp].astype(F32) + from_dp[k].astype(F32)).astype(BF)
        y_copy(k).start()

    def y_done(k):
        y_copy(k).wait_recv()
        y_sum[k] = (dp_sum[k, :, my_side].astype(F32) + from_y[k].astype(F32)).astype(BF)
        for r in range(DEEP - 1):
            z_copy(k, r).start()

    def z_done(k):
        total = y_sum[k, rows_at(deep * tall, tall), :].astype(F32)
        for r in range(DEEP - 1):
            z_copy(k, r).wait_recv()
            total = total + from_z[k, r].astype(F32)
        mine[k] = total.astype(BF)
        out_ref[k, my_part, my_side] = mine[k]
        for r in range(DEEP - 1):
            tall_copy(k, r).start()

    def tall_done(k):
        for r in range(DEEP - 1):
            tall_copy(k, r).wait_recv()
        wide_copy(k).start()

    def wide_done(k):
        wide_copy(k).wait_recv()
        last_copy(k).start()

    stages = (core_start, core_done, dp_done, y_done, z_done, tall_done, wide_done)

    def turn(number):
        if reduce:
            for k in reversed(range(CHUNKS)):
                if 0 <= number - k < len(stages):
                    stages[number - k](k)

    def small_go(i):
        if reduce:
            small_copy(i).start()

    def small_take(i):
        if reduce:
            small_copy(i).wait()
            small_out[...] = small_out[...] + small_in[i]

    def line_up(source):
        def step(i, carry):
            both = [source[2 * i + k].astype(F32) for k in range(2)]
            results_ref[rows_at(i * 2 * cp, 2 * cp), :] = jnp.concatenate(both, axis=0).astype(BF)
            return carry

        lax.fori_loop(0, exps // 2, step, 0)

    line_up(back_ref)
    spare = hot(iota((exps, rows), 1) == iota((exps, rows), 0) * cp + cap)
    lines = dot(spare, results_ref[:, 0:384])
    exp_id = iota((exps, nt), 0)
    dgate, match = [], []
    for k in range(2):
        pick = picks_ref[k : k + 1, :]
        place = place_ref[k : k + 1, :]
        slot = jnp.where(place >= 0, place - pick * cp, -1)
        slot_hot = hot(iota((128, nt), 0) == slot)
        found = (
            dot(lines[:, 0:128].astype(BF), slot_hot)
            + dot(lines[:, 128:256].astype(BF), slot_hot)
            + dot(lines[:, 256:384].astype(BF), slot_hot)
        )
        match.append(jnp.where(exp_id == pick, 1.0, 0.0))
        dgate.append(jnp.sum(match[k] * found, axis=0, keepdims=True))
    chosen = (gates_ref[0:1, :], gates_ref[1:2, :])
    total = chosen[0] + chosen[1]
    total = jnp.where(total > 0.0, total, 1.0)
    cross = (dgate[0] * chosen[0] + dgate[1] * chosen[1]) / (total * total)
    drouter = match[0] * (dgate[0] / total - cross) + match[1] * (dgate[1] / total - cross)
    router = router_ref[...]
    dlogits = (router * (drouter - jnp.sum(router * drouter, axis=0, keepdims=True))).astype(BF)
    norm = small_ref[exps : exps + 4, :].astype(F32)
    small_out[0:exps, :] = dot(dlogits, h2_ref[...])
    small_out[exps:, :] = jnp.zeros((small_out.shape[0] - exps, feat), F32)

    for start in range(0, nt, BIG):
        at = slice(start, start + BIG)
        slots = iota((BIG, rows), 1)
        pick = hot((slots == place_col_ref[at, 0:1]) | (slots == place_col_ref[at, 1:2]))
        dh2 = dot(pick, results_ref[...]) + dot_tn(dlogits[:, at], small_ref[0:exps, :])
        normed, rstd = normed_of(after_ref[at, :])
        small_out[exps + 2 : exps + 3, :] += jnp.sum(dh2 * normed, axis=0, keepdims=True)
        small_out[exps + 3 : exps + 4, :] += jnp.sum(dh2, axis=0, keepdims=True)
        dafter = cot_ref[at, :].astype(F32) + norm_back_rows(dh2, normed, rstd, norm[2:3])
        dafter_ref[at, :] = dafter
        dattn = dafter.astype(BF)
        dattn_ref[at, :] = dattn
        dctx_ref[at, :] = dot_nt(dattn, w_ref[:, 3 * feat : 4 * feat]).astype(BF)

    def attend(group):
        def image(i, carry):
            lines = rows_at(i * sp, sp)
            for p in range(per):
                col = (group * per + p) * 128
                at_q, at_k, at_v = (
                    slice(c, c + 128) for c in (group * feat + n * width + p * 128 for n in range(3))
                )
                query, keys, values = mixed_ref[lines, at_q], mixed_ref[lines, at_k], mixed_ref[lines, at_v]
                dctx = dctx_ref[lines, col : col + 128]
                zero = jnp.zeros_like(query)
                dq = dk = dv = 0.0
                for mask in (left, ~left):
                    query_h = jnp.where(mask, query, zero)
                    keys_h = jnp.where(mask, keys, zero)
                    dctx_h = jnp.where(mask, dctx, zero)
                    scores = jnp.where(key_ok, dot_nt(query_h, keys) * SCALE, NEG)
                    top = jnp.max(scores, axis=-1, keepdims=True)
                    grown = jnp.exp(scores - top)
                    probs = grown / jnp.sum(grown, axis=-1, keepdims=True)
                    dv = dv + dot_tn(probs.astype(BF), dctx_h)
                    dweights = dot_nt(dctx_h, values)
                    dscores = (
                        probs * (dweights - jnp.sum(probs * dweights, axis=-1, keepdims=True))
                    ).astype(BF)
                    dq = dq + dot(dscores, keys_h)
                    dk = dk + dot_tn(dscores, query_h)
                dmixed_ref[lines, at_q] = (dq * SCALE).astype(BF)
                dmixed_ref[lines, at_k] = (dk * SCALE).astype(BF)
                dmixed_ref[lines, at_v] = dv.astype(BF)
            return carry

        lax.fori_loop(0, imgs, image, 0)
        for n in range(2):
            at = slice(n * (feat // 2), (n + 1) * (feat // 2))
            grads_ref[1 + group, :, at] = dot(
                turned_ref[...], dmixed_ref[:, group * feat + at.start : group * feat + at.stop]
            ).astype(BF)

    def first_norm(start):
        at = slice(start, start + BIG)
        dh1 = dot_nt(dmixed_ref[at, :], w_ref[:, : 3 * feat])
        normed, rstd = normed_of(x_ref[at, :].astype(F32))
        small_out[exps : exps + 1, :] += jnp.sum(dh1 * normed, axis=0, keepdims=True)
        small_out[exps + 1 : exps + 2, :] += jnp.sum(dh1, axis=0, keepdims=True)
        rows_out_ref[at, :] = (dafter_ref[at, :] + norm_back_rows(dh1, normed, rstd, norm[0:1])).astype(BF)

    def deliver(ref):
        for i in range(imgs):
            ref[i] = rows_out_ref[i * sp : i * sp + seq, :]

    def final_rows(start):
        at = slice(start, start + BIG)
        slots = iota((BIG, rows), 1)
        final = after_ref[at, :]
        for k in range(2):
            pick = hot(slots == place_col_ref[at, k : k + 1])
            final = final + gates_col_ref[at, 2 + k : 3 + k] * dot(pick, results_ref[...])
        rows_out_ref[at, :] = final.astype(BF)

    dmixed_ref[imgs * sp : nt, :] = jnp.zeros((nt - imgs * sp, 3 * feat), BF)
    turned_ref[...] = ctx_ref[...].T
    for n in range(2):
        at = slice(n * (feat // 2), (n + 1) * (feat // 2))
        grads_ref[0, :, at] = dot(turned_ref[...], dattn_ref[:, at]).astype(BF)
    turn(0)
    turned_ref[...] = h1_ref[...].T
    for group in range(groups):
        attend(group)
        turn(1 + group)
    first_norm(0)
    if reduce:
        core_done(3)
        dp_done(2)
        y_done(1)
    for start in range(BIG, nt, BIG):
        first_norm(start)
    deliver(input_grad_ref)
    if not reduce:
        out_ref[...] = grads_ref[...]
        line_up(result_ref)
        for start in range(0, nt, BIG):
            final_rows(start)
        deliver(output_ref)
        return
    small_go(0)
    dp_done(3)
    y_done(2)
    small_take(0)
    small_go(1)
    outer_copy(1).start()
    y_done(3)
    z_done(0)
    z_done(1)
    small_take(1)
    small_go(2)
    z_done(2)
    z_done(3)
    result_rows.finish()
    line_up(landed)
    final_rows(0)
    tall_done(0)
    small_take(2)
    small_go(3)
    tall_done(1)
    tall_done(2)
    for start in range(BIG, nt, BIG):
        final_rows(start)
    deliver(output_ref)
    small_take(3)
    small_go(4)
    tall_done(3)
    for k in range(CHUNKS):
        wide_done(k)
    small_take(4)
    outer_copy(0).wait()
    outer_copy(1).wait()
    for k in range(CHUNKS):
        last_copy(k).wait()
        core_copy(k, 0).wait_send()
        core_copy(k, 1).wait_send()
        dp_copy(k).wait_send()
        y_copy(k).wait_send()
        wide_copy(k).wait_send()
        for r in range(DEEP - 1):
            z_copy(k, r).wait_send()
            tall_copy(k, r).wait_send()


def run_back(reduce, imgs, seq, sp, cap, cp, exps, *args):
    nt, feat = args[8].shape
    vmem = pl.BlockSpec(memory_space=pltpu.VMEM)
    small = up(exps + 4, 8)
    quarter = feat // 4
    scratch = [
        pltpu.VMEM((nt, feat), F32),
        pltpu.VMEM((nt, feat), BF),
        pltpu.VMEM((nt, feat), BF),
        pltpu.VMEM((nt, 3 * feat), BF),
        pltpu.VMEM((CHUNKS, feat, feat), BF),
        pltpu.VMEM((feat, nt), BF),
        pltpu.VMEM((nt, feat), BF),
        pltpu.VMEM((exps * cp, feat), BF),
    ]
    if reduce:
        dma = pltpu.SemaphoreType.DMA
        tall, wide = quarter // DEEP, feat // 2
        line = (CHUNKS, DEEP - 1)
        one, many = dma((CHUNKS,)), dma(line)
        scratch += [
            pltpu.VMEM((exps, cp, feat), BF),
            pltpu.VMEM((CHUNKS, 2, quarter, feat), BF),
            pltpu.VMEM((CHUNKS, 2, quarter, feat), BF),
            pltpu.VMEM((CHUNKS, quarter, feat), BF),
            pltpu.VMEM((CHUNKS, quarter, feat), BF),
            pltpu.VMEM((CHUNKS, quarter, wide), BF),
            pltpu.VMEM((CHUNKS, quarter, wide), BF),
            pltpu.VMEM(line + (tall, wide), BF),
            pltpu.VMEM((CHUNKS, tall, wide), BF),
            pltpu.VMEM((5, small, feat), F32),
            dma((exps,)), dma((exps,)), dma, dma((CHUNKS, 2)), dma((CHUNKS, 2)),
            one, one, one, one, many, many, many, many, one, one, one, one, dma((5,)), dma((5,)),
            dma((2,)), dma((2,)),
        ]
    hbm = pl.BlockSpec(memory_space=pl.ANY)
    extra = [shape(args[-1].shape, BF)] if reduce else []
    return pl.pallas_call(
        functools.partial(
            back_kernel, reduce=reduce, imgs=imgs, seq=seq, sp=sp, cap=cap, cp=cp, exps=exps
        ),
        out_shape=(
            shape((CHUNKS, feat // 2 if reduce else feat, feat), BF),
            shape((small, feat), F32),
            shape((imgs, seq, feat), BF),
            shape((imgs, seq, feat), BF),
            *extra,
        ),
        in_specs=[vmem] * (len(args) - 2) + [hbm] * 2 if reduce else [vmem] * len(args),
        out_specs=(vmem,) * 4 + (hbm,) * len(extra),
        scratch_shapes=scratch,
        compiler_params=pltpu.CompilerParams(
            vmem_limit_bytes=50 * 1024 * 1024, collective_id=1 if reduce else None, has_side_effects=reduce
        ),
        cost_estimate=pl.CostEstimate(flops=60_000_000_000, bytes_accessed=60_000_000, transcendentals=0),
    )(*args)


def adam_rows(weight, first, second, grad, rate, decay):
    new_first = BETA_ONE * first + (1.0 - BETA_ONE) * grad
    new_second = BETA_TWO * second + (1.0 - BETA_TWO) * grad * grad
    first_hat = new_first * (1.0 / (1.0 - BETA_ONE**STEP))
    second_hat = new_second * (1.0 / (1.0 - BETA_TWO**STEP))
    new_weight = weight - rate * (first_hat / (jnp.sqrt(second_hat) + ADAM_EPS) + decay * weight)
    return new_weight, new_first, new_second


def total_kernel(small_ref, dense_in, *refs, shards, exps):
    far_in = refs[:4]
    norm_ref, inner_out, outer_out, dense_ref, far, part_ref, landed, dense_sem, far_sem, store_sem, send_sem, recv_sem = refs[4:]
    tall, feat = dense_ref.shape[1:]
    at_dp, me = lax.axis_index("dp"), lax.axis_index("expert")
    count = shards * exps
    flat = at_dp * exps + me
    devices = [(((flat + r) % count) // exps, ((flat + r) % count) % exps) for r in range(1, count)]
    pieces = [
        (2 * i, down, right)
        for i in range(2)
        for down in range(far_in[2 * i].shape[0] // tall)
        for right in range(far_in[2 * i].shape[1] // feat)
    ]

    def load(t, n):
        i, down, right = pieces[t]
        source = far_in[i + n].at[pl.ds(down * tall, tall), pl.ds(right * feat, feat)]
        return pltpu.make_async_copy(source, far.at[t, n], far_sem.at[t, n])

    def store(t):
        i, down, right = pieces[t]
        target = (inner_out, outer_out)[i // 2].at[pl.ds(down * tall, tall), pl.ds(right * feat, feat)]
        return pltpu.make_async_copy(far.at[t, 0], target, store_sem.at[t])

    def load_dense(k):
        return pltpu.make_async_copy(dense_in.at[k], dense_ref.at[k], dense_sem.at[k])

    for k in range(CHUNKS):
        load_dense(k).start()
    for t in range(len(pieces)):
        load(t, 0).start()
        load(t, 1).start()
    barrier = pltpu.get_barrier_semaphore()

    def greet(r, carry):
        there = (flat + r) % count
        pl.semaphore_signal(barrier, inc=1, device_id=(there // exps, there % exps), device_id_type=MESH)
        return carry

    lax.fori_loop(1, count, greet, 0)
    unit = 32

    def squares_of(read):
        def step(i, total):
            values = read(rows_at(i * unit, unit))
            return total + jnp.sum((values * values).reshape(unit // 8, 8, feat), axis=0)

        return lax.fori_loop(0, tall // unit, step, jnp.zeros((8, feat), F32))

    half = feat // shards
    small = small_ref[:, rows_at(at_dp * half, half, 128)]
    dense_part = jnp.zeros((8, feat), F32)
    for k in range(CHUNKS):
        load_dense(k).wait()
        dense_part += squares_of(lambda at, k=k: dense_ref[k, at, :].astype(F32))
    local = jnp.where(me == 0, jnp.sum(dense_part) + jnp.sum(small * small), 0.0)
    part = jnp.zeros((8, feat), F32)
    for t in range(len(pieces)):
        load(t, 0).wait()
        load(t, 1).wait()

        def both(at, t=t):
            values = far[t, 0, at, :].astype(F32) + far[t, 1, at, :].astype(F32)
            far[t, 0, at, :] = values.astype(BF)
            return values

        part += squares_of(both)
        store(t).start()
    part_ref[...] = jnp.full(part_ref.shape, local + jnp.sum(part), F32)
    pl.semaphore_wait(barrier, count - 1)
    copies = [
        remote(part_ref, landed.at[r], send_sem.at[r], recv_sem.at[r], device) for r, device in enumerate(devices)
    ]
    for made in copies:
        made.start()
    total = part_ref[...]
    for r, made in enumerate(copies):
        made.wait_recv()
        total = total + landed[r]
    norm_ref[...] = jnp.sqrt(total)
    for t in range(len(pieces)):
        store(t).wait()
    for made in copies:
        made.wait_send()


def run_total(shards, exps, small, dense, *far):
    count = shards * exps
    vmem, hbm = pl.BlockSpec(memory_space=pltpu.VMEM), pl.BlockSpec(memory_space=pl.ANY)
    dma = pltpu.SemaphoreType.DMA
    tall, feat = dense.shape[1:]
    pieces = sum(a.size for a in far) // (2 * tall * feat)
    return pl.pallas_call(
        functools.partial(total_kernel, shards=shards, exps=exps),
        out_shape=(shape((8, 128), F32), shape(far[0].shape, BF), shape(far[2].shape, BF)),
        in_specs=[vmem] + [hbm] * (1 + len(far)),
        out_specs=(vmem, hbm, hbm),
        scratch_shapes=[
            pltpu.VMEM(dense.shape, BF),
            pltpu.VMEM((pieces, 2, tall, feat), BF),
            pltpu.VMEM((8, 128), F32),
            pltpu.VMEM((count - 1, 8, 128), F32),
            dma((CHUNKS,)), dma((pieces, 2)), dma((pieces,)), dma((count - 1,)), dma((count - 1,)),
        ],
        compiler_params=pltpu.CompilerParams(
            vmem_limit_bytes=60 * 1024 * 1024, collective_id=2, has_side_effects=True
        ),
        cost_estimate=pl.CostEstimate(flops=100_000_000, bytes_accessed=20_000_000, transcendentals=0),
    )(small, dense, *far)


SLOTS = 4


def adam_kernel(*refs, exps, pieces):
    refs = list(refs)

    def take(count):
        taken = refs[:count]
        del refs[:count]
        return taken

    norm_ref, small_ref, dense_ref = take(3)
    router_in, norm_in = take(3), take(3)
    far_in = take(2)
    state_in = [take(3) for _ in range(4)]
    norm_out, router_out, vector_out = take(1)[0], take(3), take(3)
    state_out = [take(3) for _ in range(4)]
    far, state, far_sem, load_sem, store_sem = refs
    tall, feat = far.shape[-2:]
    unit = 32

    def part(ref, t):
        _, down, right = pieces[t]
        return ref.at[pl.ds(down * tall, tall), pl.ds(right * feat, feat)]

    def loads(t):
        i, slot = pieces[t][0], t % SLOTS
        made = [
            pltpu.make_async_copy(part(state_in[i][n], t), state.at[slot, n], load_sem.at[slot, n]) for n in range(3)
        ]
        if i < 2:
            made += [
                pltpu.make_async_copy(part(far_in[i], t), far.at[slot], far_sem.at[slot])
                for _ in range(1)
            ]
        return made

    def stores(t):
        i, slot = pieces[t][0], t % SLOTS
        return [
            pltpu.make_async_copy(state.at[slot, n], part(state_out[i][n], t), store_sem.at[slot, n]) for n in range(3)
        ]

    def each(copies, what):
        for made in copies:
            getattr(made, what)()

    for t in range(SLOTS - 1):
        each(loads(t), "start")
    norm_out[...] = norm_ref[0:1, 0:1]
    clip = CLIP_NORM / jnp.maximum(norm_ref[0:1, 0:1], CLIP_NORM)
    small = small_ref[...]
    router_grad = small[0:exps] * clip
    for ref, new in zip(router_out, adam_rows(*(r[...] for r in router_in), router_grad, RATE_MATRIX, DECAY)):
        ref[...] = new
    vector_grad = small[exps : exps + 4] * clip
    for ref, new in zip(vector_out, adam_rows(*(r[...] for r in norm_in), vector_grad, RATE_VECTOR, 0.0)):
        ref[...] = new

    for t, (i, _, right) in enumerate(pieces):
        slot = t % SLOTS
        each(loads(t), "wait")

        def rows(u, carry, i=i, right=right, slot=slot):
            at = rows_at(u * unit, unit)
            if i < 2:
                grad = far[slot, at, :].astype(F32)
            elif i == 2:
                width = feat // (CHUNKS - 1)
                grad = jnp.concatenate(
                    [dense_ref[g, at, right * width : (right + 1) * width] for g in range(1, CHUNKS)], axis=1
                ).astype(F32)
            else:
                grad = dense_ref[0, at, :].astype(F32)
            new = adam_rows(*(state[slot, n, at, :] for n in range(3)), grad * clip, RATE_MATRIX, DECAY)
            for n in range(3):
                state[slot, n, at, :] = new[n]
            return carry

        lax.fori_loop(0, tall // unit, rows, 0)
        each(stores(t), "start")
        if t + SLOTS - 1 < len(pieces):
            if t >= 1:
                each(stores(t - 1), "wait")
            each(loads(t + SLOTS - 1), "start")
    for t in range(len(pieces) - SLOTS, len(pieces)):
        each(stores(t), "wait")


def run_adam(exps, norm, small, dense, router, vector, far, states):
    vmem, hbm = pl.BlockSpec(memory_space=pltpu.VMEM), pl.BlockSpec(memory_space=pl.ANY)
    dma = pltpu.SemaphoreType.DMA
    tall, feat = dense.shape[1:]
    pieces = [
        (i, down, right)
        for i, group in enumerate(states)
        for down in range(group[0].shape[0] // tall)
        for right in range(group[0].shape[1] // feat)
    ]
    flat_states = [a for group in states for a in group]
    args = [norm, small, dense, *router, *vector, *far, *flat_states]
    return pl.pallas_call(
        functools.partial(adam_kernel, exps=exps, pieces=pieces),
        out_shape=[shape((1, 1), F32)] + [shape(a.shape, F32) for a in (*router, *vector, *flat_states)],
        in_specs=[vmem] * 9 + [hbm] * 14,
        out_specs=[vmem] * 7 + [hbm] * 12,
        scratch_shapes=[
            pltpu.VMEM((SLOTS, tall, feat), BF),
            pltpu.VMEM((SLOTS, 3, tall, feat), F32),
            dma((SLOTS,)), dma((SLOTS, 3)), dma((SLOTS, 3)),
        ],
        compiler_params=pltpu.CompilerParams(vmem_limit_bytes=60 * 1024 * 1024),
        cost_estimate=pl.CostEstimate(flops=100_000_000, bytes_accessed=100_000_000, transcendentals=0),
    )(*args)


def adam_step(weight, first, second, grad, rate, decay):
    new_first = BETA_ONE * first + (1.0 - BETA_ONE) * grad
    new_second = BETA_TWO * second + (1.0 - BETA_TWO) * grad * grad
    first_hat = new_first / (1.0 - BETA_ONE**STEP)
    second_hat = new_second / (1.0 - BETA_TWO**STEP)
    new_weight = weight - rate * (first_hat / (jnp.sqrt(second_hat) + ADAM_EPS) + decay * weight)
    return (new_weight, new_first, new_second)


def body(
    images,
    cotangent,
    routes,
    priority,
    qkv_weight,
    qkv_first,
    qkv_second,
    proj_weight,
    proj_first,
    proj_second,
    router_weight,
    router_first,
    router_second,
    norm_params,
    norm_first,
    norm_second,
    inner_weight,
    inner_first,
    inner_second,
    outer_weight,
    outer_first,
    outer_second,
):
    exps = lax.axis_size("expert")
    shards = lax.axis_size("dp")
    imgs, seq, feat = images.shape
    tok = imgs * seq
    cap = (18 * tok + 8 * exps - 1) // (8 * exps)
    cp = up(cap + 1, 8)
    sp = up(seq, 16)
    nt = up(imgs * sp, BLOCK)
    rows = exps * cp
    at_dp, at_exp = lax.axis_index("dp"), lax.axis_index("expert")
    shard_rows = qkv_weight.shape[0]
    by_kernel = shards == 2 and exps == 4 * DEEP

    qkv_in, proj_in = qkv_weight, proj_weight
    small = jnp.concatenate([router_weight.astype(BF).T, norm_params.astype(BF)], axis=0)
    small = jnp.pad(small, ((0, up(exps + 4, 16) - exps - 4), (0, 0)))
    if not by_kernel:
        qkv_in = lax.all_gather(qkv_weight.astype(BF), "dp", axis=0, tiled=True)
        proj_in = lax.all_gather(proj_weight.astype(BF), "dp", axis=0, tiled=True)
        small = lax.all_gather(small, "dp", axis=1, tiled=True)
    picks = jnp.pad(routes.transpose(2, 0, 1), ((0, 0), (0, 0), (0, sp - seq)), constant_values=-1)
    picks = jnp.pad(picks.reshape(2, imgs * sp), ((0, 0), (0, nt - imgs * sp)), constant_values=-1)
    order = priority[0] + (priority[0] // seq) * (sp - seq)
    order = jnp.pad(order, (0, nt - tok), constant_values=-1)
    w_full, small, h1, mixed, context, after, h2, router, gates, place, gates_col, place_col, x, cot, recv, recv_cot, *others = (
        run_front(
        images, cotangent, picks, order[None, :], small, qkv_in, proj_in,
        (inner_weight[0], outer_weight[0]) if by_kernel else None,
        nt=nt, sp=sp, cap=cap, cp=cp, exps=exps,
    ))
    if by_kernel:
        own, far = tuple(others[:2]), tuple(others[2:])
    else:
        own, far = (
            lax.all_gather(inner_weight[0].astype(BF), "dp", axis=1, tiled=True),
            lax.all_gather(outer_weight[0].astype(BF), "dp", axis=0, tiled=True),
        ), None

    back_grad, result, own_inner, own_outer, *rest = run_expert(recv, recv_cot, own, far, cap, cp, exps)
    if by_kernel:
        far_outer, sent_inner = rest
    else:
        back_grad = lax.all_to_all(back_grad, "expert", split_axis=0, concat_axis=0, tiled=True)
        shard_inner = lax.psum_scatter(own_inner, "dp", scatter_dimension=1, tiled=True).astype(F32)[None]
        shard_outer = lax.psum_scatter(own_outer, "dp", scatter_dimension=0, tiled=True).astype(F32)[None]

    if not by_kernel:
        result = lax.all_to_all(result, "expert", split_axis=0, concat_axis=0, tiled=True)
    dense_grad, small_grad, input_grad, output, *sent = run_back(
        by_kernel, imgs, seq, sp, cap, cp, exps,
        back_grad, place_col, place, picks, gates, gates_col, router, h2, after, cot, small, w_full,
        mixed, h1, context, x, result, *((far_outer,) if by_kernel else ()),
    )

    if by_kernel:
        far = (own_inner, sent_inner, own_outer, *sent)
        norm, *far = run_total(shards, exps, small_grad, dense_grad, *far)
        small_half = lax.dynamic_slice_in_dim(small_grad, at_dp * shard_rows, shard_rows, 1)
        norm, *new = run_adam(
            exps, norm, small_half, dense_grad,
            (router_weight.T, router_first.T, router_second.T),
            (norm_params, norm_first, norm_second),
            far,
            (
                (inner_weight[0], inner_first[0], inner_second[0]),
                (outer_weight[0], outer_first[0], outer_second[0]),
                (qkv_weight, qkv_first, qkv_second),
                (proj_weight, proj_first, proj_second),
            ),
        )
        router_new, norm_new, inner_new, outer_new, qkv_new, proj_new = (new[3 * i : 3 * i + 3] for i in range(6))
        return (
            output,
            input_grad,
            norm[0, 0],
            *qkv_new,
            *proj_new,
            *(a.T for a in router_new),
            *norm_new,
            *(a[None] for a in inner_new),
            *(a[None] for a in outer_new),
        )

    dense_grad = lax.psum(dense_grad, ("dp", "expert"))
    small_grad = lax.psum(small_grad, ("dp", "expert"))
    width = feat // (CHUNKS - 1)
    dense_grad = lax.dynamic_slice_in_dim(dense_grad, at_dp * shard_rows, shard_rows, 1).astype(F32)
    shard_small = lax.dynamic_slice_in_dim(small_grad, at_dp * shard_rows, shard_rows, 1)
    shard_qkv = jnp.concatenate(
        [dense_grad[g, :, n * width : (n + 1) * width] for n in range(3) for g in range(1, CHUNKS)], axis=1
    )
    shard_proj = dense_grad[0]
    shard_router, shard_vector = shard_small[:exps].T, shard_small[exps : exps + 4]
    dense_squares = jnp.sum(dense_grad * dense_grad) + jnp.sum(shard_small * shard_small)
    expert_squares = jnp.sum(shard_inner * shard_inner) + jnp.sum(shard_outer * shard_outer)
    local_squares = expert_squares + jnp.where(at_exp == 0, dense_squares, jnp.float32(0.0))
    grad_norm = jnp.sqrt(lax.psum(local_squares, ("dp", "expert")))
    clip = CLIP_NORM / jnp.maximum(grad_norm, CLIP_NORM)
    qkv_new = adam_step(qkv_weight, qkv_first, qkv_second, shard_qkv * clip, RATE_MATRIX, DECAY)
    proj_new = adam_step(proj_weight, proj_first, proj_second, shard_proj * clip, RATE_MATRIX, DECAY)
    router_new = adam_step(
        router_weight, router_first, router_second, shard_router * clip, RATE_MATRIX, DECAY
    )
    norm_new = adam_step(norm_params, norm_first, norm_second, shard_vector * clip, RATE_VECTOR, 0.0)
    inner_new = adam_step(
        inner_weight, inner_first, inner_second, shard_inner * clip, RATE_MATRIX, DECAY
    )
    outer_new = adam_step(
        outer_weight, outer_first, outer_second, shard_outer * clip, RATE_MATRIX, DECAY
    )
    return (
        output,
        input_grad,
        grad_norm,
        *qkv_new,
        *proj_new,
        *router_new,
        *norm_new,
        *inner_new,
        *outer_new,
    )


def solution(mesh):
    tokens = P(("dp", "expert"), None, None)
    dense = P("dp", None)
    vector = P(None, "dp")
    inner = P("expert", None, "dp")
    outer = P("expert", "dp", None)
    return jax.shard_map(
        body,
        mesh=mesh,
        in_specs=(tokens, tokens, tokens, P(("dp", "expert"), None))
        + (dense,) * 9
        + (vector,) * 3
        + (inner,) * 3
        + (outer,) * 3,
        out_specs=(tokens, tokens, P())
        + (dense,) * 9
        + (vector,) * 3
        + (inner,) * 3
        + (outer,) * 3,
        check_vma=False,
    )
```
